256 devices in a mesh: head: 4 (over x), inner: 16 (over z, core), outer: 4 (over y).
Axes of the slice: x: 4, y: 4, z: 8, core: 2. Of those that a mesh axis runs over, the one named last changes fastest.
Arguments:
- queries: bfloat16 [8192, 64, 128], P(('outer', 'inner'), None, 'head'), may hold values from -6 to 6
- keys: bfloat16 [8192, 8, 128], P(('outer', 'inner'), None, 'head'), may hold values from -6 to 6
- values: bfloat16 [8192, 8, 128], P(('outer', 'inner'), None, 'head'), may hold values from -6 to 6
- grad_out: bfloat16 [8192, 64, 128], P(('outer', 'inner'), None, 'head'), may hold values from -6 to 6
- span_order: int32 [128], replicated, may hold values from 0 to 127, as said below
- doc_ids: int32 [8192], replicated, may hold values from 0 to 3, never falling along the last dimension, each value on 1 to 4096 neighbouring positions
Outputs:
- attn_out: bfloat16 [8192, 64, 128], P(('outer', 'inner'), 'head')
- query_grads: float32 [8192, 64, 128], P(('outer', 'inner'), 'head')
- key_grads: float32 [8192, 8, 128], P(('outer', 'inner'), 'head')
- value_grads: float32 [8192, 8, 128], P(('outer', 'inner'), 'head')
The draws below stay inside these ranges and needn't reach their ends.
Inputs may be any that keep to these rules, and one draw needn't show every extreme that they name: `span_order`: stored span slots 2r and 2r+1 hold the spans c and 127 - c for some c; every span appears once. doc_ids never falls along the sequence.
All inputs are finite; a program needn't handle non-finite values.
Results may differ from the reference program's by a relative error of at most 0.025.
Values may be sent and summed in bfloat16 or wider, within the bound.
A program may use at most 64 MiB of HBM per device.

```python
import math
import jax
import jax.numpy as jnp
import numpy as np
from jax import lax

HEADS = 64
KV = 8
HD = 128
DOCS = 4
GROUP = 8
SPAN = 64
CYCLE = 64
GROUPS = 4
GROUP_ROWS = 2048
SEQ = 8192


def draw_queries(key, part):
    key = jax.random.fold_in(key, 11)
    first_key = jax.random.fold_in(key, 0)
    normal_part = jnp.clip(jax.random.normal(first_key, (SEQ, HEADS, HD), dtype=jnp.float32), -4.0, 4.0)
    return normal_part.astype(jnp.bfloat16)


def draw_keys(key, part):
    key = jax.random.fold_in(key, 23)
    first_key = jax.random.fold_in(key, 0)
    normal_part = jnp.clip(jax.random.normal(first_key, (SEQ, KV, HD), dtype=jnp.float32), -4.0, 4.0)
    return normal_part.astype(jnp.bfloat16)


def draw_span_order(key, part):
    key = jax.random.fold_in(key, 5)
    first_key, second_key = jax.random.split(key)
    early = jax.random.permutation(first_key, CYCLE).astype(jnp.int32)
    flipped = jax.random.randint(second_key, (CYCLE,), 0, 2)
    late = 2 * CYCLE - 1 - early
    leading = jnp.where(flipped == 1, late, early)
    trailing = jnp.where(flipped == 1, early, late)
    return jnp.stack((leading, trailing), axis=1).reshape(2 * CYCLE).astype(jnp.int32)


def level_of(rng, dims, shards, low, high):
    gain = 1.0
    for dim, shards_of in shards:
        steps = jax.random.uniform(jax.random.fold_in(jax.random.fold_in(rng, 6), dim), (shards_of,), jnp.float32, low / len(shards), high / len(shards))
        gain = gain * jnp.repeat(jnp.exp(steps), dims[dim] // shards_of).reshape((-1,) + (1,) * (len(dims) - 1 - dim))
    return gain


def profile(number_of, total, reach, slope):
    loads = [(1 << 20) // math.isqrt(grade ** slope) + 1 for grade in range(2, number_of + 1)]
    surplus, holding = total - reach - (number_of - 1), [1] * (number_of - 1)
    while surplus > 0:
        free = [i for i in range(number_of - 1) if holding[i] < reach]
        mass, budget = sum([loads[i] for i in free]), surplus
        for i in free:
            more = min(reach - holding[i], max(1, budget * loads[i] // mass), surplus)
            holding[i] = holding[i] + more
            surplus = surplus - more
    return np.array([reach] + holding)


def ragged(own_key, count, total, limit, skew):
    if count == 2:
        one = jax.random.randint(own_key, (), max(1, total - limit), min(limit, total - 1) + 1)
        return jnp.stack([one, total - one])
    lengths = jnp.asarray(profile(count, total, limit, skew), jnp.int32)
    couples = (count - 1) // 2
    giver, receiver = lengths[1:1 + 2 * couples:2], lengths[2:2 + 2 * couples:2]
    slack = jnp.minimum(giver - 1, limit - receiver)
    passed = jax.random.randint(jax.random.fold_in(own_key, 1), (couples,), 0, 1 << 20) % (slack + 1)
    lengths = lengths.at[1:1 + 2 * couples:2].set(giver - passed).at[2:2 + 2 * couples:2].set(receiver + passed)
    return lengths[jax.random.permutation(jax.random.fold_in(own_key, 2), count)]


def gaussian(rng, shape, scale, bound, pieces=(), kind=jnp.bfloat16):
    drawn = scale * jax.random.normal(rng, shape, jnp.float32)
    if pieces:
        drawn = drawn * level_of(rng, shape, pieces, -0.22, 0.18)
    return jnp.clip(drawn, -bound, bound).astype(kind)


def setup_inputs(seed: int = 0) -> dict:
    splits = jax.random.split(jax.random.key(seed), 7)
    return {
        "queries": draw_queries(jax.random.fold_in(splits[6], 71), 0),
        "keys": draw_keys(jax.random.fold_in(splits[6], 71), 0),
        "values": gaussian(splits[2], (SEQ, KV, HD), 1.0, 6.0, ((0, 64), (2, 4))),
        "grad_out": gaussian(splits[3], (SEQ, HEADS, HD), 1.0, 6.0, ((0, 64), (2, 4))),
        "span_order": draw_span_order(jax.random.fold_in(splits[6], 71), 0),
        "doc_ids": jnp.searchsorted(jnp.cumsum(ragged(splits[5], DOCS, SEQ, SEQ // 2, 2)), jnp.arange(SEQ), side="right").astype(jnp.int32),
    }


NEG = -1e+30

def token_info(span_order, doc_ids):
    row_ids = jnp.arange(SEQ, dtype=jnp.int32)
    position = (span_order[row_ids // SPAN] * SPAN + row_ids % SPAN).astype(jnp.int32)
    return (position, doc_ids[position])

def group_attention(query_part, grad_part, key_part, value_part, query_pos, query_doc, key_pos, key_doc):
    score_scale = 1.0 / math.sqrt(HD)
    high = lax.Precision.HIGHEST
    query_f = query_part.astype(jnp.float32)
    grad_f = grad_part.astype(jnp.float32)
    key_f = key_part.astype(jnp.float32)
    value_f = value_part.astype(jnp.float32)
    scores = jnp.einsum('qgd,kd->qgk', query_f, key_f, precision=high) * score_scale
    allowed = (key_pos[None, :] <= query_pos[:, None]) & (key_doc[None, :] == query_doc[:, None])
    allowed = allowed[:, None, :]
    row_max = lax.optimization_barrier(jnp.max(jnp.where(allowed, scores, NEG), axis=-1))
    probs_fwd = jnp.where(allowed, jnp.exp(scores - row_max[..., None]), 0.0)
    row_sum = lax.optimization_barrier(jnp.sum(probs_fwd, axis=-1))
    weights = probs_fwd.astype(jnp.bfloat16).astype(jnp.float32)
    attn_out = (jnp.einsum('qgk,kd->qgd', weights, value_f, precision=high) / row_sum[..., None]).astype(jnp.bfloat16)
    log_total = row_max + jnp.log(row_sum)
    row_dot = lax.optimization_barrier(jnp.sum(grad_f * attn_out.astype(jnp.float32), axis=-1))
    probs = jnp.where(allowed, jnp.exp(scores - log_total[..., None]), 0.0)
    probs_b = probs.astype(jnp.bfloat16).astype(jnp.float32)
    value_grads = jnp.einsum('qgk,qgd->kd', probs_b, grad_f, precision=high)
    prob_grads = jnp.einsum('qgd,kd->qgk', grad_f, value_f, precision=high)
    score_grads = (probs * (prob_grads - row_dot[..., None])).astype(jnp.bfloat16).astype(jnp.float32)
    query_grads = jnp.einsum('qgk,kd->qgd', score_grads, key_f, precision=high) * score_scale
    key_grads = jnp.einsum('qgk,qgd->kd', score_grads, query_f, precision=high) * score_scale
    return (attn_out, query_grads, key_grads, value_grads)

def reference(queries, keys, values, grad_out, span_order, doc_ids):
    position, document = token_info(span_order, doc_ids)
    query_groups = queries.reshape(GROUPS, GROUP_ROWS, KV, GROUP, HD)
    grad_groups = grad_out.reshape(GROUPS, GROUP_ROWS, KV, GROUP, HD)
    key_groups = keys.reshape(GROUPS, GROUP_ROWS, KV, HD)
    value_groups = values.reshape(GROUPS, GROUP_ROWS, KV, HD)
    pos_groups = position.reshape(GROUPS, GROUP_ROWS)
    doc_groups = document.reshape(GROUPS, GROUP_ROWS)
    key_window = jnp.concatenate((key_groups, jnp.roll(key_groups, 1, axis=0)), axis=1)
    value_window = jnp.concatenate((value_groups, jnp.roll(value_groups, 1, axis=0)), axis=1)
    pos_window = jnp.concatenate((pos_groups, jnp.roll(pos_groups, 1, axis=0)), axis=1)
    doc_window = jnp.concatenate((doc_groups, jnp.roll(doc_groups, 1, axis=0)), axis=1)

    def per_group(inputs):
        query_g, grad_g, key_g, value_g, query_pos, query_doc, key_pos, key_doc = inputs

        def per_head(head_inputs):
            return group_attention(head_inputs[0], head_inputs[1], head_inputs[2], head_inputs[3], query_pos, query_doc, key_pos, key_doc)
        results = lax.map(per_head, (jnp.moveaxis(query_g, 1, 0), jnp.moveaxis(grad_g, 1, 0), jnp.moveaxis(key_g, 1, 0), jnp.moveaxis(value_g, 1, 0)))
        return (jnp.moveaxis(results[0], 0, 1), jnp.moveaxis(results[1], 0, 1), jnp.moveaxis(results[2], 0, 1), jnp.moveaxis(results[3], 0, 1))
    outputs = lax.map(per_group, (query_groups, grad_groups, key_window, value_window, pos_groups, doc_groups, pos_window, doc_window))
    attn_out = outputs[0].reshape(SEQ, HEADS, HD)
    query_grads = outputs[1].reshape(SEQ, HEADS, HD)
    key_terms = outputs[2]
    value_terms = outputs[3]
    key_grads = key_terms[:, :GROUP_ROWS] + jnp.roll(key_terms[:, GROUP_ROWS:], -1, axis=0)
    value_grads = value_terms[:, :GROUP_ROWS] + jnp.roll(value_terms[:, GROUP_ROWS:], -1, axis=0)
    return (attn_out, query_grads, key_grads.reshape(SEQ, KV, HD), value_grads.reshape(SEQ, KV, HD))
```

```python
import functools
import math

import jax
import jax.numpy as jnp
from jax import lax
from jax.experimental import pallas as pl
from jax.experimental.pallas import tpu as pltpu
from jax.sharding import PartitionSpec as P

MESH = pl.DeviceIdType.MESH
ANY = pl.BlockSpec(memory_space=pl.ANY)
VMEM = pl.BlockSpec(memory_space=pltpu.VMEM)
SMEM = pl.BlockSpec(memory_space=pltpu.SMEM)
NEG = -1e30
FAR = 1 << 24
NX = 4
NY = 4
NZ = 8
HD = 128
ROWS = 128
SPAN = 64
GROUP = 8
SLOTS = 64
LANES = GROUP * SPAN
SCALE = 1.0 / math.sqrt(HD)
LOG2E = math.log2(math.e)
BF16 = jnp.bfloat16
F32 = jnp.float32


def place():
    inner = lax.axis_index("inner")
    return (
        lax.axis_index("head"),
        lax.axis_index("outer"),
        lax.div(inner, 2),
        lax.rem(inner, 2),
    )


def where_is(x, y, z, core):
    return {"head": x, "outer": y, "inner": z * 2 + core}


def greet(partners):
    barrier = pltpu.get_barrier_semaphore()
    for partner in partners:
        pl.semaphore_signal(barrier, inc=1, device_id=partner, device_id_type=MESH)
    pl.semaphore_wait(barrier, len(partners))


def send(src, dst, send_sem, recv_sem, partner):
    copy = pltpu.make_async_remote_copy(
        src_ref=src,
        dst_ref=dst,
        send_sem=send_sem,
        recv_sem=recv_sem,
        device_id=partner,
        device_id_type=MESH,
    )
    copy.start()
    return copy


def bring_kernel(
    q, k, v, g, q_out, g_out, kv_out,
    kv_in, kv_rows, own_sem, x_send, x_recv, y_sem, z_send, z_recv,
):
    x, y, z, core = place()
    peers = [(dx, dc) for dx in range(NX) for dc in range(2) if (dx, dc) != (0, 0)]

    def peer(dx, dc):
        return where_is(lax.rem(x + dx, NX), y, z, lax.rem(core + dc, 2))

    up = where_is(x, y, lax.rem(z + 1, NZ), core)
    down = where_is(x, y, lax.rem(z + NZ - 1, NZ), core)
    later = where_is(x, lax.rem(y + 1, NY), z, core)
    earlier = where_is(x, lax.rem(y + NY - 1, NY), z, core)
    greet([peer(*p) for p in peers] + [up, down, later, earlier])

    here = pl.ds(pl.multiple_of(x * 32, 32), 32)
    copies = []
    own = []
    for index, (dx, dc) in enumerate([(0, 0)] + peers):
        head = lax.rem(x + dx, NX) * 2 + lax.rem(core + dc, 2)
        for kind, src in enumerate((k, v)):
            dst = kv_in.at[kind, core, here]
            if index == 0:
                copy = pltpu.make_async_copy(src.at[head], dst, own_sem.at[kind])
                copy.start()
                own.append(copy)
            else:
                copies.append(
                    send(src.at[head], dst, x_send.at[kind, index], x_recv.at[kind, index], peer(dx, dc))
                )
    heads = pl.ds((x * 2 + core) * GROUP, GROUP)
    for kind, (src, dst) in enumerate(((q, q_out), (g, g_out))):
        copy = pltpu.make_async_copy(
            src.at[heads], dst.at[core, :, here], own_sem.at[2 + kind]
        )
        copy.start()
        own.append(copy)
    wide = []
    for index, (dx, dc) in enumerate([(0, 0)] + peers):
        if index == 0:
            continue
        head = lax.rem(x + dx, NX) * 2 + lax.rem(core + dc, 2)
        for kind, (src, dst) in enumerate(((q, q_out), (g, g_out))):
            wide.append(
                send(
                    src.at[pl.ds(head * GROUP, GROUP)],
                    dst.at[core, :, here],
                    x_send.at[2 + kind, index],
                    x_recv.at[2 + kind, index],
                    peer(dx, dc),
                )
            )
    own[0].wait()
    own[1].wait()
    for copy in copies:
        copy.wait()
    for kind in range(2):
        for block in range(2):
            kv_rows[kind, block * ROWS : (block + 1) * ROWS, :] = (
                kv_in[kind, block].astype(F32).T.astype(BF16)
            )
    keep = pltpu.make_async_copy(kv_rows, kv_out.at[z], own_sem.at[4])
    keep.start()

    def ring(group, step):
        waits = []
        for way in range(2):
            if step == 1 and group == 0:
                src = kv_rows
                block = z
            else:
                block = lax.rem(z + NZ + (step - 1) * (1 if way else -1), NZ)
                src = kv_out.at[group * NZ + block]
            dst = kv_out.at[group * NZ + block]
            if step == 4:
                src, dst = src.at[way], dst.at[way]
            waits.append(
                send(
                    src, dst, z_send.at[group, way, step - 1], z_recv.at[group, way, step - 1],
                    down if way else up,
                )
            )
        return waits

    flying = [ring(0, 1), None]
    shift = send(kv_rows, kv_out.at[NZ + z], y_sem.at[0], y_sem.at[1], later)
    shift.wait_recv()
    flying[1] = ring(1, 1)
    sent = []
    for step in range(2, 5):
        for group in range(2):
            for copy in flying[group]:
                copy.wait_recv()
            sent.extend(flying[group])
            flying[group] = ring(group, step)
    for group in range(2):
        for copy in flying[group]:
            copy.wait_recv()
        sent.extend(flying[group])
    for copy in sent:
        copy.wait_send()
    shift.wait_send()
    keep.wait()
    own[2].wait()
    own[3].wait()
    for copy in wide:
        copy.wait()


def bring(q, k, v, g):
    return pl.pallas_call(
        bring_kernel,
        out_shape=(
            jax.ShapeDtypeStruct((2, GROUP, HD, ROWS), BF16),
            jax.ShapeDtypeStruct((2, GROUP, HD, ROWS), BF16),
            jax.ShapeDtypeStruct((2 * NZ, 2, 2 * ROWS, HD), BF16),
        ),
        in_specs=[ANY] * 4,
        out_specs=(ANY, ANY, ANY),
        scratch_shapes=[
            pltpu.VMEM((2, 2, HD, ROWS), BF16),
            pltpu.VMEM((2, 2 * ROWS, HD), BF16),
            pltpu.SemaphoreType.DMA((5,)),
            pltpu.SemaphoreType.DMA((4, 8)),
            pltpu.SemaphoreType.DMA((4, 8)),
            pltpu.SemaphoreType.DMA((2,)),
            pltpu.SemaphoreType.DMA((2, 2, 4)),
            pltpu.SemaphoreType.DMA((2, 2, 4)),
        ],
        compiler_params=pltpu.CompilerParams(
            collective_id=0, has_side_effects=True, vmem_limit_bytes=16 << 20
        ),
        name="bring",
    )(q, k, v, g)


def attend_kernel(
    order, docs, q, g, kv, attn, dq, dkv,
    q_cols, g_cols, q_rows, g_rows, scores, key_acc, value_acc, out_acc, rows_tmp, slot_list, base_list,
):
    outer = lax.axis_index("outer")
    chip = lax.div(lax.axis_index("inner"), 2)
    doc = docs[...]
    starts = [
        jnp.sum(jnp.where(doc < d, 1.0, 0.0)).astype(jnp.int32) for d in range(1, 4)
    ]

    def start_of(position):
        found = jnp.zeros_like(position)
        for start in starts:
            found = jnp.where(position >= start, jnp.maximum(found, start), found)
        return found

    key_acc[...] = jnp.zeros_like(key_acc)
    value_acc[...] = jnp.zeros_like(value_acc)

    low = lax.broadcasted_iota(jnp.int32, (HD, ROWS), 1) < SPAN

    @pl.loop(0, 8)
    def _(index):
        block = lax.div(index, 4)
        pair = lax.rem(index, 4)
        lanes = pl.ds(pl.multiple_of(pair * ROWS, ROWS), ROWS)
        for src, cols, rows in ((q, q_cols, q_rows), (g, g_cols, g_rows)):
            first = src[block, 2 * pair].astype(F32)
            second = src[block, 2 * pair + 1].astype(F32)
            halves = (
                jnp.where(low, first, pltpu.roll(second, SPAN, 1)),
                jnp.where(low, pltpu.roll(first, SPAN, 1), second),
            )
            for half in range(2):
                cols[2 * block + half, :, lanes] = halves[half].astype(BF16)
                rows[2 * block + half, lanes, :] = halves[half].T.astype(BF16)

    iota_keys = lax.broadcasted_iota(jnp.int32, (SPAN, 256), 0)
    iota_lanes = lax.rem(lax.broadcasted_iota(jnp.int32, (1, 256), 1), SPAN)

    @pl.loop(0, 4)
    def _(unit):
        query_span = order[outer * 32 + chip * 4 + unit]
        first_span = lax.div(start_of(query_span * SPAN), SPAN)

        def note(slot, count):
            stored = lax.rem(outer + 4 - lax.div(slot, 32), 4) * 32 + lax.rem(slot, 32)
            span = order[stored]
            slot_list[count] = slot
            base_list[count] = span * SPAN
            return count + jnp.where((span >= first_span) & (span <= query_span), 1, 0)

        count = lax.fori_loop(0, SLOTS, note, 0)
        for extra in range(4):
            slot_list[count + extra] = 0
            base_list[count + extra] = FAR
        chunks = lax.div(count + 3, 4)
        query_pos = query_span * SPAN + iota_lanes
        query_start = start_of(query_pos)

        def spans(chunk, kind):
            parts = []
            for part in range(4):
                slot = slot_list[chunk * 4 + part]
                parts.append(kv[lax.div(slot, 4), kind, lax.rem(slot, 4)])
            return jnp.concatenate(parts, axis=0)

        def score_step(chunk, tops):
            keys = spans(chunk, 0)
            new = []
            for side in range(2):
                lanes = pl.ds(side * 256, 256)
                tile = jnp.dot(keys, q_cols[unit, :, lanes], preferred_element_type=F32)
                top = tops[side]
                for part in range(4):
                    base = base_list[chunk * 4 + part]
                    allowed = (iota_keys <= query_pos - base) & (iota_keys >= query_start - base)
                    piece = jnp.where(allowed, tile[part * SPAN : (part + 1) * SPAN], NEG)
                    scores[chunk, pl.ds(part * SPAN, SPAN), lanes] = piece
                    top = jnp.maximum(top, jnp.max(piece.reshape(8, 8, 256), axis=0))
                new.append(top)
            return tuple(new)

        floor = jnp.full((8, 256), NEG, F32)
        tops = lax.fori_loop(0, chunks, score_step, (floor, floor))
        row_max = [jnp.max(top, axis=0, keepdims=True) for top in tops]
        out_acc[...] = jnp.zeros_like(out_acc)

        def value_step(chunk, sums):
            values_t = spans(chunk, 1).astype(F32).T.astype(BF16)
            new = []
            for side in range(2):
                lanes = pl.ds(side * 256, 256)
                probs = jnp.exp2((scores[chunk, :, lanes] - row_max[side]) * (SCALE * LOG2E))
                scores[chunk, :, lanes] = probs
                new.append(sums[side] + jnp.sum(probs.reshape(32, 8, 256), axis=0))
                out_acc[:, lanes] += jnp.dot(
                    values_t, probs.astype(BF16), preferred_element_type=F32
                )
            return tuple(new)

        nothing = jnp.zeros((8, 256), F32)
        sums = lax.fori_loop(0, chunks, value_step, (nothing, nothing))
        inverse = []
        row_dot = []
        half_rows = pl.ds(pl.multiple_of(lax.rem(unit, 2) * LANES, LANES), LANES)
        block = lax.div(unit, 2)
        for side in range(2):
            lanes = pl.ds(side * 256, 256)
            row_sum = jnp.sum(sums[side], axis=0, keepdims=True)
            inverse.append(1.0 / row_sum)
            out = (out_acc[:, lanes] / row_sum).astype(BF16).astype(F32)
            row_dot.append(
                jnp.sum(out * g_cols[unit, :, lanes].astype(F32), axis=0, keepdims=True)
            )
            out_t = out.T
            for part in range(4):
                rows_tmp[pl.ds(side * 4 + part, SPAN, stride=GROUP), :] = out_t[
                    part * SPAN : (part + 1) * SPAN
                ]
        attn[block, half_rows, :] = rows_tmp[...].astype(BF16)
        out_acc[...] = jnp.zeros_like(out_acc)

        def grad_step(chunk, _):
            keys = spans(chunk, 0)
            values = spans(chunk, 1)
            keys_t = keys.astype(F32).T.astype(BF16)
            key_part = None
            value_part = None
            for side in range(2):
                lanes = pl.ds(side * 256, 256)
                probs = scores[chunk, :, lanes] * inverse[side]
                prob_grads = jnp.dot(values, g_cols[unit, :, lanes], preferred_element_type=F32)
                score_grads = (probs * (prob_grads - row_dot[side])).astype(BF16)
                out_acc[:, lanes] += jnp.dot(keys_t, score_grads, preferred_element_type=F32)
                to_values = jnp.dot(
                    probs.astype(BF16), g_rows[unit, lanes, :], preferred_element_type=F32
                )
                to_keys = jnp.dot(score_grads, q_rows[unit, lanes, :], preferred_element_type=F32)
                value_part = to_values if side == 0 else value_part + to_values
                key_part = to_keys if side == 0 else key_part + to_keys
            for part in range(4):
                slot = slot_list[chunk * 4 + part]
                rows = slice(part * SPAN, (part + 1) * SPAN)
                key_acc[slot] += key_part[rows]
                value_acc[slot] += value_part[rows]
            return 0

        lax.fori_loop(0, chunks, grad_step, 0)
        for side in range(2):
            grad_t = (out_acc[:, pl.ds(side * 256, 256)] * SCALE).T
            for part in range(4):
                rows_tmp[pl.ds(side * 4 + part, SPAN, stride=GROUP), :] = grad_t[
                    part * SPAN : (part + 1) * SPAN
                ]
        dq[block, half_rows, :] = rows_tmp[...]

    @pl.loop(0, 2 * NZ)
    def _(index):
        for part in range(4):
            dkv[index, 0, part] = (key_acc[index * 4 + part] * SCALE).astype(BF16)
            dkv[index, 1, part] = value_acc[index * 4 + part].astype(BF16)


def attend(order, docs, q, g, kv):
    return pl.pallas_call(
        attend_kernel,
        out_shape=(
            jax.ShapeDtypeStruct((2, ROWS * GROUP, HD), BF16),
            jax.ShapeDtypeStruct((2, ROWS * GROUP, HD), F32),
            jax.ShapeDtypeStruct((2 * NZ, 2, 4, SPAN, HD), BF16),
        ),
        in_specs=[SMEM, VMEM, VMEM, VMEM, VMEM],
        out_specs=(VMEM, VMEM, VMEM),
        scratch_shapes=[
            pltpu.VMEM((4, HD, LANES), BF16),
            pltpu.VMEM((4, HD, LANES), BF16),
            pltpu.VMEM((4, LANES, HD), BF16),
            pltpu.VMEM((4, LANES, HD), BF16),
            pltpu.VMEM((SLOTS // 4, 4 * SPAN, LANES), F32),
            pltpu.VMEM((SLOTS, SPAN, HD), F32),
            pltpu.VMEM((SLOTS, SPAN, HD), F32),
            pltpu.VMEM((HD, LANES), F32),
            pltpu.VMEM((LANES, HD), F32),
            pltpu.SMEM((SLOTS + 8,), jnp.int32),
            pltpu.SMEM((SLOTS + 8,), jnp.int32),
        ],
        compiler_params=pltpu.CompilerParams(vmem_limit_bytes=48 << 20),
        cost_estimate=pl.CostEstimate(
            flops=6 * 2 * 2048 * 2048 * HD, bytes_accessed=12 << 20, transcendentals=2048 * 2048
        ),
        name="attend",
    )(order, docs, q, g, kv)


def return_kernel(
    attn, dq, dkv, attn_out, dq_out, dkv_out,
    landed, summed, from_later, final, pair_send, pair_recv, own_sem, y_sem, z_send, z_recv,
):
    x, y, z, core = place()
    sibling = where_is(x, y, z, 1 - core)
    up = where_is(x, y, lax.rem(z + 1, NZ), core)
    down = where_is(x, y, lax.rem(z + NZ - 1, NZ), core)
    later = where_is(x, lax.rem(y + 1, NY), z, core)
    earlier = where_is(x, lax.rem(y + NY - 1, NY), z, core)
    greet([sibling, up, down, later, earlier])

    def ring(group, step):
        sends = []
        for way in range(2):
            if step == 1:
                block = lax.rem(z + 4, NZ)
                src = dkv.at[group * NZ + block, way]
                dst = landed.at[group, way, 0, way]
            else:
                src = landed.at[group, way, step - 2]
                dst = landed.at[group, way, step - 1]
            sends.append(
                send(
                    src, dst, z_send.at[group, way, step - 1], z_recv.at[group, way, step - 1],
                    down if way else up,
                )
            )
        return sends

    def add(group, step):
        for way in range(2):
            block = lax.rem(z + NZ + (4 - step) * (-1 if way else 1), NZ)
            for kind in range(2):
                term = dkv[group * NZ + block, kind]
                if step > 1 or kind == way:
                    term = (
                        landed[group, way, step - 1, kind].astype(F32) + term.astype(F32)
                    ).astype(BF16)
                landed[group, way, step - 1, kind] = term

    flying = [None, None]
    flying[1] = ring(1, 1)
    flying[0] = ring(0, 1)
    swaps = []
    own = []
    for kind, (src, dst) in enumerate(((attn, attn_out), (dq, dq_out))):
        swaps.append(
            send(src.at[1 - core], dst.at[core], pair_send.at[kind], pair_recv.at[kind], sibling)
        )
        copy = pltpu.make_async_copy(src.at[core], dst.at[core], own_sem.at[kind])
        copy.start()
        own.append(copy)
    sent = []
    for step in range(1, 4):
        for group in (1, 0):
            for copy in flying[group]:
                copy.wait_recv()
            sent.extend(flying[group])
            add(group, step)
            flying[group] = ring(group, step + 1)
    back = None
    for group in (1, 0):
        for copy in flying[group]:
            copy.wait_recv()
        sent.extend(flying[group])
        for kind in range(2):
            total = (
                landed[group, 0, 3, kind].astype(F32)
                + landed[group, 1, 3, kind].astype(F32)
                + dkv[group * NZ + z, kind].astype(F32)
            )
            if group == 1:
                summed[kind] = total.astype(BF16)
            else:
                final[kind] = total
        if group == 1:
            back = send(summed, from_later, y_sem.at[0], y_sem.at[1], earlier)
    back.wait_recv()
    for kind in range(2):
        final[kind] = final[kind] + from_later[kind].astype(F32)
    mine = pl.ds(pl.multiple_of(core * ROWS, ROWS), ROWS)
    other = pl.ds(pl.multiple_of((1 - core) * ROWS, ROWS), ROWS)
    for kind in range(2):
        swaps.append(
            send(
                final.at[kind, other], dkv_out.at[kind, core],
                pair_send.at[2 + kind], pair_recv.at[2 + kind], sibling,
            )
        )
        copy = pltpu.make_async_copy(
            final.at[kind, mine], dkv_out.at[kind, core], own_sem.at[2 + kind]
        )
        copy.start()
        own.append(copy)
    for copy in sent:
        copy.wait_send()
    back.wait_send()
    for copy in swaps:
        copy.wait()
    for copy in own:
        copy.wait()


def give_back(attn, dq, dkv):
    return pl.pallas_call(
        return_kernel,
        out_shape=(
            jax.ShapeDtypeStruct((2, ROWS * GROUP, HD), BF16),
            jax.ShapeDtypeStruct((2, ROWS * GROUP, HD), F32),
            jax.ShapeDtypeStruct((2, 2, ROWS, HD), F32),
        ),
        in_specs=[ANY, ANY, VMEM],
        out_specs=(ANY, ANY, ANY),
        scratch_shapes=[
            pltpu.VMEM((2, 2, 4, 2, 2 * ROWS, HD), BF16),
            pltpu.VMEM((2, 2 * ROWS, HD), BF16),
            pltpu.VMEM((2, 2 * ROWS, HD), BF16),
            pltpu.VMEM((2, 2 * ROWS, HD), F32),
            pltpu.SemaphoreType.DMA((4,)),
            pltpu.SemaphoreType.DMA((4,)),
            pltpu.SemaphoreType.DMA((4,)),
            pltpu.SemaphoreType.DMA((2,)),
            pltpu.SemaphoreType.DMA((2, 2, 4)),
            pltpu.SemaphoreType.DMA((2, 2, 4)),
        ],
        compiler_params=pltpu.CompilerParams(
            collective_id=1, has_side_effects=True, vmem_limit_bytes=24 << 20
        ),
        name="give_back",
    )(attn, dq, dkv)


def local(queries, keys, values, grad_out, span_order, doc_ids):
    turned = [jnp.transpose(a, (1, 2, 0)) for a in (queries, keys, values, grad_out)]
    q, g, kv = bring(*turned)
    kv = kv.reshape(2 * NZ, 2, 4, SPAN, HD)
    attn, dq, dkv = attend(span_order, doc_ids.reshape(64, 128), q, g, kv)
    attn, dq, dkv = give_back(attn, dq, dkv.reshape(2 * NZ, 2, 2 * ROWS, HD))

    def join(halves):
        return (
            halves.reshape(2, ROWS, GROUP, HD)
            .transpose(1, 0, 2, 3)
            .reshape(ROWS, 2 * GROUP, HD)
        )

    grads = dkv.transpose(0, 2, 1, 3)
    return (join(attn), join(dq), grads[0], grads[1])


def solution(mesh):
    entry = P(("outer", "inner"), None, "head")
    leave = P(("outer", "inner"), "head", None)
    return jax.shard_map(
        local,
        mesh=mesh,
        in_specs=(entry, entry, entry, entry, P(), P()),
        out_specs=(leave, leave, leave, leave),
        check_vma=False,
    )
```

```python
import functools
import math

import jax
import jax.numpy as jnp
from jax import lax
from jax.experimental import pallas as pl
from jax.experimental.pallas import tpu as pltpu
from jax.sharding import PartitionSpec as P

MESH = pl.DeviceIdType.MESH
HBM = pl.BlockSpec(memory_space=pltpu.HBM)
NEG = -1e30
FAR = 1 << 24
NX = 4
NY = 4
NZ = 8
HD = 128
ROWS = 128
SPAN = 64
GROUP = 8
SLOTS = 64
LANES = GROUP * SPAN
SCALE = 1.0 / math.sqrt(HD)
LOG2E = math.log2(math.e)
ITEM = 4
BF16 = jnp.bfloat16
F32 = jnp.float32


def place():
    inner = lax.axis_index("inner")
    return (
        lax.axis_index("head"),
        lax.axis_index("outer"),
        lax.div(inner, 2),
        lax.rem(inner, 2),
    )


def where_is(x, y, z, core):
    return {"head": x, "outer": y, "inner": z * 2 + core}


def greet(partners):
    barrier = pltpu.get_barrier_semaphore()
    for partner in partners:
        pl.semaphore_signal(barrier, inc=1, device_id=partner, device_id_type=MESH)
    pl.semaphore_wait(barrier, len(partners))


def send(src, dst, send_sem, recv_sem, partner):
    copy = pltpu.make_async_remote_copy(
        src_ref=src,
        dst_ref=dst,
        send_sem=send_sem,
        recv_sem=recv_sem,
        device_id=partner,
        device_id_type=MESH,
    )
    copy.start()
    return copy


def bring_kernel(
    q, k, v, g, q_cols_out, g_cols_out, q_rows_out, g_rows_out, kv_out,
    q_cols, g_cols, q_rows, g_rows, out_sem, q_in, g_in, kv_in, ring_kv, own_sem, keep_sem, x_send, x_recv, y_send, y_recv, z_send, z_recv,
):
    x, y, z, core = place()
    peers = [(dx, dc) for dx in range(NX) for dc in range(2) if (dx, dc) != (0, 0)]

    def peer(dx, dc):
        return where_is(lax.rem(x + dx, NX), y, z, lax.rem(core + dc, 2))

    up = where_is(x, y, lax.rem(z + 1, NZ), core)
    down = where_is(x, y, lax.rem(z + NZ - 1, NZ), core)
    later = where_is(x, lax.rem(y + 1, NY), z, core)
    earlier = where_is(x, lax.rem(y + NY - 1, NY), z, core)
    greet([peer(*p) for p in peers] + [up, down, later, earlier])

    here = pl.ds(pl.multiple_of(x * 32, 32), 32)
    copies = []
    own = []
    for index, (dx, dc) in enumerate([(0, 0)] + peers):
        head = lax.rem(x + dx, NX) * 2 + lax.rem(core + dc, 2)
        for kind, src in enumerate((k, v)):
            dst = kv_in.at[kind, core, here]
            if index == 0:
                copy = pltpu.make_async_copy(src.at[head], dst, own_sem.at[kind])
                copy.start()
                own.append(copy)
            else:
                copies.append(
                    send(src.at[head], dst, x_send.at[kind, index], x_recv.at[kind, index], peer(dx, dc))
                )
    own[0].wait()
    own[1].wait()
    for copy in copies:
        copy.wait()
    for kind in range(2):
        for block in range(2):
            ring_kv[z, kind, block * ROWS : (block + 1) * ROWS, :] = (
                kv_in[kind, block].astype(F32).T.astype(BF16)
            )
    keeps = []
    sent = []
    ways = (up, down)

    def block_at(group, way, step):
        return group * NZ + lax.rem(z + NZ + step * (1 if way else -1), NZ)

    def keep(block, index):
        copy = pltpu.make_async_copy(ring_kv.at[block], kv_out.at[block], keep_sem.at[index])
        copy.start()
        keeps.append(copy)

    def hop(group, way, step, kind):
        block = block_at(group, way, step - 1)
        copy = send(
            ring_kv.at[block, kind], ring_kv.at[block, kind],
            z_send.at[group, way, step - 1, kind], z_recv.at[group, way, step - 1, kind],
            ways[way],
        )
        sent.append(copy)
        return copy

    def shift(way, step, kind):
        block = block_at(0, way, step)
        copy = send(
            ring_kv.at[block, kind], ring_kv.at[NZ + block, kind],
            y_send.at[way, step // 2, kind], y_recv.at[way, step // 2, kind], later,
        )
        sent.append(copy)
        return copy

    def settle(kind):
        src, cols, rows = ((q_in, q_cols, q_rows), (g_in, g_cols, g_rows))[kind]
        own[2 + kind].wait()
        for copy in wide[kind]:
            copy.wait()
        low = lax.broadcasted_iota(jnp.int32, (HD, ROWS), 1) < SPAN

        @pl.loop(0, 8)
        def _(index):
            block = lax.div(index, 4)
            pair = lax.rem(index, 4)
            lanes = pl.ds(pl.multiple_of(pair * ROWS, ROWS), ROWS)
            first = src[block, 2 * pair].astype(F32)
            second = src[block, 2 * pair + 1].astype(F32)
            halves = (
                jnp.where(low, first, pltpu.roll(second, SPAN, 1)),
                jnp.where(low, pltpu.roll(first, SPAN, 1), second),
            )
            for half in range(2):
                cols[2 * block + half, :, lanes] = halves[half].astype(BF16)
                rows[2 * block + half, lanes, :] = halves[half].T.astype(BF16)

        outs = ((q_cols_out, q_rows_out), (g_cols_out, g_rows_out))[kind]
        for index, (src, dst) in enumerate(zip((cols, rows), outs)):
            copy = pltpu.make_async_copy(src, dst, out_sem.at[kind, index])
            copy.start()
            own.append(copy)

    near = {}
    self_shift = {}
    for kind in range(2):
        for way in range(2):
            near[way, 1, kind] = hop(0, way, 1, kind)
        self_shift[kind] = shift(0, 0, kind)
    keep(z, 0)
    heads = pl.ds((x * 2 + core) * GROUP, GROUP)
    for kind, (src, dst) in enumerate(((q, q_in), (g, g_in))):
        copy = pltpu.make_async_copy(
            src.at[heads], dst.at[core, :, here], own_sem.at[2 + kind]
        )
        copy.start()
        own.append(copy)
    wide = ([], [])
    for kind, (src, dst) in enumerate(((q, q_in), (g, g_in))):
        for index, (dx, dc) in enumerate(peers):
            head = lax.rem(x + dx, NX) * 2 + lax.rem(core + dc, 2)
            wide[kind].append(
                send(
                    src.at[pl.ds(head * GROUP, GROUP)],
                    dst.at[core, :, here],
                    x_send.at[2 + kind, index],
                    x_recv.at[2 + kind, index],
                    peer(dx, dc),
                )
            )
    far_shift = {}
    for step in range(1, 4):
        for kind in range(2):
            for way in range(2):
                near[way, step, kind].wait_recv()
                if step < 3 or kind == way:
                    near[way, step + 1, kind] = hop(0, way, step + 1, kind)
                if step == 2:
                    far_shift[way, kind] = shift(way, 2, kind)
        for way in range(2):
            keep(block_at(0, way, step), 1 + 2 * step + way)
    hops = {}
    for kind in range(2):
        self_shift[kind].wait_recv()
        for way in range(2):
            hops[way, 1, kind] = hop(1, way, 1, kind)
    keep(NZ + z, 1)
    last_shift = []
    for way in range(2):
        near[way, 4, way].wait_recv()
        last_shift.append(shift(way, 4, way))
    keep(block_at(0, 0, 4), 2)
    for kind in range(2):
        for way in range(2):
            far_shift[way, kind].wait_recv()
            hops[way, 3, kind] = hop(1, way, 3, kind)
    for way in range(2):
        keep(block_at(1, way, 2), 9 + way)
    settle(0)
    for step in (1, 3):
        for way in range(2):
            for kind in range(2):
                hops[way, step, kind].wait_recv()
            keep(block_at(1, way, step), 10 + step + way)
        if step == 1:
            for way in range(2):
                last_shift[way].wait_recv()
            keep(block_at(1, 0, 4), 15)
            settle(1)
    for copy in sent:
        copy.wait_send()
    for copy in keeps:
        copy.wait()
    for copy in own[4:]:
        copy.wait()


def bring(q, k, v, g):
    return pl.pallas_call(
        bring_kernel,
        out_shape=(
            jax.ShapeDtypeStruct((4, HD, LANES), BF16),
            jax.ShapeDtypeStruct((4, HD, LANES), BF16),
            jax.ShapeDtypeStruct((4, LANES, HD), BF16),
            jax.ShapeDtypeStruct((4, LANES, HD), BF16),
            jax.ShapeDtypeStruct((2 * NZ, 2, 2 * ROWS, HD), BF16),
        ),
        in_specs=[HBM] * 4,
        out_specs=(HBM,) * 5,
        scratch_shapes=[
            pltpu.VMEM((4, HD, LANES), BF16),
            pltpu.VMEM((4, HD, LANES), BF16),
            pltpu.VMEM((4, LANES, HD), BF16),
            pltpu.VMEM((4, LANES, HD), BF16),
            pltpu.SemaphoreType.DMA((2, 2)),
            pltpu.VMEM((2, GROUP, HD, ROWS), BF16),
            pltpu.VMEM((2, GROUP, HD, ROWS), BF16),
            pltpu.VMEM((2, 2, HD, ROWS), BF16),
            pltpu.VMEM((2 * NZ, 2, 2 * ROWS, HD), BF16),
            pltpu.SemaphoreType.DMA((4,)),
            pltpu.SemaphoreType.DMA((16,)),
            pltpu.SemaphoreType.DMA((4, 8)),
            pltpu.SemaphoreType.DMA((4, 8)),
            pltpu.SemaphoreType.DMA((2, 3, 2)),
            pltpu.SemaphoreType.DMA((2, 3, 2)),
            pltpu.SemaphoreType.DMA((2, 2, 4, 2)),
            pltpu.SemaphoreType.DMA((2, 2, 4, 2)),
        ],
        compiler_params=pltpu.CompilerParams(
            collective_id=0, has_side_effects=True, vmem_limit_bytes=60 << 20
        ),
        name="bring",
    )(q, k, v, g)


def attend_kernel(
    order_in, docs_in, q_cols_in, g_cols_in, q_rows_in, g_rows_in, kv_in, attn_out, dq_out, dkv,
    order, docs, q_cols, g_cols, q_rows, g_rows, attn, dq, kv, scores, key_acc, value_acc, out_acc, tops, sums, shift, dots,
    pos_rows, start_rows, item_list, span_list, in_sem, out_sem,
):
    outer = lax.axis_index("outer")
    chip = lax.div(lax.axis_index("inner"), 2)
    loads = [
        pltpu.make_async_copy(order_in, order, in_sem.at[0]),
        pltpu.make_async_copy(docs_in, docs, in_sem.at[1]),
        pltpu.make_async_copy(q_cols_in, q_cols, in_sem.at[2]),
        pltpu.make_async_copy(kv_in.at[:, 0], kv.at[:, 0], in_sem.at[3]),
        pltpu.make_async_copy(kv_in.at[:, 1], kv.at[:, 1], in_sem.at[4]),
        pltpu.make_async_copy(g_cols_in, g_cols, in_sem.at[5]),
        pltpu.make_async_copy(q_rows_in, q_rows, in_sem.at[6]),
        pltpu.make_async_copy(g_rows_in, g_rows, in_sem.at[7]),
    ]
    for load in loads:
        load.start()
    key_acc[...] = jnp.zeros_like(key_acc)
    value_acc[...] = jnp.zeros_like(value_acc)
    out_acc[...] = jnp.zeros_like(out_acc)
    dq[...] = jnp.zeros_like(dq)
    tops[...] = jnp.full_like(tops, NEG)
    sums[...] = jnp.zeros_like(sums)
    loads[0].wait()
    loads[1].wait()
    doc = docs[...]
    starts = [
        jnp.sum(jnp.where(doc < d, 1.0, 0.0)).astype(jnp.int32) for d in range(1, 4)
    ]

    def start_of(position):
        found = jnp.zeros_like(position)
        for start in starts:
            found = jnp.where(position >= start, jnp.maximum(found, start), found)
        return found

    iota_lanes = lax.rem(lax.broadcasted_iota(jnp.int32, (8, ROWS), 1), SPAN)
    lows = []
    highs = []
    for unit in range(4):
        query_span = order[outer * 32 + chip * 4 + unit]
        lows.append(lax.div(start_of(query_span * SPAN), SPAN))
        highs.append(query_span)
        query_pos = query_span * SPAN + iota_lanes
        pos_rows[unit] = query_pos
        start_rows[unit] = start_of(query_pos)

    counts = tuple(jnp.int32(unit * 128) for unit in range(4))
    for group in range(2):
        stored = lax.rem(outer + 4 - group, 4) * 32

        def note(step, counts):
            for part in range(8):
                slot = step * 8 + part
                span = order[stored + slot]
                entry = span * SPAN + (group * 32 + slot)
                new = []
                for unit in range(4):
                    span_list[counts[unit]] = entry
                    allowed = (span >= lows[unit]) & (span <= highs[unit])
                    new.append(counts[unit] + jnp.where(allowed, 1, 0))
                counts = tuple(new)
            return counts

        counts = lax.fori_loop(0, 4, note, counts)
    items = jnp.int32(0)
    for unit in range(4):
        for extra in range(ITEM):
            span_list[counts[unit] + extra] = FAR
        for chunk in range(SLOTS // ITEM):
            item_list[items + chunk] = unit * 128 + chunk * ITEM
        items = items + lax.div(counts[unit] - unit * 128 + ITEM - 1, ITEM)
    blank = 3 * 128 + 72
    for extra in range(ITEM):
        span_list[blank + extra] = FAR
    item_list[items] = blank
    steps = lax.div(items + 1, 2)

    iota_keys = (
        lax.broadcasted_iota(jnp.int32, (8, 8, ROWS), 0) * 8
        + lax.broadcasted_iota(jnp.int32, (8, 8, ROWS), 1)
    )

    def entries(item):
        first = item_list[item]
        found = [span_list[first + part] for part in range(ITEM)]
        slots = [lax.rem(entry, SLOTS) for entry in found]
        return lax.div(first, 128), slots, [a - b for a, b in zip(found, slots)]

    def spans(slots, kind):
        parts = []
        for slot in slots:
            parts.append(kv[lax.div(slot, 4), kind, lax.rem(slot, 4)])
        return jnp.concatenate(parts, axis=0)

    sides = [pl.ds(side * 256, 256) for side in range(2)]
    loads[2].wait()
    loads[3].wait()

    @functools.partial(lax.fori_loop, 0, steps, init_val=0)
    def _(step, _):
        results = []
        for item in (2 * step, 2 * step + 1):
            unit, slots, bases = entries(item)
            keys = spans(slots, 0)
            biases = []
            for base in bases:
                allowed = (iota_keys <= (pos_rows[unit] - base)[None]) & (
                    iota_keys >= (start_rows[unit] - base)[None]
                )
                biases.append(jnp.where(allowed, 0.0, NEG).reshape(SPAN, ROWS))
            bias = jnp.concatenate(biases, axis=0)
            bias = jnp.concatenate([bias, bias], axis=1)
            for lanes in sides:
                tile = jnp.dot(keys, q_cols[unit, :, lanes], preferred_element_type=F32)
                tile = tile * (SCALE * LOG2E) + bias
                scores[item, :, lanes] = tile
                results.append((unit, lanes, jnp.max(tile.reshape(32, 8, 256), axis=0)))
        for unit, lanes, top in results:
            tops[unit, :, lanes] = jnp.maximum(tops[unit, :, lanes], top)
        return 0

    for unit in range(4):
        shift[unit] = jnp.broadcast_to(jnp.max(tops[unit], axis=0, keepdims=True), (8, LANES))
    loads[4].wait()

    @functools.partial(lax.fori_loop, 0, steps, init_val=0)
    def _(step, _):
        results = []
        for item in (2 * step, 2 * step + 1):
            unit, slots, _ = entries(item)
            values_t = spans(slots, 1).T
            for lanes in sides:
                logits = scores[item, :, lanes].reshape(32, 8, 256)
                probs = jnp.exp2(logits - shift[unit, :, lanes][None])
                part = jnp.dot(
                    values_t, probs.reshape(256, 256).astype(BF16), preferred_element_type=F32
                )
                results.append((unit, lanes, jnp.sum(probs, axis=0), part))
        for unit, lanes, total, part in results:
            sums[unit, :, lanes] += total
            out_acc[unit, :, lanes] += part
        return 0

    for load in loads[5:]:
        load.wait()
    for unit in range(4):
        row_sum = jnp.sum(sums[unit], axis=0, keepdims=True)
        out = (out_acc[unit] * (1.0 / row_sum)).astype(BF16)
        attn[unit] = out
        row_dot = jnp.sum(
            out.astype(F32) * g_cols[unit].astype(F32), axis=0, keepdims=True
        )
        dots[unit] = jnp.broadcast_to(row_dot, (8, LANES))
        shift[unit] = shift[unit] + jnp.log(row_sum) * LOG2E
    attn_store = pltpu.make_async_copy(attn, attn_out, out_sem.at[2 * NZ])
    attn_store.start()

    @functools.partial(lax.fori_loop, 0, steps, init_val=0)
    def _(step, _):
        results = []
        for item in (2 * step, 2 * step + 1):
            unit, slots, _ = entries(item)
            keys = spans(slots, 0)
            values = spans(slots, 1)
            keys_t = keys.T
            probs_b = []
            score_grads = []
            for lanes in sides:
                logits = scores[item, :, lanes].reshape(32, 8, 256)
                probs = jnp.exp2(logits - shift[unit, :, lanes][None])
                grads = jnp.dot(values, g_cols[unit, :, lanes], preferred_element_type=F32)
                grads = probs * (grads.reshape(32, 8, 256) - dots[unit, :, lanes][None])
                probs_b.append(probs.reshape(256, 256).astype(BF16))
                score_grads.append(grads.reshape(256, 256).astype(BF16))
            probs_b = jnp.concatenate(probs_b, axis=1)
            score_grads = jnp.concatenate(score_grads, axis=1)
            to_values = jnp.dot(probs_b, g_rows[unit], preferred_element_type=F32)
            to_keys = jnp.dot(score_grads, q_rows[unit], preferred_element_type=F32)
            to_query = jnp.dot(keys_t, score_grads, preferred_element_type=F32)
            results.append((slots, unit, to_values, to_keys, to_query))
        for slots, unit, to_values, to_keys, to_query in results:
            dq[unit] += to_query
            for part, slot in enumerate(slots):
                rows = slice(part * SPAN, (part + 1) * SPAN)
                key_acc[slot] += to_keys[rows]
                value_acc[slot] += to_values[rows]
        return 0

    dq_store = pltpu.make_async_copy(dq, dq_out, out_sem.at[2 * NZ + 1])
    dq_store.start()
    stores = [attn_store, dq_store]
    for index in range(2 * NZ):
        for part in range(4):
            kv[index, 0, part] = (key_acc[index * 4 + part] * SCALE).astype(BF16)
            kv[index, 1, part] = value_acc[index * 4 + part].astype(BF16)
        store = pltpu.make_async_copy(kv.at[index], dkv.at[index], out_sem.at[index])
        store.start()
        stores.append(store)
    for store in stores:
        store.wait()


def attend(order, docs, q_cols, g_cols, q_rows, g_rows, kv):
    return pl.pallas_call(
        attend_kernel,
        out_shape=(
            jax.ShapeDtypeStruct((4, HD, LANES), BF16),
            jax.ShapeDtypeStruct((4, HD, LANES), F32),
            jax.ShapeDtypeStruct((2 * NZ, 2, 4, SPAN, HD), BF16),
        ),
        in_specs=[HBM] * 7,
        out_specs=(HBM,) * 3,
        scratch_shapes=[
            pltpu.SMEM((2 * SLOTS,), jnp.int32),
            pltpu.VMEM((SLOTS, ROWS), jnp.int32),
            pltpu.VMEM((4, HD, LANES), BF16),
            pltpu.VMEM((4, HD, LANES), BF16),
            pltpu.VMEM((4, LANES, HD), BF16),
            pltpu.VMEM((4, LANES, HD), BF16),
            pltpu.VMEM((4, HD, LANES), BF16),
            pltpu.VMEM((4, HD, LANES), F32),
            pltpu.VMEM((2 * NZ, 2, 4, SPAN, HD), BF16),
            pltpu.VMEM((4 * SLOTS // ITEM, ITEM * SPAN, LANES), F32),
            pltpu.VMEM((SLOTS, SPAN, HD), F32),
            pltpu.VMEM((SLOTS, SPAN, HD), F32),
            pltpu.VMEM((4, HD, LANES), F32),
            pltpu.VMEM((4, 8, LANES), F32),
            pltpu.VMEM((4, 8, LANES), F32),
            pltpu.VMEM((4, 8, LANES), F32),
            pltpu.VMEM((4, 8, LANES), F32),
            pltpu.VMEM((4, 8, ROWS), jnp.int32),
            pltpu.VMEM((4, 8, ROWS), jnp.int32),
            pltpu.SMEM((80,), jnp.int32),
            pltpu.SMEM((512,), jnp.int32),
            pltpu.SemaphoreType.DMA((8,)),
            pltpu.SemaphoreType.DMA((2 * NZ + 2,)),
        ],
        compiler_params=pltpu.CompilerParams(vmem_limit_bytes=60 << 20),
        cost_estimate=pl.CostEstimate(
            flops=6 * 2 * 2048 * 2048 * HD, bytes_accessed=12 << 20, transcendentals=2048 * 2048
        ),
        name="attend",
    )(order, docs, q_cols, g_cols, q_rows, g_rows, kv)


def return_kernel(
    attn_in, dq_in, dkv, attn_out, dq_out, dkv_out,
    attn, dq, terms, attn_rows, dq_rows, rows_tmp, landed, final, pair_send, pair_recv, own_sem, l_send, l_recv,
):
    x, y, z, core = place()
    sibling = where_is(x, y, z, 1 - core)
    up = where_is(x, y, lax.rem(z + 1, NZ), core)
    down = where_is(x, y, lax.rem(z + NZ - 1, NZ), core)
    later = where_is(x, lax.rem(y + 1, NY), z, core)
    earlier = where_is(x, lax.rem(y + NY - 1, NY), z, core)
    loads = [
        pltpu.make_async_copy(attn_in, attn, own_sem.at[5]),
        pltpu.make_async_copy(dq_in, dq, own_sem.at[6]),
        pltpu.make_async_copy(dkv, terms, own_sem.at[4]),
    ]
    for load in loads:
        load.start()
    greet([sibling, up, down, later, earlier])

    ways = (up, down)
    sent = []

    def at(group, distance, way):
        return group * NZ + lax.rem(z + NZ + distance * (-1 if way else 1), NZ)

    def ship(src, index, partner):
        copy = send(src, landed.at[index], l_send.at[index], l_recv.at[index], partner)
        sent.append(copy)
        return copy

    def add(block, kind, *indices):
        total = terms[block, kind].astype(F32)
        for index in indices:
            total = total + landed[index].astype(F32)
        terms[block, kind] = total.astype(BF16)

    flying = {}
    for step, distance in ((0, 3), (1, 1)):
        for kind in range(2):
            for way in range(2):
                flying["z", step, way, kind] = ship(
                    dkv.at[at(1, distance, way), kind], step * 4 + way * 2 + kind, ways[way]
                )
        if step == 0:
            for kind in range(2):
                flying["y", 4, kind] = ship(dkv.at[at(1, 4, 0), kind], 8 + kind, earlier)
    swaps = []
    own = []

    def turn(block):
        for half in range(2):
            unit = 2 * block + half
            rows = pl.ds(half * LANES, LANES)
            for source, scale, target in ((attn, None, rows_tmp), (dq, SCALE, dq_rows.at[block, rows])):
                for pair in range(4):
                    tile = source[unit, :, pair * ROWS : (pair + 1) * ROWS].astype(F32)
                    tile = tile.T if scale is None else (tile * scale).T
                    for part in range(2):
                        target[pl.ds(2 * pair + part, SPAN, stride=GROUP), :] = tile[
                            part * SPAN : (part + 1) * SPAN
                        ]
                if scale is None:
                    attn_rows[block, rows, :] = rows_tmp[...].astype(BF16)

    def swap():
        turn(1 - core)
        for kind, (src, dst) in enumerate(((attn_rows, attn_out), (dq_rows, dq_out))):
            swaps.append(
                send(src.at[1 - core], dst.at[core], pair_send.at[kind], pair_recv.at[kind], sibling)
            )

    def stay():
        turn(core)
        for kind, (src, dst) in enumerate(((attn_rows, attn_out), (dq_rows, dq_out))):
            copy = pltpu.make_async_copy(src.at[core], dst.at[core], own_sem.at[kind])
            copy.start()
            own.append(copy)

    loads[2].wait()
    for kind in range(2):
        for way in range(2):
            flying["z", 0, way, kind].wait_recv()
            block = at(1, 2, way)
            add(block, kind, way * 2 + kind)
            flying["y", 2, way, kind] = ship(
                terms.at[block, kind], 10 + way * 2 + kind, earlier
            )
    for way in range(2):
        flying["y", 4, way].wait_recv()
        block = at(0, 4, 0)
        add(block, way, 8 + way)
        flying["s", 1, way, way] = ship(terms.at[block, way], 16 + way, ways[way])
    for way in range(2):
        kind = 1 - way
        flying["s", 2, way, kind] = ship(
            terms.at[at(0, 3, way), kind], 18 + way * 2 + kind, ways[way]
        )
    loads[0].wait()
    loads[1].wait()
    swap()
    for way in range(2):
        flying["s", 1, way, way].wait_recv()
        add(at(0, 3, way), way, 16 + way)
        flying["s", 2, way, way] = ship(
            terms.at[at(0, 3, way), way], 18 + way * 2 + way, ways[way]
        )
    for kind in range(2):
        for way in range(2):
            flying["z", 1, way, kind].wait_recv()
        add(NZ + z, kind, 4 + kind, 6 + kind)
        flying["y", 0, kind] = ship(terms.at[NZ + z, kind], 14 + kind, earlier)
    for step in (3, 4):
        for turn_of in range(2):
            for way in range(2):
                kind = turn_of if way else 1 - turn_of
                flying["s", step - 1, way, kind].wait_recv()
                indices = [18 + (step - 3) * 4 + way * 2 + kind]
                if step == 3:
                    flying["y", 2, way, kind].wait_recv()
                    indices.append(10 + way * 2 + kind)
                block = at(0, 5 - step, way)
                add(block, kind, *indices)
                flying["s", step, way, kind] = ship(
                    terms.at[block, kind], 18 + (step - 2) * 4 + way * 2 + kind, ways[way]
                )
        if step == 3:
            stay()
    for kind in range(2):
        flying["y", 0, kind].wait_recv()
        for way in range(2):
            flying["s", 4, way, kind].wait_recv()
        total = terms[z, kind].astype(F32)
        for index in (14 + kind, 26 + kind, 28 + kind):
            total = total + landed[index].astype(F32)
        final[kind] = total
    mine = pl.ds(pl.multiple_of(core * ROWS, ROWS), ROWS)
    other = pl.ds(pl.multiple_of((1 - core) * ROWS, ROWS), ROWS)
    for kind in range(2):
        swaps.append(
            send(
                final.at[kind, other], dkv_out.at[kind, core],
                pair_send.at[2 + kind], pair_recv.at[2 + kind], sibling,
            )
        )
        copy = pltpu.make_async_copy(
            final.at[kind, mine], dkv_out.at[kind, core], own_sem.at[2 + kind]
        )
        copy.start()
        own.append(copy)
    for copy in sent:
        copy.wait_send()
    for copy in swaps:
        copy.wait()
    for copy in own:
        copy.wait()


def give_back(attn, dq, dkv):
    return pl.pallas_call(
        return_kernel,
        out_shape=(
            jax.ShapeDtypeStruct((2, ROWS * GROUP, HD), BF16),
            jax.ShapeDtypeStruct((2, ROWS * GROUP, HD), F32),
            jax.ShapeDtypeStruct((2, 2, ROWS, HD), F32),
        ),
        in_specs=[HBM] * 3,
        out_specs=(HBM,) * 3,
        scratch_shapes=[
            pltpu.VMEM((4, HD, LANES), BF16),
            pltpu.VMEM((4, HD, LANES), F32),
            pltpu.VMEM((2 * NZ, 2, 2 * ROWS, HD), BF16),
            pltpu.VMEM((2, ROWS * GROUP, HD), BF16),
            pltpu.VMEM((2, ROWS * GROUP, HD), F32),
            pltpu.VMEM((LANES, HD), F32),
            pltpu.VMEM((30, 2 * ROWS, HD), BF16),
            pltpu.VMEM((2, 2 * ROWS, HD), F32),
            pltpu.SemaphoreType.DMA((4,)),
            pltpu.SemaphoreType.DMA((4,)),
            pltpu.SemaphoreType.DMA((7,)),
            pltpu.SemaphoreType.DMA((30,)),
            pltpu.SemaphoreType.DMA((30,)),
        ],
        compiler_params=pltpu.CompilerParams(
            collective_id=1, has_side_effects=True, vmem_limit_bytes=60 << 20
        ),
        name="give_back",
    )(attn, dq, dkv)


def finish_kernel(
    attn, dq, dkv, attn_out, dq_out, dk_out, dv_out, halves, joined, wide, wide_joined, parts, dk, dv, sem
):
    loads = [
        pltpu.make_async_copy(dkv, parts, sem.at[0]),
        pltpu.make_async_copy(attn, halves, sem.at[1]),
        pltpu.make_async_copy(dq, wide, sem.at[2]),
    ]
    for load in loads:
        load.start()
    stores = []
    loads[0].wait()
    for kind, (rows, dst) in enumerate(((dk, dk_out), (dv, dv_out))):
        for half in range(2):
            rows[pl.ds(half, ROWS, stride=2), :] = parts[kind, half]
        store = pltpu.make_async_copy(rows, dst, sem.at[4 + kind])
        store.start()
        stores.append(store)
    loads[1].wait()
    both = [halves[half].astype(F32).reshape(ROWS, GROUP, HD) for half in range(2)]
    joined[...] = jnp.concatenate(both, axis=1).astype(BF16)
    store = pltpu.make_async_copy(joined, attn_out, sem.at[6])
    store.start()
    stores.append(store)
    loads[2].wait()
    wide_joined[...] = jnp.concatenate(
        [wide[half].reshape(ROWS, GROUP, HD) for half in range(2)], axis=1
    )
    store = pltpu.make_async_copy(wide_joined, dq_out, sem.at[3])
    store.start()
    stores.append(store)
    for store in stores:
        store.wait()


def finish(attn, dq, dkv):
    return pl.pallas_call(
        finish_kernel,
        out_shape=(
            jax.ShapeDtypeStruct((ROWS, 2 * GROUP, HD), BF16),
            jax.ShapeDtypeStruct((ROWS, 2 * GROUP, HD), F32),
            jax.ShapeDtypeStruct((2 * ROWS, HD), F32),
            jax.ShapeDtypeStruct((2 * ROWS, HD), F32),
        ),
        in_specs=[HBM] * 3,
        out_specs=(HBM,) * 4,
        scratch_shapes=[
            pltpu.VMEM((2, ROWS * GROUP, HD), BF16),
            pltpu.VMEM((ROWS, 2 * GROUP, HD), BF16),
            pltpu.VMEM((2, ROWS * GROUP, HD), F32),
            pltpu.VMEM((ROWS, 2 * GROUP, HD), F32),
            pltpu.VMEM((2, 2, ROWS, HD), F32),
            pltpu.VMEM((2 * ROWS, HD), F32),
            pltpu.VMEM((2 * ROWS, HD), F32),
            pltpu.SemaphoreType.DMA((7,)),
        ],
        compiler_params=pltpu.CompilerParams(vmem_limit_bytes=60 << 20),
        cost_estimate=pl.CostEstimate(flops=0, bytes_accessed=4 << 20, transcendentals=0),
        name="finish",
    )(attn, dq, dkv)


def local(queries, keys, values, grad_out, span_order, doc_ids):
    turned = [jnp.transpose(a, (1, 2, 0)) for a in (queries, keys, values, grad_out)]
    q_cols, g_cols, q_rows, g_rows, kv = bring(*turned)
    kv = kv.reshape(2 * NZ, 2, 4, SPAN, HD)
    attn, dq, dkv = attend(
        span_order, doc_ids.reshape(SLOTS, ROWS), q_cols, g_cols, q_rows, g_rows, kv
    )
    attn, dq, dkv = give_back(attn, dq, dkv.reshape(2 * NZ, 2, 2 * ROWS, HD))
    attn, dq, dk, dv = finish(attn, dq, dkv)
    return (attn, dq, dk.reshape(ROWS, 2, HD), dv.reshape(ROWS, 2, HD))


def solution(mesh):
    entry = P(("outer", "inner"), None, "head")
    leave = P(("outer", "inner"), "head", None)
    return jax.shard_map(
        local,
        mesh=mesh,
        in_specs=(entry, entry, entry, entry, P(), P()),
        out_specs=(leave, leave, leave, leave),
        check_vma=False,
    )
```

```python
import functools
import math

import jax
import jax.numpy as jnp
from jax import lax
from jax.experimental import pallas as pl
from jax.experimental.pallas import tpu as pltpu
from jax.sharding import PartitionSpec as P

MESH = pl.DeviceIdType.MESH
HBM = pl.BlockSpec(memory_space=pltpu.HBM)
NEG = -1e30
FAR = 1 << 24
NX = 4
NY = 4
NZ = 8
HD = 128
ROWS = 128
SPAN = 64
GROUP = 8
SLOTS = 64
LANES = GROUP * SPAN
SCALE = 1.0 / math.sqrt(HD)
LOG2E = math.log2(math.e)
ITEM = 4
BF16 = jnp.bfloat16
F32 = jnp.float32


def place():
    inner = lax.axis_index("inner")
    return (
        lax.axis_index("head"),
        lax.axis_index("outer"),
        lax.div(inner, 2),
        lax.rem(inner, 2),
    )


def where_is(x, y, z, core):
    return {"head": x, "outer": y, "inner": z * 2 + core}


def greet(partners):
    barrier = pltpu.get_barrier_semaphore()
    for partner in partners:
        pl.semaphore_signal(barrier, inc=1, device_id=partner, device_id_type=MESH)
    pl.semaphore_wait(barrier, len(partners))


def send(src, dst, send_sem, recv_sem, partner):
    copy = pltpu.make_async_remote_copy(
        src_ref=src,
        dst_ref=dst,
        send_sem=send_sem,
        recv_sem=recv_sem,
        device_id=partner,
        device_id_type=MESH,
    )
    copy.start()
    return copy


def bring_kernel(
    q, k, v, g, q_cols_out, g_cols_out, q_rows_out, g_rows_out, kv_out,
    q_cols, g_cols, q_rows, g_rows, out_sem, q_in, g_in, kv_in, ring_kv, relay, relay_sem, own_sem, keep_sem, x_send, x_recv, y_send, y_recv, z_send, z_recv,
):
    x, y, z, core = place()
    peers = [(dx, dc) for dx in range(NX) for dc in range(2) if (dx, dc) != (0, 0)]

    def peer(dx, dc):
        return where_is(lax.rem(x + dx, NX), y, z, lax.rem(core + dc, 2))

    up = where_is(x, y, lax.rem(z + 1, NZ), core)
    down = where_is(x, y, lax.rem(z + NZ - 1, NZ), core)
    later = where_is(x, lax.rem(y + 1, NY), z, core)
    earlier = where_is(x, lax.rem(y + NY - 1, NY), z, core)
    greet([peer(*p) for p in peers] + [up, down, later, earlier])

    here = pl.ds(pl.multiple_of(x * 32, 32), 32)
    copies = []
    own = []
    for index, (dx, dc) in enumerate([(0, 0)] + peers):
        head = lax.rem(x + dx, NX) * 2 + lax.rem(core + dc, 2)
        for kind, src in enumerate((k, v)):
            dst = kv_in.at[kind, core, here]
            if index == 0:
                copy = pltpu.make_async_copy(src.at[head], dst, own_sem.at[kind])
                copy.start()
                own.append(copy)
            else:
                copies.append(
                    send(src.at[head], dst, x_send.at[kind, index], x_recv.at[kind, index], peer(dx, dc))
                )
    own[0].wait()
    own[1].wait()
    for copy in copies:
        copy.wait()
    for kind in range(2):
        for block in range(2):
            ring_kv[z, kind, block * ROWS : (block + 1) * ROWS, :] = (
                kv_in[kind, block].astype(F32).T.astype(BF16)
            )
    keeps = []
    sent = []
    ways = (up, down)

    def block_at(group, way, step):
        return group * NZ + lax.rem(z + NZ + step * (1 if way else -1), NZ)

    def keep(block, index):
        copy = pltpu.make_async_copy(ring_kv.at[block], kv_out.at[block], keep_sem.at[index])
        copy.start()
        keeps.append(copy)

    def hop(group, way, step, kind):
        block = block_at(group, way, step - 1)
        copy = send(
            ring_kv.at[block, kind], ring_kv.at[block, kind],
            z_send.at[group, way, step - 1, kind], z_recv.at[group, way, step - 1, kind],
            ways[way],
        )
        sent.append(copy)
        return copy

    def shift(way, step, kind):
        block = block_at(0, way, step)
        copy = send(
            ring_kv.at[block, kind], ring_kv.at[NZ + block, kind],
            y_send.at[way, step, kind], y_recv.at[way, step, kind], later,
        )
        sent.append(copy)
        return copy

    def settle(kind):
        src, cols, rows = ((q_in, q_cols, q_rows), (g_in, g_cols, g_rows))[kind]
        own[2 + kind].wait()
        for copy in wide[kind]:
            copy.wait()
        low = lax.broadcasted_iota(jnp.int32, (HD, ROWS), 1) < SPAN

        @pl.loop(0, 8)
        def _(index):
            block = lax.div(index, 4)
            pair = lax.rem(index, 4)
            lanes = pl.ds(pl.multiple_of(pair * ROWS, ROWS), ROWS)
            first = src[block, 2 * pair].astype(F32)
            second = src[block, 2 * pair + 1].astype(F32)
            halves = (
                jnp.where(low, first, pltpu.roll(second, SPAN, 1)),
                jnp.where(low, pltpu.roll(first, SPAN, 1), second),
            )
            for half in range(2):
                cols[2 * block + half, :, lanes] = halves[half].astype(BF16)
                rows[2 * block + half, lanes, :] = halves[half].T.astype(BF16)

        outs = ((q_cols_out, q_rows_out), (g_cols_out, g_rows_out))[kind]
        for index, (src, dst) in enumerate(zip((cols, rows), outs)):
            copy = pltpu.make_async_copy(src, dst, out_sem.at[kind, index])
            copy.start()
            own.append(copy)

    near = {}
    self_shift = {}
    for kind in range(2):
        for way in range(2):
            near[way, 1, kind] = hop(0, way, 1, kind)
        self_shift[kind] = shift(0, 0, kind)
    keep(z, 0)
    heads = pl.ds((x * 2 + core) * GROUP, GROUP)
    for kind, (src, dst) in enumerate(((q, q_in), (g, g_in))):
        copy = pltpu.make_async_copy(
            src.at[heads], dst.at[core, :, here], own_sem.at[2 + kind]
        )
        copy.start()
        own.append(copy)
    wide = ([], [])
    relays = []
    for kind, src in enumerate((q, g)):
        relays.append(
            send(
                src.at[pl.ds(lax.rem(x + 2, NX) * 2 * GROUP, 2 * GROUP)], relay.at[kind],
                relay_sem.at[0, kind], relay_sem.at[1, kind], peer(3 if kind else 1, 0),
            )
        )
    for kind, (src, dst) in enumerate(((q, q_in), (g, g_in))):
        for index, (dx, dc) in enumerate(peers):
            if dx == 2:
                continue
            head = lax.rem(x + dx, NX) * 2 + lax.rem(core + dc, 2)
            wide[kind].append(
                send(
                    src.at[pl.ds(head * GROUP, GROUP)],
                    dst.at[core, :, here],
                    x_send.at[2 + kind, index],
                    x_recv.at[2 + kind, index],
                    peer(dx, dc),
                )
            )
    def forward(kind):
        relays[kind].wait_recv()
        from_x = lax.rem(x + (1 if kind else 3), NX)
        there = pl.ds(pl.multiple_of(from_x * 32, 32), 32)
        for index, (dx, dc) in enumerate(peers):
            if dx != 2:
                continue
            head = pl.ds(lax.rem(core + dc, 2) * GROUP, GROUP)
            wide[kind].append(
                send(
                    relay.at[kind, head],
                    (q_in, g_in)[kind].at[core, :, there],
                    x_send.at[2 + kind, index],
                    x_recv.at[2 + kind, index],
                    peer(3 if kind else 1, dc),
                )
            )

    far_shift = {}
    for step in range(1, 4):
        for kind in range(2):
            for way in range(2):
                near[way, step, kind].wait_recv()
                if step < 3 or kind == way:
                    near[way, step + 1, kind] = hop(0, way, step + 1, kind)
                if step == 2 or (step == 1 and kind == way):
                    far_shift[way, step, kind] = shift(way, step, kind)
        for way in range(2):
            keep(block_at(0, way, step), 1 + 2 * step + way)
        if step == 1:
            forward(0)
            forward(1)
    hops = {}
    for kind in range(2):
        self_shift[kind].wait_recv()
        hops[1 - kind, 1, kind] = hop(1, 1 - kind, 1, kind)
    keep(NZ + z, 1)
    last_shift = []
    for way in range(2):
        near[way, 4, way].wait_recv()
        last_shift.append(shift(way, 4, way))
    keep(block_at(0, 0, 4), 2)
    for kind in range(2):
        for way in range(2):
            far_shift[way, 2, kind].wait_recv()
            hops[way, 3, kind] = hop(1, way, 3, kind)
    for way in range(2):
        keep(block_at(1, way, 2), 9 + way)
    settle(0)
    for step in (1, 3):
        for way in range(2):
            for kind in range(2):
                arriving = far_shift if step == 1 and kind == way else hops
                arriving[way, step, kind].wait_recv()
            keep(block_at(1, way, step), 10 + step + way)
        if step == 1:
            for way in range(2):
                last_shift[way].wait_recv()
            keep(block_at(1, 0, 4), 15)
            settle(1)
    for copy in sent + relays:
        copy.wait_send()
    for copy in keeps:
        copy.wait()
    for copy in own[4:]:
        copy.wait()


def bring(q, k, v, g):
    return pl.pallas_call(
        bring_kernel,
        out_shape=(
            jax.ShapeDtypeStruct((4, HD, LANES), BF16),
            jax.ShapeDtypeStruct((4, HD, LANES), BF16),
            jax.ShapeDtypeStruct((4, LANES, HD), BF16),
            jax.ShapeDtypeStruct((4, LANES, HD), BF16),
            jax.ShapeDtypeStruct((2 * NZ, 2, 2 * ROWS, HD), BF16),
        ),
        in_specs=[HBM] * 4,
        out_specs=(HBM,) * 5,
        scratch_shapes=[
            pltpu.VMEM((4, HD, LANES), BF16),
            pltpu.VMEM((4, HD, LANES), BF16),
            pltpu.VMEM((4, LANES, HD), BF16),
            pltpu.VMEM((4, LANES, HD), BF16),
            pltpu.SemaphoreType.DMA((2, 2)),
            pltpu.VMEM((2, GROUP, HD, ROWS), BF16),
            pltpu.VMEM((2, GROUP, HD, ROWS), BF16),
            pltpu.VMEM((2, 2, HD, ROWS), BF16),
            pltpu.VMEM((2 * NZ, 2, 2 * ROWS, HD), BF16),
            pltpu.VMEM((2, 2 * GROUP, HD // NX, ROWS), BF16),
            pltpu.SemaphoreType.DMA((2, 2)),
            pltpu.SemaphoreType.DMA((4,)),
            pltpu.SemaphoreType.DMA((16,)),
            pltpu.SemaphoreType.DMA((4, 8)),
            pltpu.SemaphoreType.DMA((4, 8)),
            pltpu.SemaphoreType.DMA((2, 5, 2)),
            pltpu.SemaphoreType.DMA((2, 5, 2)),
            pltpu.SemaphoreType.DMA((2, 2, 4, 2)),
            pltpu.SemaphoreType.DMA((2, 2, 4, 2)),
        ],
        compiler_params=pltpu.CompilerParams(
            collective_id=0, has_side_effects=True, vmem_limit_bytes=60 << 20
        ),
        name="bring",
    )(q, k, v, g)


def attend_kernel(
    order_in, docs_in, q_cols_in, g_cols_in, q_rows_in, g_rows_in, kv_in, attn_out, dq_out, dkv,
    order, docs, q_cols, g_cols, q_rows, g_rows, attn, dq, kv, scores, key_acc, value_acc, out_acc, tops, sums, shift, dots, grads,
    pos_rows, start_rows, item_list, span_list, in_sem, out_sem,
):
    outer = lax.axis_index("outer")
    chip = lax.div(lax.axis_index("inner"), 2)
    loads = [
        pltpu.make_async_copy(order_in, order, in_sem.at[0]),
        pltpu.make_async_copy(docs_in, docs, in_sem.at[1]),
        pltpu.make_async_copy(q_cols_in, q_cols, in_sem.at[2]),
        pltpu.make_async_copy(kv_in.at[:, 0], kv.at[:, 0], in_sem.at[3]),
        pltpu.make_async_copy(kv_in.at[:, 1], kv.at[:, 1], in_sem.at[4]),
        pltpu.make_async_copy(g_cols_in, g_cols, in_sem.at[5]),
        pltpu.make_async_copy(q_rows_in, q_rows, in_sem.at[6]),
        pltpu.make_async_copy(g_rows_in, g_rows, in_sem.at[7]),
    ]
    for load in loads:
        load.start()
    tops[...] = jnp.full_like(tops, NEG)
    sums[...] = jnp.zeros_like(sums)
    loads[0].wait()
    loads[1].wait()
    doc = docs[...]
    starts = [
        jnp.sum(jnp.where(doc < d, 1.0, 0.0)).astype(jnp.int32) for d in range(1, 4)
    ]

    def start_of(position):
        found = jnp.zeros_like(position)
        for start in starts:
            found = jnp.where(position >= start, jnp.maximum(found, start), found)
        return found

    iota_lanes = lax.rem(lax.broadcasted_iota(jnp.int32, (8, ROWS), 1), SPAN)
    lows = []
    highs = []
    for unit in range(4):
        query_span = order[outer * 32 + chip * 4 + unit]
        lows.append(lax.div(start_of(query_span * SPAN), SPAN))
        highs.append(query_span)
        query_pos = query_span * SPAN + iota_lanes
        pos_rows[unit] = query_pos
        start_rows[unit] = start_of(query_pos)

    counts = tuple(jnp.int32(unit * 128) for unit in range(4))
    for group in range(2):
        stored = lax.rem(outer + 4 - group, 4) * 32

        def note(step, counts):
            for part in range(8):
                slot = step * 8 + part
                span = order[stored + slot]
                entry = span * SPAN + (group * 32 + slot)
                new = []
                for unit in range(4):
                    span_list[counts[unit]] = entry
                    allowed = (span >= lows[unit]) & (span <= highs[unit])
                    new.append(counts[unit] + jnp.where(allowed, 1, 0))
                counts = tuple(new)
            nothing = jnp.zeros((8, SPAN, HD), F32)
            rows = pl.ds(pl.multiple_of((group * 4 + step) * 8, 8), 8)
            key_acc[rows] = nothing
            value_acc[rows] = nothing
            flat = pl.ds(pl.multiple_of(step * 32, 32), 32)
            for unit in range(2 * group, 2 * group + 2):
                out_acc[unit, flat, :] = jnp.zeros((32, LANES), F32)
                dq[unit, flat, :] = jnp.zeros((32, LANES), F32)
            return counts

        counts = lax.fori_loop(0, 4, note, counts)
    items = jnp.int32(0)
    for unit in range(4):
        for extra in range(ITEM):
            span_list[counts[unit] + extra] = FAR
        for chunk in range(SLOTS // ITEM):
            item_list[items + chunk] = unit * 128 + chunk * ITEM
        items = items + lax.div(counts[unit] - unit * 128 + ITEM - 1, ITEM)
    blank = 3 * 128 + 72
    for extra in range(ITEM):
        span_list[blank + extra] = FAR
    for extra in range(4):
        item_list[items + extra] = blank
    steps = lax.div(items + 1, 2)
    long_steps = lax.div(items + 3, 4)

    iota_keys = (
        lax.broadcasted_iota(jnp.int32, (8, 8, ROWS), 0) * 8
        + lax.broadcasted_iota(jnp.int32, (8, 8, ROWS), 1)
    )

    def entries(item):
        first = item_list[item]
        found = [span_list[first + part] for part in range(ITEM)]
        slots = [lax.rem(entry, SLOTS) for entry in found]
        return lax.div(first, 128), slots, [a - b for a, b in zip(found, slots)]

    def spans(slots, kind):
        parts = []
        for slot in slots:
            parts.append(kv[lax.div(slot, 4), kind, lax.rem(slot, 4)])
        return jnp.concatenate(parts, axis=0)

    sides = [pl.ds(side * 256, 256) for side in range(2)]
    loads[2].wait()
    loads[3].wait()

    @functools.partial(lax.fori_loop, 0, long_steps, init_val=0)
    def _(step, _):
        results = []
        for item in [4 * step + part for part in range(4)]:
            unit, slots, bases = entries(item)
            keys = spans(slots, 0)
            biases = []
            for base in bases:
                allowed = (iota_keys <= (pos_rows[unit] - base)[None]) & (
                    iota_keys >= (start_rows[unit] - base)[None]
                )
                biases.append(jnp.where(allowed, 0.0, NEG).reshape(SPAN, ROWS))
            bias = jnp.concatenate(biases, axis=0)
            bias = jnp.concatenate([bias, bias], axis=1)
            for lanes in sides:
                tile = jnp.dot(keys, q_cols[unit, :, lanes], preferred_element_type=F32)
                tile = tile * (SCALE * LOG2E) + bias
                scores[item, :, lanes] = tile
                results.append((unit, lanes, jnp.max(tile.reshape(32, 8, 256), axis=0)))
        for unit, lanes, top in results:
            tops[unit, :, lanes] = jnp.maximum(tops[unit, :, lanes], top)
        return 0

    for unit in range(4):
        shift[unit] = jnp.broadcast_to(jnp.max(tops[unit], axis=0, keepdims=True), (8, LANES))
    loads[4].wait()

    @functools.partial(lax.fori_loop, 0, long_steps, init_val=0)
    def _(step, _):
        results = []
        for item in [4 * step + part for part in range(4)]:
            unit, slots, _ = entries(item)
            values_t = spans(slots, 1).T
            for lanes in sides:
                logits = scores[item, :, lanes].reshape(32, 8, 256)
                probs = jnp.exp2(logits - shift[unit, :, lanes][None])
                part = jnp.dot(
                    values_t, probs.reshape(256, 256).astype(BF16), preferred_element_type=F32
                )
                results.append((unit, lanes, jnp.sum(probs, axis=0), part))
        for unit, lanes, total, part in results:
            sums[unit, :, lanes] += total
            out_acc[unit, :, lanes] += part
        return 0

    for load in loads[5:]:
        load.wait()
    for unit in range(4):
        row_sum = jnp.sum(sums[unit], axis=0, keepdims=True)
        out = (out_acc[unit] * (1.0 / row_sum)).astype(BF16)
        attn[unit] = out
        row_dot = jnp.sum(
            out.astype(F32) * g_cols[unit].astype(F32), axis=0, keepdims=True
        )
        dots[unit] = jnp.broadcast_to(row_dot, (8, LANES))
        shift[unit] = shift[unit] + jnp.log(row_sum) * LOG2E
    attn_store = pltpu.make_async_copy(attn, attn_out, out_sem.at[2 * NZ])
    attn_store.start()

    def ahead(step):
        half = lax.rem(step, 2)
        for part in range(2):
            unit, slots, _ = entries(2 * step + part)
            values = spans(slots, 1)
            for lanes in sides:
                grads[half, part, :, lanes] = jnp.dot(
                    values, g_cols[unit, :, lanes], preferred_element_type=F32
                )

    ahead(0)

    @functools.partial(lax.fori_loop, 0, steps, init_val=0)
    def _(step, _):
        results = []
        mine = []
        for part in range(2):
            item = 2 * step + part
            unit, slots, _ = entries(item)
            probs_b = []
            score_grads = []
            for lanes in sides:
                logits = scores[item, :, lanes].reshape(32, 8, 256)
                probs = jnp.exp2(logits - shift[unit, :, lanes][None])
                steep = grads[lax.rem(step, 2), part, :, lanes].reshape(32, 8, 256)
                steep = probs * (steep - dots[unit, :, lanes][None])
                probs_b.append(probs.reshape(256, 256).astype(BF16))
                score_grads.append(steep.reshape(256, 256).astype(BF16))
            mine.append((unit, slots, probs_b, score_grads))
        ahead(step + 1)
        for unit, slots, probs_b, score_grads in mine:
            keys_t = spans(slots, 0).T
            probs_b = jnp.concatenate(probs_b, axis=1)
            score_grads = jnp.concatenate(score_grads, axis=1)
            to_values = jnp.dot(probs_b, g_rows[unit], preferred_element_type=F32)
            to_keys = jnp.dot(score_grads, q_rows[unit], preferred_element_type=F32)
            to_query = jnp.dot(keys_t, score_grads, preferred_element_type=F32)
            results.append((slots, unit, to_values, to_keys, to_query))
        for slots, unit, to_values, to_keys, to_query in results:
            dq[unit] += to_query
            for part, slot in enumerate(slots):
                rows = slice(part * SPAN, (part + 1) * SPAN)
                key_acc[slot] += to_keys[rows]
                value_acc[slot] += to_values[rows]
        return 0

    dq_store = pltpu.make_async_copy(dq, dq_out, out_sem.at[2 * NZ + 1])
    dq_store.start()
    stores = [attn_store, dq_store]
    for index in range(2 * NZ):
        for part in range(4):
            kv[index, 0, part] = (key_acc[index * 4 + part] * SCALE).astype(BF16)
            kv[index, 1, part] = value_acc[index * 4 + part].astype(BF16)
        store = pltpu.make_async_copy(kv.at[index], dkv.at[index], out_sem.at[index])
        store.start()
        stores.append(store)
    for store in stores:
        store.wait()


def attend(order, docs, q_cols, g_cols, q_rows, g_rows, kv):
    return pl.pallas_call(
        attend_kernel,
        out_shape=(
            jax.ShapeDtypeStruct((4, HD, LANES), BF16),
            jax.ShapeDtypeStruct((4, HD, LANES), F32),
            jax.ShapeDtypeStruct((2 * NZ, 2, 4, SPAN, HD), BF16),
        ),
        in_specs=[HBM] * 7,
        out_specs=(HBM,) * 3,
        scratch_shapes=[
            pltpu.SMEM((2 * SLOTS,), jnp.int32),
            pltpu.VMEM((SLOTS, ROWS), jnp.int32),
            pltpu.VMEM((4, HD, LANES), BF16),
            pltpu.VMEM((4, HD, LANES), BF16),
            pltpu.VMEM((4, LANES, HD), BF16),
            pltpu.VMEM((4, LANES, HD), BF16),
            pltpu.VMEM((4, HD, LANES), BF16),
            pltpu.VMEM((4, HD, LANES), F32),
            pltpu.VMEM((2 * NZ, 2, 4, SPAN, HD), BF16),
            pltpu.VMEM((4 * SLOTS // ITEM, ITEM * SPAN, LANES), F32),
            pltpu.VMEM((SLOTS, SPAN, HD), F32),
            pltpu.VMEM((SLOTS, SPAN, HD), F32),
            pltpu.VMEM((4, HD, LANES), F32),
            pltpu.VMEM((4, 8, LANES), F32),
            pltpu.VMEM((4, 8, LANES), F32),
            pltpu.VMEM((4, 8, LANES), F32),
            pltpu.VMEM((4, 8, LANES), F32),
            pltpu.VMEM((2, 2, ITEM * SPAN, LANES), F32),
            pltpu.VMEM((4, 8, ROWS), jnp.int32),
            pltpu.VMEM((4, 8, ROWS), jnp.int32),
            pltpu.SMEM((80,), jnp.int32),
            pltpu.SMEM((512,), jnp.int32),
            pltpu.SemaphoreType.DMA((8,)),
            pltpu.SemaphoreType.DMA((2 * NZ + 2,)),
        ],
        compiler_params=pltpu.CompilerParams(vmem_limit_bytes=60 << 20),
        cost_estimate=pl.CostEstimate(
            flops=6 * 2 * 2048 * 2048 * HD, bytes_accessed=12 << 20, transcendentals=2048 * 2048
        ),
        name="attend",
    )(order, docs, q_cols, g_cols, q_rows, g_rows, kv)


def return_kernel(
    attn_in, dq_in, dkv, attn_out, dq_out, dkv_out,
    attn, dq, terms, attn_rows, dq_rows, rows_tmp, landed, final, pair_send, pair_recv, own_sem, l_send, l_recv,
):
    x, y, z, core = place()
    sibling = where_is(x, y, z, 1 - core)
    up = where_is(x, y, lax.rem(z + 1, NZ), core)
    down = where_is(x, y, lax.rem(z + NZ - 1, NZ), core)
    later = where_is(x, lax.rem(y + 1, NY), z, core)
    earlier = where_is(x, lax.rem(y + NY - 1, NY), z, core)
    loads = [
        pltpu.make_async_copy(attn_in, attn, own_sem.at[5]),
        pltpu.make_async_copy(dq_in, dq, own_sem.at[6]),
        pltpu.make_async_copy(dkv, terms, own_sem.at[4]),
    ]
    for load in loads:
        load.start()
    greet([sibling, up, down, later, earlier])

    ways = (up, down)
    sent = []

    def at(group, distance, way):
        return group * NZ + lax.rem(z + NZ + distance * (-1 if way else 1), NZ)

    def ship(src, index, partner):
        copy = send(src, landed.at[index], l_send.at[index], l_recv.at[index], partner)
        sent.append(copy)
        return copy

    def add(block, kind, *indices):
        total = terms[block, kind].astype(F32)
        for index in indices:
            total = total + landed[index].astype(F32)
        terms[block, kind] = total.astype(BF16)

    flying = {}
    for step, distance in ((0, 3), (1, 1)):
        for kind in range(2):
            for way in range(2):
                if step == 1 and kind == way:
                    continue
                flying["z", step, way, kind] = ship(
                    dkv.at[at(1, distance, way), kind], step * 4 + way * 2 + kind, ways[way]
                )
        if step == 0:
            for kind in range(2):
                flying["y", 4, kind] = ship(dkv.at[at(1, 4, 0), kind], 8 + kind, earlier)
    swaps = []
    own = []

    def turn(block):
        for half in range(2):
            unit = 2 * block + half
            rows = pl.ds(half * LANES, LANES)
            for source, scale, target in ((attn, None, rows_tmp), (dq, SCALE, dq_rows.at[block, rows])):
                for pair in range(4):
                    tile = source[unit, :, pair * ROWS : (pair + 1) * ROWS].astype(F32)
                    tile = tile.T if scale is None else (tile * scale).T
                    for part in range(2):
                        target[pl.ds(2 * pair + part, SPAN, stride=GROUP), :] = tile[
                            part * SPAN : (part + 1) * SPAN
                        ]
                if scale is None:
                    attn_rows[block, rows, :] = rows_tmp[...].astype(BF16)

    def swap():
        turn(1 - core)
        for kind, (src, dst) in enumerate(((attn_rows, attn_out), (dq_rows, dq_out))):
            swaps.append(
                send(src.at[1 - core], dst.at[core], pair_send.at[kind], pair_recv.at[kind], sibling)
            )

    def stay():
        turn(core)
        for kind, (src, dst) in enumerate(((attn_rows, attn_out), (dq_rows, dq_out))):
            copy = pltpu.make_async_copy(src.at[core], dst.at[core], own_sem.at[kind])
            copy.start()
            own.append(copy)

    loads[2].wait()
    for kind in range(2):
        for way in range(2):
            flying["z", 0, way, kind].wait_recv()
            block = at(1, 2, way)
            add(block, kind, way * 2 + kind)
            flying["y", 2, way, kind] = ship(
                terms.at[block, kind], 10 + way * 2 + kind, earlier
            )
    for way in range(2):
        flying["y", 1, way] = ship(dkv.at[at(1, 1, way), way], 30 + way, earlier)
    for way in range(2):
        flying["y", 4, way].wait_recv()
        block = at(0, 4, 0)
        add(block, way, 8 + way)
        flying["s", 1, way, way] = ship(terms.at[block, way], 16 + way, ways[way])
    for way in range(2):
        kind = 1 - way
        flying["s", 2, way, kind] = ship(
            terms.at[at(0, 3, way), kind], 18 + way * 2 + kind, ways[way]
        )
    loads[0].wait()
    loads[1].wait()
    swap()
    for way in range(2):
        flying["s", 1, way, way].wait_recv()
        add(at(0, 3, way), way, 16 + way)
        flying["s", 2, way, way] = ship(
            terms.at[at(0, 3, way), way], 18 + way * 2 + way, ways[way]
        )
    for kind in range(2):
        way = 1 - kind
        flying["z", 1, way, kind].wait_recv()
        add(NZ + z, kind, 4 + way * 2 + kind)
        flying["y", 0, kind] = ship(terms.at[NZ + z, kind], 14 + kind, earlier)
    for step in (3, 4):
        for turn_of in range(2):
            for way in range(2):
                kind = turn_of if way else 1 - turn_of
                flying["s", step - 1, way, kind].wait_recv()
                indices = [18 + (step - 3) * 4 + way * 2 + kind]
                if step == 3:
                    flying["y", 2, way, kind].wait_recv()
                    indices.append(10 + way * 2 + kind)
                elif kind == way:
                    flying["y", 1, way].wait_recv()
                    indices.append(30 + way)
                block = at(0, 5 - step, way)
                add(block, kind, *indices)
                flying["s", step, way, kind] = ship(
                    terms.at[block, kind], 18 + (step - 2) * 4 + way * 2 + kind, ways[way]
                )
        if step == 3:
            stay()
    for kind in range(2):
        flying["y", 0, kind].wait_recv()
        for way in range(2):
            flying["s", 4, way, kind].wait_recv()
        total = terms[z, kind].astype(F32)
        for index in (14 + kind, 26 + kind, 28 + kind):
            total = total + landed[index].astype(F32)
        final[kind] = total
    mine = pl.ds(pl.multiple_of(core * ROWS, ROWS), ROWS)
    other = pl.ds(pl.multiple_of((1 - core) * ROWS, ROWS), ROWS)
    for kind in range(2):
        swaps.append(
            send(
                final.at[kind, other], dkv_out.at[kind, core],
                pair_send.at[2 + kind], pair_recv.at[2 + kind], sibling,
            )
        )
        copy = pltpu.make_async_copy(
            final.at[kind, mine], dkv_out.at[kind, core], own_sem.at[2 + kind]
        )
        copy.start()
        own.append(copy)
    for copy in sent:
        copy.wait_send()
    for copy in swaps:
        copy.wait()
    for copy in own:
        copy.wait()


def give_back(attn, dq, dkv):
    return pl.pallas_call(
        return_kernel,
        out_shape=(
            jax.ShapeDtypeStruct((2, ROWS * GROUP, HD), BF16),
            jax.ShapeDtypeStruct((2, ROWS * GROUP, HD), F32),
            jax.ShapeDtypeStruct((2, 2, ROWS, HD), F32),
        ),
        in_specs=[HBM] * 3,
        out_specs=(HBM,) * 3,
        scratch_shapes=[
            pltpu.VMEM((4, HD, LANES), BF16),
            pltpu.VMEM((4, HD, LANES), F32),
            pltpu.VMEM((2 * NZ, 2, 2 * ROWS, HD), BF16),
            pltpu.VMEM((2, ROWS * GROUP, HD), BF16),
            pltpu.VMEM((2, ROWS * GROUP, HD), F32),
            pltpu.VMEM((LANES, HD), F32),
            pltpu.VMEM((32, 2 * ROWS, HD), BF16),
            pltpu.VMEM((2, 2 * ROWS, HD), F32),
            pltpu.SemaphoreType.DMA((4,)),
            pltpu.SemaphoreType.DMA((4,)),
            pltpu.SemaphoreType.DMA((7,)),
            pltpu.SemaphoreType.DMA((32,)),
            pltpu.SemaphoreType.DMA((32,)),
        ],
        compiler_params=pltpu.CompilerParams(
            collective_id=1, has_side_effects=True, vmem_limit_bytes=60 << 20
        ),
        name="give_back",
    )(attn, dq, dkv)


def finish_kernel(
    attn, dq, dkv, attn_out, dq_out, dk_out, dv_out, halves, joined, wide, wide_joined, parts, dk, dv, sem
):
    loads = [
        pltpu.make_async_copy(dkv, parts, sem.at[0]),
        pltpu.make_async_copy(attn, halves, sem.at[1]),
        pltpu.make_async_copy(dq, wide, sem.at[2]),
    ]
    for load in loads:
        load.start()
    stores = []
    loads[0].wait()
    for kind, (rows, dst) in enumerate(((dk, dk_out), (dv, dv_out))):
        for half in range(2):
            rows[pl.ds(half, ROWS, stride=2), :] = parts[kind, half]
        store = pltpu.make_async_copy(rows, dst, sem.at[4 + kind])
        store.start()
        stores.append(store)
    loads[1].wait()
    both = [halves[half].astype(F32).reshape(ROWS, GROUP, HD) for half in range(2)]
    joined[...] = jnp.concatenate(both, axis=1).astype(BF16)
    store = pltpu.make_async_copy(joined, attn_out, sem.at[6])
    store.start()
    stores.append(store)
    loads[2].wait()
    wide_joined[...] = jnp.concatenate(
        [wide[half].reshape(ROWS, GROUP, HD) for half in range(2)], axis=1
    )
    store = pltpu.make_async_copy(wide_joined, dq_out, sem.at[3])
    store.start()
    stores.append(store)
    for store in stores:
        store.wait()


def finish(attn, dq, dkv):
    return pl.pallas_call(
        finish_kernel,
        out_shape=(
            jax.ShapeDtypeStruct((ROWS, 2 * GROUP, HD), BF16),
            jax.ShapeDtypeStruct((ROWS, 2 * GROUP, HD), F32),
            jax.ShapeDtypeStruct((2 * ROWS, HD), F32),
            jax.ShapeDtypeStruct((2 * ROWS, HD), F32),
        ),
        in_specs=[HBM] * 3,
        out_specs=(HBM,) * 4,
        scratch_shapes=[
            pltpu.VMEM((2, ROWS * GROUP, HD), BF16),
            pltpu.VMEM((ROWS, 2 * GROUP, HD), BF16),
            pltpu.VMEM((2, ROWS * GROUP, HD), F32),
            pltpu.VMEM((ROWS, 2 * GROUP, HD), F32),
            pltpu.VMEM((2, 2, ROWS, HD), F32),
            pltpu.VMEM((2 * ROWS, HD), F32),
            pltpu.VMEM((2 * ROWS, HD), F32),
            pltpu.SemaphoreType.DMA((7,)),
        ],
        compiler_params=pltpu.CompilerParams(vmem_limit_bytes=60 << 20),
        cost_estimate=pl.CostEstimate(flops=0, bytes_accessed=4 << 20, transcendentals=0),
        name="finish",
    )(attn, dq, dkv)


def local(queries, keys, values, grad_out, span_order, doc_ids):
    turned = [jnp.transpose(a, (1, 2, 0)) for a in (queries, keys, values, grad_out)]
    q_cols, g_cols, q_rows, g_rows, kv = bring(*turned)
    kv = kv.reshape(2 * NZ, 2, 4, SPAN, HD)
    attn, dq, dkv = attend(
        span_order, doc_ids.reshape(SLOTS, ROWS), q_cols, g_cols, q_rows, g_rows, kv
    )
    attn, dq, dkv = give_back(attn, dq, dkv.reshape(2 * NZ, 2, 2 * ROWS, HD))
    attn, dq, dk, dv = finish(attn, dq, dkv)
    return (attn, dq, dk.reshape(ROWS, 2, HD), dv.reshape(ROWS, 2, HD))


def solution(mesh):
    entry = P(("outer", "inner"), None, "head")
    leave = P(("outer", "inner"), "head", None)
    return jax.shard_map(
        local,
        mesh=mesh,
        in_specs=(entry, entry, entry, entry, P(), P()),
        out_specs=(leave, leave, leave, leave),
        check_vma=False,
    )
```

```python
import functools
import math

import jax
import jax.numpy as jnp
from jax import lax
from jax.experimental import pallas as pl
from jax.experimental.pallas import tpu as pltpu
from jax.sharding import PartitionSpec as P

MESH = pl.DeviceIdType.MESH
HBM = pl.BlockSpec(memory_space=pltpu.HBM)
NEG = -1e30
FAR = 1 << 24
NX = 4
NY = 4
NZ = 8
HD = 128
ROWS = 128
SPAN = 64
GROUP = 8
SLOTS = 64
LANES = GROUP * SPAN
SCALE = 1.0 / math.sqrt(HD)
LOG2E = math.log2(math.e)
ITEM = 4
BF16 = jnp.bfloat16
F32 = jnp.float32


def place():
    inner = lax.axis_index("inner")
    return (
        lax.axis_index("head"),
        lax.axis_index("outer"),
        lax.div(inner, 2),
        lax.rem(inner, 2),
    )


def where_is(x, y, z, core):
    return {"head": x, "outer": y, "inner": z * 2 + core}


def greet(partners):
    barrier = pltpu.get_barrier_semaphore()
    for partner in partners:
        pl.semaphore_signal(barrier, inc=1, device_id=partner, device_id_type=MESH)
    pl.semaphore_wait(barrier, len(partners))


def send(src, dst, send_sem, recv_sem, partner):
    copy = pltpu.make_async_remote_copy(
        src_ref=src,
        dst_ref=dst,
        send_sem=send_sem,
        recv_sem=recv_sem,
        device_id=partner,
        device_id_type=MESH,
    )
    copy.start()
    return copy


def bring_kernel(
    q, k, v, g, q_cols_out, g_cols_out, q_rows_out, g_rows_out, kv_out,
    q_cols, g_cols, q_rows, g_rows, out_sem, q_in, g_in, kv_in, ring_kv, relay, relay_sem, own_sem, keep_sem, x_send, x_recv, y_send, y_recv, z_send, z_recv,
):
    x, y, z, core = place()
    peers = [(dx, dc) for dx in range(NX) for dc in range(2) if (dx, dc) != (0, 0)]

    def peer(dx, dc):
        return where_is(lax.rem(x + dx, NX), y, z, lax.rem(core + dc, 2))

    up = where_is(x, y, lax.rem(z + 1, NZ), core)
    down = where_is(x, y, lax.rem(z + NZ - 1, NZ), core)
    later = where_is(x, lax.rem(y + 1, NY), z, core)
    earlier = where_is(x, lax.rem(y + NY - 1, NY), z, core)
    up_z, down_z = lax.rem(z + 1, NZ), lax.rem(z + NZ - 1, NZ)
    later_y, earlier_y = lax.rem(y + 1, NY), lax.rem(y + NY - 1, NY)
    corners = (where_is(x, later_y, up_z, core), where_is(x, later_y, down_z, core))
    behind = [where_is(x, earlier_y, up_z, core), where_is(x, earlier_y, down_z, core)]
    greet([peer(*p) for p in peers] + [up, down, later, earlier, *corners, *behind])

    here = pl.ds(pl.multiple_of(x * 32, 32), 32)
    copies = []
    own = []
    for index, (dx, dc) in enumerate([(0, 0)] + peers):
        head = lax.rem(x + dx, NX) * 2 + lax.rem(core + dc, 2)
        for kind, src in enumerate((k, v)):
            dst = kv_in.at[kind, core, here]
            if index == 0:
                copy = pltpu.make_async_copy(src.at[head], dst, own_sem.at[kind])
                copy.start()
                own.append(copy)
            else:
                copies.append(
                    send(src.at[head], dst, x_send.at[kind, index], x_recv.at[kind, index], peer(dx, dc))
                )
    own[0].wait()
    own[1].wait()
    for copy in copies:
        copy.wait()
    for kind in range(2):
        for block in range(2):
            ring_kv[z, kind, block * ROWS : (block + 1) * ROWS, :] = (
                kv_in[kind, block].astype(F32).T.astype(BF16)
            )
    keeps = []
    sent = []
    ways = (up, down)

    def block_at(group, way, step):
        return group * NZ + lax.rem(z + NZ + step * (1 if way else -1), NZ)

    def keep(block, index):
        copy = pltpu.make_async_copy(ring_kv.at[block], kv_out.at[block], keep_sem.at[index])
        copy.start()
        keeps.append(copy)

    def hop(group, way, step, kind):
        block = block_at(group, way, step - 1)
        copy = send(
            ring_kv.at[block, kind], ring_kv.at[block, kind],
            z_send.at[group, way, step - 1, kind], z_recv.at[group, way, step - 1, kind],
            ways[way],
        )
        sent.append(copy)
        return copy

    def shift(way, step, kind):
        block = block_at(0, way, min(step, 3))
        copy = send(
            ring_kv.at[block, kind], ring_kv.at[NZ + block, kind],
            y_send.at[way, step, kind], y_recv.at[way, step, kind],
            corners[way] if step == 4 else later,
        )
        sent.append(copy)
        return copy

    def settle(kind):
        src, cols, rows = ((q_in, q_cols, q_rows), (g_in, g_cols, g_rows))[kind]
        own[2 + kind].wait()
        for copy in wide[kind]:
            copy.wait()
        low = lax.broadcasted_iota(jnp.int32, (HD, ROWS), 1) < SPAN

        @pl.loop(0, 8)
        def _(index):
            block = lax.div(index, 4)
            pair = lax.rem(index, 4)
            lanes = pl.ds(pl.multiple_of(pair * ROWS, ROWS), ROWS)
            first = src[block, 2 * pair].astype(F32)
            second = src[block, 2 * pair + 1].astype(F32)
            halves = (
                jnp.where(low, first, pltpu.roll(second, SPAN, 1)),
                jnp.where(low, pltpu.roll(first, SPAN, 1), second),
            )
            for half in range(2):
                cols[2 * block + half, :, lanes] = halves[half].astype(BF16)
                rows[2 * block + half, lanes, :] = halves[half].T.astype(BF16)

        outs = ((q_cols_out, q_rows_out), (g_cols_out, g_rows_out))[kind]
        for index, (src, dst) in enumerate(zip((cols, rows), outs)):
            copy = pltpu.make_async_copy(src, dst, out_sem.at[kind, index])
            copy.start()
            own.append(copy)

    near = {}
    self_shift = {}
    for kind in range(2):
        for way in range(2):
            near[way, 1, kind] = hop(0, way, 1, kind)
        self_shift[kind] = shift(0, 0, kind)
    keep(z, 0)
    heads = pl.ds((x * 2 + core) * GROUP, GROUP)
    for kind, (src, dst) in enumerate(((q, q_in), (g, g_in))):
        copy = pltpu.make_async_copy(
            src.at[heads], dst.at[core, :, here], own_sem.at[2 + kind]
        )
        copy.start()
        own.append(copy)
    wide = ([], [])
    relays = []
    for kind, src in enumerate((q, g)):
        relays.append(
            send(
                src.at[pl.ds(lax.rem(x + 2, NX) * 2 * GROUP, 2 * GROUP)], relay.at[kind],
                relay_sem.at[0, kind], relay_sem.at[1, kind], peer(3 if kind else 1, 0),
            )
        )
    for kind, (src, dst) in enumerate(((q, q_in), (g, g_in))):
        for index, (dx, dc) in enumerate(peers):
            if dx == 2:
                continue
            head = lax.rem(x + dx, NX) * 2 + lax.rem(core + dc, 2)
            wide[kind].append(
                send(
                    src.at[pl.ds(head * GROUP, GROUP)],
                    dst.at[core, :, here],
                    x_send.at[2 + kind, index],
                    x_recv.at[2 + kind, index],
                    peer(dx, dc),
                )
            )
    def forward(kind):
        relays[kind].wait_recv()
        from_x = lax.rem(x + (1 if kind else 3), NX)
        there = pl.ds(pl.multiple_of(from_x * 32, 32), 32)
        for index, (dx, dc) in enumerate(peers):
            if dx != 2:
                continue
            head = pl.ds(lax.rem(core + dc, 2) * GROUP, GROUP)
            wide[kind].append(
                send(
                    relay.at[kind, head],
                    (q_in, g_in)[kind].at[core, :, there],
                    x_send.at[2 + kind, index],
                    x_recv.at[2 + kind, index],
                    peer(3 if kind else 1, dc),
                )
            )

    far_shift = {}
    for step in range(1, 4):
        for kind in range(2):
            for way in range(2):
                near[way, step, kind].wait_recv()
                if step < 3 or kind == way:
                    near[way, step + 1, kind] = hop(0, way, step + 1, kind)
                if step == 3 and kind == way:
                    far_shift[way, 4] = shift(way, 4, way)
                if step == 2 or (step == 1 and kind == way):
                    far_shift[way, step, kind] = shift(way, step, kind)
        for way in range(2):
            keep(block_at(0, way, step), 1 + 2 * step + way)
        if step == 1:
            forward(0)
            forward(1)
    hops = {}
    for kind in range(2):
        self_shift[kind].wait_recv()
        hops[1 - kind, 1, kind] = hop(1, 1 - kind, 1, kind)
    keep(NZ + z, 1)
    for kind in range(2):
        for way in range(2):
            far_shift[way, 2, kind].wait_recv()
            hops[way, 3, kind] = hop(1, way, 3, kind)
    for way in range(2):
        keep(block_at(1, way, 2), 9 + way)
    settle(0)
    settle(1)
    for way in range(2):
        near[way, 4, way].wait_recv()
    keep(block_at(0, 0, 4), 2)
    for step in (1, 3):
        for way in range(2):
            for kind in range(2):
                arriving = far_shift if step == 1 and kind == way else hops
                arriving[way, step, kind].wait_recv()
            keep(block_at(1, way, step), 10 + step + way)
    for way in range(2):
        far_shift[way, 4].wait_recv()
    keep(block_at(1, 0, 4), 15)
    for copy in sent + relays:
        copy.wait_send()
    for copy in keeps:
        copy.wait()
    for copy in own[4:]:
        copy.wait()


def bring(q, k, v, g):
    return pl.pallas_call(
        bring_kernel,
        out_shape=(
            jax.ShapeDtypeStruct((4, HD, LANES), BF16),
            jax.ShapeDtypeStruct((4, HD, LANES), BF16),
            jax.ShapeDtypeStruct((4, LANES, HD), BF16),
            jax.ShapeDtypeStruct((4, LANES, HD), BF16),
            jax.ShapeDtypeStruct((2 * NZ, 2, 2 * ROWS, HD), BF16),
        ),
        in_specs=[HBM] * 4,
        out_specs=(HBM,) * 5,
        scratch_shapes=[
            pltpu.VMEM((4, HD, LANES), BF16),
            pltpu.VMEM((4, HD, LANES), BF16),
            pltpu.VMEM((4, LANES, HD), BF16),
            pltpu.VMEM((4, LANES, HD), BF16),
            pltpu.SemaphoreType.DMA((2, 2)),
            pltpu.VMEM((2, GROUP, HD, ROWS), BF16),
            pltpu.VMEM((2, GROUP, HD, ROWS), BF16),
            pltpu.VMEM((2, 2, HD, ROWS), BF16),
            pltpu.VMEM((2 * NZ, 2, 2 * ROWS, HD), BF16),
            pltpu.VMEM((2, 2 * GROUP, HD // NX, ROWS), BF16),
            pltpu.SemaphoreType.DMA((2, 2)),
            pltpu.SemaphoreType.DMA((4,)),
            pltpu.SemaphoreType.DMA((16,)),
            pltpu.SemaphoreType.DMA((4, 8)),
            pltpu.SemaphoreType.DMA((4, 8)),
            pltpu.SemaphoreType.DMA((2, 5, 2)),
            pltpu.SemaphoreType.DMA((2, 5, 2)),
            pltpu.SemaphoreType.DMA((2, 2, 4, 2)),
            pltpu.SemaphoreType.DMA((2, 2, 4, 2)),
        ],
        compiler_params=pltpu.CompilerParams(
            collective_id=0, has_side_effects=True, vmem_limit_bytes=60 << 20
        ),
        name="bring",
    )(q, k, v, g)


def attend_kernel(
    order_in, docs_in, q_cols_in, g_cols_in, q_rows_in, g_rows_in, kv_in, attn_out, dq_out, dkv,
    order, docs, q_cols, g_cols, q_rows, g_rows, attn, dq, kv, scores, key_acc, value_acc, out_acc, tops, sums, shift, dots,
    pos_rows, start_rows, item_list, span_list, in_sem, out_sem,
):
    outer = lax.axis_index("outer")
    chip = lax.div(lax.axis_index("inner"), 2)
    loads = [
        pltpu.make_async_copy(order_in, order, in_sem.at[0]),
        pltpu.make_async_copy(docs_in, docs, in_sem.at[1]),
        pltpu.make_async_copy(q_cols_in, q_cols, in_sem.at[2]),
        pltpu.make_async_copy(kv_in.at[:, 0], kv.at[pl.ds(0, 2 * NZ), 0], in_sem.at[3]),
        pltpu.make_async_copy(kv_in.at[:, 1], kv.at[pl.ds(0, 2 * NZ), 1], in_sem.at[4]),
        pltpu.make_async_copy(g_cols_in, g_cols, in_sem.at[5]),
        pltpu.make_async_copy(q_rows_in, q_rows, in_sem.at[6]),
        pltpu.make_async_copy(g_rows_in, g_rows, in_sem.at[7]),
    ]
    for load in loads:
        load.start()
    kv[2 * NZ] = jnp.zeros((2, 4, SPAN, HD), BF16)
    tops[...] = jnp.full_like(tops, NEG)
    sums[...] = jnp.zeros_like(sums)
    loads[0].wait()
    loads[1].wait()
    doc = docs[...]
    starts = [
        jnp.sum(jnp.where(doc < d, 1.0, 0.0)).astype(jnp.int32) for d in range(1, 4)
    ]

    def start_of(position):
        found = jnp.zeros_like(position)
        for start in starts:
            found = jnp.where(position >= start, jnp.maximum(found, start), found)
        return found

    iota_lanes = lax.rem(lax.broadcasted_iota(jnp.int32, (8, ROWS), 1), SPAN)
    lows = []
    highs = []
    for unit in range(4):
        query_span = order[outer * 32 + chip * 4 + unit]
        lows.append(lax.div(start_of(query_span * SPAN), SPAN))
        highs.append(query_span)
        query_pos = query_span * SPAN + iota_lanes
        pos_rows[unit] = query_pos
        start_rows[unit] = start_of(query_pos)

    counts = tuple(jnp.int32(unit * 128) for unit in range(4))
    for group in range(2):
        stored = lax.rem(outer + 4 - group, 4) * 32

        def note(step, counts):
            for part in range(8):
                slot = step * 8 + part
                span = order[stored + slot]
                entry = span * (2 * SPAN) + (group * 32 + slot)
                new = []
                for unit in range(4):
                    span_list[counts[unit]] = entry
                    allowed = (span >= lows[unit]) & (span <= highs[unit])
                    new.append(counts[unit] + jnp.where(allowed, 1, 0))
                counts = tuple(new)
            nothing = jnp.zeros((8, SPAN, HD), F32)
            rows = pl.ds((group * 4 + step) * 8, 8)
            key_acc[rows] = nothing
            value_acc[rows] = nothing
            flat = pl.ds(pl.multiple_of(step * 32, 32), 32)
            for unit in range(2 * group, 2 * group + 2):
                out_acc[unit, flat, :] = jnp.zeros((32, LANES), F32)
                dq[unit, flat, :] = jnp.zeros((32, LANES), F32)
            return counts

        counts = lax.fori_loop(0, 4, note, counts)
    items = jnp.int32(0)
    for unit in range(4):
        for extra in range(ITEM):
            span_list[counts[unit] + extra] = 2 * FAR + SLOTS
        for chunk in range(SLOTS // ITEM):
            item_list[items + chunk] = unit * 128 + chunk * ITEM
        items = items + lax.div(counts[unit] - unit * 128 + ITEM - 1, ITEM)
    blank = 3 * 128 + 72
    for extra in range(ITEM):
        span_list[blank + extra] = 2 * FAR + SLOTS
    for extra in range(4):
        item_list[items + extra] = blank
    steps = lax.div(items + 1, 2)
    long_steps = lax.div(items + 3, 4)

    iota_keys = (
        lax.broadcasted_iota(jnp.int32, (8, 8, ROWS), 0) * 8
        + lax.broadcasted_iota(jnp.int32, (8, 8, ROWS), 1)
    )

    def entries(item):
        first = item_list[item]
        found = [span_list[first + part] for part in range(ITEM)]
        slots = [lax.rem(entry, 2 * SPAN) for entry in found]
        return lax.div(first, 128), slots, [lax.div(a - b, 2) for a, b in zip(found, slots)]

    def spans(slots, kind):
        parts = []
        for slot in slots:
            parts.append(kv[lax.div(slot, 4), kind, lax.rem(slot, 4)])
        return jnp.concatenate(parts, axis=0)

    sides = [pl.ds(side * 256, 256) for side in range(2)]
    loads[2].wait()
    loads[3].wait()

    @functools.partial(lax.fori_loop, 0, long_steps, init_val=0)
    def _(step, _):
        results = []
        for item in [4 * step + part for part in range(4)]:
            unit, slots, bases = entries(item)
            keys = spans(slots, 0)
            biases = []
            for base in bases:
                allowed = (iota_keys <= (pos_rows[unit] - base)[None]) & (
                    iota_keys >= (start_rows[unit] - base)[None]
                )
                biases.append(jnp.where(allowed, 0.0, NEG).reshape(SPAN, ROWS))
            bias = jnp.concatenate(biases, axis=0)
            bias = jnp.concatenate([bias, bias], axis=1)
            for lanes in sides:
                tile = jnp.dot(keys, q_cols[unit, :, lanes], preferred_element_type=F32)
                tile = tile * (SCALE * LOG2E) + bias
                scores[item, :, lanes] = tile
                results.append((unit, lanes, jnp.max(tile.reshape(32, 8, 256), axis=0)))
        for unit, lanes, top in results:
            tops[unit, :, lanes] = jnp.maximum(tops[unit, :, lanes], top)
        return 0

    for unit in range(4):
        shift[unit] = jnp.broadcast_to(jnp.max(tops[unit], axis=0, keepdims=True), (8, LANES))
    loads[4].wait()

    @functools.partial(lax.fori_loop, 0, long_steps, init_val=0)
    def _(step, _):
        results = []
        for item in [4 * step + part for part in range(4)]:
            unit, slots, _ = entries(item)
            values_t = spans(slots, 1).T
            for lanes in sides:
                logits = scores[item, :, lanes].reshape(32, 8, 256)
                probs = jnp.exp2(logits - shift[unit, :, lanes][None])
                part = jnp.dot(
                    values_t, probs.reshape(256, 256).astype(BF16), preferred_element_type=F32
                )
                results.append((unit, lanes, jnp.sum(probs, axis=0), part))
        for unit, lanes, total, part in results:
            sums[unit, :, lanes] += total
            out_acc[unit, :, lanes] += part
        return 0

    for load in loads[5:]:
        load.wait()
    for unit in range(4):
        row_sum = jnp.sum(sums[unit], axis=0, keepdims=True)
        out = (out_acc[unit] * (1.0 / row_sum)).astype(BF16)
        attn[unit] = out
        row_dot = jnp.sum(
            out.astype(F32) * g_cols[unit].astype(F32), axis=0, keepdims=True
        )
        dots[unit] = jnp.broadcast_to(row_dot, (8, LANES))
        shift[unit] = shift[unit] + jnp.log(row_sum) * LOG2E
    attn_store = pltpu.make_async_copy(attn, attn_out, out_sem.at[2 * NZ])
    attn_store.start()

    @functools.partial(lax.fori_loop, 0, steps, init_val=0)
    def _(step, _):
        results = []
        for item in (2 * step, 2 * step + 1):
            unit, slots, _ = entries(item)
            keys_t = spans(slots, 0).T
            values = spans(slots, 1)
            probs_b = []
            score_grads = []
            for lanes in sides:
                logits = scores[item, :, lanes].reshape(32, 8, 256)
                probs = jnp.exp2(logits - shift[unit, :, lanes][None])
                steep = jnp.dot(values, g_cols[unit, :, lanes], preferred_element_type=F32)
                steep = probs * (steep.reshape(32, 8, 256) - dots[unit, :, lanes][None])
                probs_b.append(probs.reshape(256, 256).astype(BF16))
                score_grads.append(steep.reshape(256, 256).astype(BF16))
            probs_b = jnp.concatenate(probs_b, axis=1)
            score_grads = jnp.concatenate(score_grads, axis=1)
            to_values = jnp.dot(probs_b, g_rows[unit], preferred_element_type=F32)
            to_keys = jnp.dot(score_grads, q_rows[unit], preferred_element_type=F32)
            to_query = jnp.dot(keys_t, score_grads, preferred_element_type=F32)
            results.append((slots, unit, to_values, to_keys, to_query))
        for slots, unit, to_values, to_keys, to_query in results:
            dq[unit] += to_query
            for acc, part in ((key_acc, to_keys), (value_acc, to_values)):
                sums_of = [
                    acc[slot] + part[index * SPAN : (index + 1) * SPAN]
                    for index, slot in enumerate(slots)
                ]
                for slot, total in zip(slots, sums_of):
                    acc[slot] = total
        return 0

    dq_store = pltpu.make_async_copy(dq, dq_out, out_sem.at[2 * NZ + 1])
    dq_store.start()
    stores = [attn_store, dq_store]
    for index in range(2 * NZ):
        for part in range(4):
            kv[index, 0, part] = (key_acc[index * 4 + part] * SCALE).astype(BF16)
            kv[index, 1, part] = value_acc[index * 4 + part].astype(BF16)
        store = pltpu.make_async_copy(kv.at[index], dkv.at[index], out_sem.at[index])
        store.start()
        stores.append(store)
    for store in stores:
        store.wait()


def attend(order, docs, q_cols, g_cols, q_rows, g_rows, kv):
    return pl.pallas_call(
        attend_kernel,
        out_shape=(
            jax.ShapeDtypeStruct((4, HD, LANES), BF16),
            jax.ShapeDtypeStruct((4, HD, LANES), F32),
            jax.ShapeDtypeStruct((2 * NZ, 2, 4, SPAN, HD), BF16),
        ),
        in_specs=[HBM] * 7,
        out_specs=(HBM,) * 3,
        scratch_shapes=[
            pltpu.SMEM((2 * SLOTS,), jnp.int32),
            pltpu.VMEM((SLOTS, ROWS), jnp.int32),
            pltpu.VMEM((4, HD, LANES), BF16),
            pltpu.VMEM((4, HD, LANES), BF16),
            pltpu.VMEM((4, LANES, HD), BF16),
            pltpu.VMEM((4, LANES, HD), BF16),
            pltpu.VMEM((4, HD, LANES), BF16),
            pltpu.VMEM((4, HD, LANES), F32),
            pltpu.VMEM((2 * NZ + 1, 2, 4, SPAN, HD), BF16),
            pltpu.VMEM((4 * SLOTS // ITEM, ITEM * SPAN, LANES), F32),
            pltpu.VMEM((SLOTS + 1, SPAN, HD), F32),
            pltpu.VMEM((SLOTS + 1, SPAN, HD), F32),
            pltpu.VMEM((4, HD, LANES), F32),
            pltpu.VMEM((4, 8, LANES), F32),
            pltpu.VMEM((4, 8, LANES), F32),
            pltpu.VMEM((4, 8, LANES), F32),
            pltpu.VMEM((4, 8, LANES), F32),
            pltpu.VMEM((4, 8, ROWS), jnp.int32),
            pltpu.VMEM((4, 8, ROWS), jnp.int32),
            pltpu.SMEM((80,), jnp.int32),
            pltpu.SMEM((512,), jnp.int32),
            pltpu.SemaphoreType.DMA((8,)),
            pltpu.SemaphoreType.DMA((2 * NZ + 2,)),
        ],
        compiler_params=pltpu.CompilerParams(vmem_limit_bytes=60 << 20),
        cost_estimate=pl.CostEstimate(
            flops=6 * 2 * 2048 * 2048 * HD, bytes_accessed=12 << 20, transcendentals=2048 * 2048
        ),
        name="attend",
    )(order, docs, q_cols, g_cols, q_rows, g_rows, kv)


def return_kernel(
    attn_in, dq_in, dkv, attn_out, dq_out, dkv_out,
    attn, dq, terms, attn_rows, dq_rows, rows_tmp, landed, landed_rows, final, pair_send, pair_recv, own_sem, l_send, l_recv, r_send, r_recv,
):
    x, y, z, core = place()
    sibling = where_is(x, y, z, 1 - core)
    up = where_is(x, y, lax.rem(z + 1, NZ), core)
    down = where_is(x, y, lax.rem(z + NZ - 1, NZ), core)
    later = where_is(x, lax.rem(y + 1, NY), z, core)
    earlier = where_is(x, lax.rem(y + NY - 1, NY), z, core)
    loads = [
        pltpu.make_async_copy(attn_in, attn, own_sem.at[5]),
        pltpu.make_async_copy(dq_in, dq, own_sem.at[6]),
        pltpu.make_async_copy(dkv, terms, own_sem.at[4]),
    ]
    for load in loads:
        load.start()
    up_z, down_z = lax.rem(z + 1, NZ), lax.rem(z + NZ - 1, NZ)
    later_y, earlier_y = lax.rem(y + 1, NY), lax.rem(y + NY - 1, NY)
    corners = (where_is(x, earlier_y, up_z, core), where_is(x, earlier_y, down_z, core))
    behind = [where_is(x, later_y, up_z, core), where_is(x, later_y, down_z, core)]
    across = [
        where_is(x, y, up_z, 1 - core),
        where_is(x, y, down_z, 1 - core),
        where_is(x, earlier_y, z, 1 - core),
    ]
    greet(
        [sibling, up, down, later, earlier, *corners, *behind, *across]
        + [where_is(x, later_y, z, 1 - core)]
    )

    ways = (up, down)
    sent = []

    def at(group, distance, way):
        return group * NZ + lax.rem(z + NZ + distance * (-1 if way else 1), NZ)

    def ship(src, index, partner):
        copy = send(src, landed.at[index], l_send.at[index], l_recv.at[index], partner)
        sent.append(copy)
        return copy

    def add(block, kind, *indices):
        total = terms[block, kind].astype(F32)
        for index in indices:
            total = total + landed[index].astype(F32)
        terms[block, kind] = total.astype(BF16)

    mine = pl.ds(pl.multiple_of(core * ROWS, ROWS), ROWS)
    other = pl.ds(pl.multiple_of((1 - core) * ROWS, ROWS), ROWS)

    def deliver(block, kind, index, straight, crossed):
        copies = []
        for half, rows, partner in ((0, mine, straight), (1, other, crossed)):
            copy = send(
                terms.at[block, kind, rows], landed_rows.at[half, index],
                r_send.at[half, index], r_recv.at[half, index], partner,
            )
            sent.append(copy)
            copies.append(copy)
        return copies

    flying = {}
    for way in range(2):
        flying["s", 1, way, way] = ship(dkv.at[at(0, 4, 0), way], 16 + way, ways[way])
    for step, distance in ((0, 3), (1, 1)):
        for kind in range(2):
            for way in range(2):
                if step == 1 and kind == way:
                    continue
                flying["z", step, way, kind] = ship(
                    dkv.at[at(1, distance, way), kind], step * 4 + way * 2 + kind, ways[way]
                )
        if step == 0:
            for kind in range(2):
                flying["y", 4, kind] = ship(dkv.at[at(1, 4, 0), kind], 8 + kind, corners[kind])
    swaps = []
    own = []

    def turn(block):
        for half in range(2):
            unit = 2 * block + half
            rows = pl.ds(half * LANES, LANES)
            for source, scale, target in ((attn, None, rows_tmp), (dq, SCALE, dq_rows.at[block, rows])):
                for pair in range(4):
                    tile = source[unit, :, pair * ROWS : (pair + 1) * ROWS].astype(F32)
                    tile = tile.T if scale is None else (tile * scale).T
                    for part in range(2):
                        target[pl.ds(2 * pair + part, SPAN, stride=GROUP), :] = tile[
                            part * SPAN : (part + 1) * SPAN
                        ]
                if scale is None:
                    attn_rows[block, rows, :] = rows_tmp[...].astype(BF16)

    def swap():
        turn(1 - core)
        for kind, (src, dst) in enumerate(((attn_rows, attn_out), (dq_rows, dq_out))):
            swaps.append(
                send(src.at[1 - core], dst.at[core], pair_send.at[kind], pair_recv.at[kind], sibling)
            )

    def stay():
        turn(core)
        for kind, (src, dst) in enumerate(((attn_rows, attn_out), (dq_rows, dq_out))):
            copy = pltpu.make_async_copy(src.at[core], dst.at[core], own_sem.at[kind])
            copy.start()
            own.append(copy)

    loads[2].wait()
    for kind in range(2):
        for way in range(2):
            flying["z", 0, way, kind].wait_recv()
            block = at(1, 2, way)
            add(block, kind, way * 2 + kind)
            flying["y", 2, way, kind] = ship(
                terms.at[block, kind], 10 + way * 2 + kind, earlier
            )
    for way in range(2):
        flying["y", 1, way] = ship(dkv.at[at(1, 1, way), way], 30 + way, earlier)
    for way in range(2):
        kind = 1 - way
        flying["s", 2, way, kind] = ship(
            terms.at[at(0, 3, way), kind], 18 + way * 2 + kind, ways[way]
        )
    loads[0].wait()
    loads[1].wait()
    swap()
    for kind in range(2):
        swaps.append(
            send(
                dkv.at[z, kind, other], landed_rows.at[1, 6 + kind],
                r_send.at[1, 6 + kind], r_recv.at[1, 6 + kind], sibling,
            )
        )
    for way in range(2):
        flying["s", 1, way, way].wait_recv()
        flying["y", 4, way].wait_recv()
        add(at(0, 3, way), way, 16 + way, 8 + way)
        flying["s", 2, way, way] = ship(
            terms.at[at(0, 3, way), way], 18 + way * 2 + way, ways[way]
        )
    for kind in range(2):
        way = 1 - kind
        flying["z", 1, way, kind].wait_recv()
        add(NZ + z, kind, 4 + way * 2 + kind)
        flying["y", 0, kind] = deliver(NZ + z, kind, kind, earlier, across[2])
    for step in (3, 4):
        for turn_of in range(2):
            for way in range(2):
                kind = turn_of if way else 1 - turn_of
                flying["s", step - 1, way, kind].wait_recv()
                indices = [18 + (step - 3) * 4 + way * 2 + kind]
                if step == 3:
                    flying["y", 2, way, kind].wait_recv()
                    indices.append(10 + way * 2 + kind)
                elif kind == way:
                    flying["y", 1, way].wait_recv()
                    indices.append(30 + way)
                block = at(0, 5 - step, way)
                add(block, kind, *indices)
                if step == 3:
                    flying["s", step, way, kind] = ship(
                        terms.at[block, kind], 22 + way * 2 + kind, ways[way]
                    )
                else:
                    flying["s", step, way, kind] = deliver(
                        block, kind, 2 + way * 2 + kind, ways[way], across[way]
                    )
        if step == 3:
            stay()
    for kind in range(2):
        for half in range(2):
            flying["y", 0, kind][half].wait_recv()
            for way in range(2):
                flying["s", 4, way, kind][half].wait_recv()
            if half:
                swaps[2 + kind].wait_recv()
                total = landed_rows[1, 6 + kind].astype(F32)
            else:
                total = terms[z, kind, mine].astype(F32)
            for index in (kind, 2 + kind, 4 + kind):
                total = total + landed_rows[half, index].astype(F32)
            final[kind, half] = total
        for half in range(2):
            copy = pltpu.make_async_copy(
                final.at[kind, half], dkv_out.at[kind, core if half == 0 else 1 - core],
                own_sem.at[2 + (0, 5)[half] + kind],
            )
            copy.start()
            own.append(copy)
    for copy in sent:
        copy.wait_send()
    for copy in swaps[:2]:
        copy.wait()
    for copy in swaps[2:]:
        copy.wait_send()
    for copy in own:
        copy.wait()


def give_back(attn, dq, dkv):
    return pl.pallas_call(
        return_kernel,
        out_shape=(
            jax.ShapeDtypeStruct((2, ROWS * GROUP, HD), BF16),
            jax.ShapeDtypeStruct((2, ROWS * GROUP, HD), F32),
            jax.ShapeDtypeStruct((2, 2, ROWS, HD), F32),
        ),
        in_specs=[HBM] * 3,
        out_specs=(HBM,) * 3,
        scratch_shapes=[
            pltpu.VMEM((4, HD, LANES), BF16),
            pltpu.VMEM((4, HD, LANES), F32),
            pltpu.VMEM((2 * NZ, 2, 2 * ROWS, HD), BF16),
            pltpu.VMEM((2, ROWS * GROUP, HD), BF16),
            pltpu.VMEM((2, ROWS * GROUP, HD), F32),
            pltpu.VMEM((LANES, HD), F32),
            pltpu.VMEM((32, 2 * ROWS, HD), BF16),
            pltpu.VMEM((2, 8, ROWS, HD), BF16),
            pltpu.VMEM((2, 2, ROWS, HD), F32),
            pltpu.SemaphoreType.DMA((2,)),
            pltpu.SemaphoreType.DMA((2,)),
            pltpu.SemaphoreType.DMA((9,)),
            pltpu.SemaphoreType.DMA((32,)),
            pltpu.SemaphoreType.DMA((32,)),
            pltpu.SemaphoreType.DMA((2, 8)),
            pltpu.SemaphoreType.DMA((2, 8)),
        ],
        compiler_params=pltpu.CompilerParams(
            collective_id=1, has_side_effects=True, vmem_limit_bytes=60 << 20
        ),
        name="give_back",
    )(attn, dq, dkv)


def finish_kernel(
    attn, dq, dkv, attn_out, dq_out, dk_out, dv_out, halves, joined, wide, wide_joined, parts, dk, dv, sem
):
    loads = [
        pltpu.make_async_copy(dkv, parts, sem.at[0]),
        pltpu.make_async_copy(attn, halves, sem.at[1]),
        pltpu.make_async_copy(dq, wide, sem.at[2]),
    ]
    for load in loads:
        load.start()
    stores = []
    loads[0].wait()
    for kind, (rows, dst) in enumerate(((dk, dk_out), (dv, dv_out))):
        for half in range(2):
            rows[pl.ds(half, ROWS, stride=2), :] = parts[kind, half]
        store = pltpu.make_async_copy(rows, dst, sem.at[4 + kind])
        store.start()
        stores.append(store)
    loads[1].wait()
    both = [halves[half].astype(F32).reshape(ROWS, GROUP, HD) for half in range(2)]
    joined[...] = jnp.concatenate(both, axis=1).astype(BF16)
    store = pltpu.make_async_copy(joined, attn_out, sem.at[6])
    store.start()
    stores.append(store)
    loads[2].wait()
    wide_joined[...] = jnp.concatenate(
        [wide[half].reshape(ROWS, GROUP, HD) for half in range(2)], axis=1
    )
    store = pltpu.make_async_copy(wide_joined, dq_out, sem.at[3])
    store.start()
    stores.append(store)
    for store in stores:
        store.wait()


def finish(attn, dq, dkv):
    return pl.pallas_call(
        finish_kernel,
        out_shape=(
            jax.ShapeDtypeStruct((ROWS, 2 * GROUP, HD), BF16),
            jax.ShapeDtypeStruct((ROWS, 2 * GROUP, HD), F32),
            jax.ShapeDtypeStruct((2 * ROWS, HD), F32),
            jax.ShapeDtypeStruct((2 * ROWS, HD), F32),
        ),
        in_specs=[HBM] * 3,
        out_specs=(HBM,) * 4,
        scratch_shapes=[
            pltpu.VMEM((2, ROWS * GROUP, HD), BF16),
            pltpu.VMEM((ROWS, 2 * GROUP, HD), BF16),
            pltpu.VMEM((2, ROWS * GROUP, HD), F32),
            pltpu.VMEM((ROWS, 2 * GROUP, HD), F32),
            pltpu.VMEM((2, 2, ROWS, HD), F32),
            pltpu.VMEM((2 * ROWS, HD), F32),
            pltpu.VMEM((2 * ROWS, HD), F32),
            pltpu.SemaphoreType.DMA((7,)),
        ],
        compiler_params=pltpu.CompilerParams(vmem_limit_bytes=60 << 20),
        cost_estimate=pl.CostEstimate(flops=0, bytes_accessed=4 << 20, transcendentals=0),
        name="finish",
    )(attn, dq, dkv)


def local(queries, keys, values, grad_out, span_order, doc_ids):
    turned = [jnp.transpose(a, (1, 2, 0)) for a in (queries, keys, values, grad_out)]
    q_cols, g_cols, q_rows, g_rows, kv = bring(*turned)
    kv = kv.reshape(2 * NZ, 2, 4, SPAN, HD)
    attn, dq, dkv = attend(
        span_order, doc_ids.reshape(SLOTS, ROWS), q_cols, g_cols, q_rows, g_rows, kv
    )
    attn, dq, dkv = give_back(attn, dq, dkv.reshape(2 * NZ, 2, 2 * ROWS, HD))
    attn, dq, dk, dv = finish(attn, dq, dkv)
    return (attn, dq, dk.reshape(ROWS, 2, HD), dv.reshape(ROWS, 2, HD))


def solution(mesh):
    entry = P(("outer", "inner"), None, "head")
    leave = P(("outer", "inner"), "head", None)
    return jax.shard_map(
        local,
        mesh=mesh,
        in_specs=(entry, entry, entry, entry, P(), P()),
        out_specs=(leave, leave, leave, leave),
        check_vma=False,
    )
```

```python
import functools
import math

import jax
import jax.numpy as jnp
from jax import lax
from jax.experimental import pallas as pl
from jax.experimental.pallas import tpu as pltpu
from jax.sharding import PartitionSpec as P

MESH = pl.DeviceIdType.MESH
HBM = pl.BlockSpec(memory_space=pltpu.HBM)
NEG = -1e30
FAR = 1 << 24
NX = 4
NY = 4
NZ = 8
HD = 128
ROWS = 128
SPAN = 64
GROUP = 8
SLOTS = 64
LANES = GROUP * SPAN
SCALE = 1.0 / math.sqrt(HD)
LOG2E = math.log2(math.e)
ITEM = 4
BF16 = jnp.bfloat16
F32 = jnp.float32


def place():
    inner = lax.axis_index("inner")
    return (
        lax.axis_index("head"),
        lax.axis_index("outer"),
        lax.div(inner, 2),
        lax.rem(inner, 2),
    )


def where_is(x, y, z, core):
    return {"head": x, "outer": y, "inner": z * 2 + core}


def greet(partners):
    barrier = pltpu.get_barrier_semaphore()
    for partner in partners:
        pl.semaphore_signal(barrier, inc=1, device_id=partner, device_id_type=MESH)
    pl.semaphore_wait(barrier, len(partners))


def send(src, dst, send_sem, recv_sem, partner):
    copy = pltpu.make_async_remote_copy(
        src_ref=src,
        dst_ref=dst,
        send_sem=send_sem,
        recv_sem=recv_sem,
        device_id=partner,
        device_id_type=MESH,
    )
    copy.start()
    return copy


def bring_kernel(
    q, k, v, g, q_cols_out, g_cols_out, q_rows_out, g_rows_out, kv_out,
    q_cols, g_cols, q_rows, g_rows, out_sem, q_in, g_in, kv_in, ring_kv, relay, relay_sem, own_sem, keep_sem, x_send, x_recv, y_send, y_recv, z_send, z_recv,
):
    x, y, z, core = place()
    peers = [(dx, dc) for dx in range(NX) for dc in range(2) if (dx, dc) != (0, 0)]

    def peer(dx, dc):
        return where_is(lax.rem(x + dx, NX), y, z, lax.rem(core + dc, 2))

    up = where_is(x, y, lax.rem(z + 1, NZ), core)
    down = where_is(x, y, lax.rem(z + NZ - 1, NZ), core)
    later = where_is(x, lax.rem(y + 1, NY), z, core)
    earlier = where_is(x, lax.rem(y + NY - 1, NY), z, core)
    up_z, down_z = lax.rem(z + 1, NZ), lax.rem(z + NZ - 1, NZ)
    later_y, earlier_y = lax.rem(y + 1, NY), lax.rem(y + NY - 1, NY)
    corners = (where_is(x, later_y, up_z, core), where_is(x, later_y, down_z, core))
    behind = [where_is(x, earlier_y, up_z, core), where_is(x, earlier_y, down_z, core)]
    greet([peer(*p) for p in peers] + [up, down, later, earlier, *corners, *behind])

    here = pl.ds(pl.multiple_of(x * 32, 32), 32)
    copies = []
    own = []
    for index, (dx, dc) in enumerate([(0, 0)] + peers):
        head = lax.rem(x + dx, NX) * 2 + lax.rem(core + dc, 2)
        for kind, src in enumerate((k, v)):
            dst = kv_in.at[kind, core, here]
            if index == 0:
                copy = pltpu.make_async_copy(src.at[head], dst, own_sem.at[kind])
                copy.start()
                own.append(copy)
            else:
                copies.append(
                    send(src.at[head], dst, x_send.at[kind, index], x_recv.at[kind, index], peer(dx, dc))
                )
    own[0].wait()
    own[1].wait()
    for copy in copies:
        copy.wait()
    for kind in range(2):
        for block in range(2):
            ring_kv[z, kind, block * ROWS : (block + 1) * ROWS, :] = (
                kv_in[kind, block].astype(F32).T.astype(BF16)
            )
    keeps = []
    sent = []
    ways = (up, down)

    def block_at(group, way, step):
        return group * NZ + lax.rem(z + NZ + step * (1 if way else -1), NZ)

    def keep(block, index):
        copy = pltpu.make_async_copy(ring_kv.at[block], kv_out.at[block], keep_sem.at[index])
        copy.start()
        keeps.append(copy)

    def hop(group, way, step, kind):
        block = block_at(group, way, step - 1)
        copy = send(
            ring_kv.at[block, kind], ring_kv.at[block, kind],
            z_send.at[group, way, step - 1, kind], z_recv.at[group, way, step - 1, kind],
            ways[way],
        )
        sent.append(copy)
        return copy

    def shift(way, step, kind):
        block = block_at(0, way, min(step, 3))
        copy = send(
            ring_kv.at[block, kind], ring_kv.at[NZ + block, kind],
            y_send.at[way, step, kind], y_recv.at[way, step, kind],
            corners[way] if step == 4 else later,
        )
        sent.append(copy)
        return copy

    def settle(kind):
        src, cols, rows = ((q_in, q_cols, q_rows), (g_in, g_cols, g_rows))[kind]
        own[2 + kind].wait()
        for copy in wide[kind]:
            copy.wait()
        low = lax.broadcasted_iota(jnp.int32, (HD, ROWS), 1) < SPAN

        @pl.loop(0, 8)
        def _(index):
            block = lax.div(index, 4)
            pair = lax.rem(index, 4)
            lanes = pl.ds(pl.multiple_of(pair * ROWS, ROWS), ROWS)
            first = src[block, 2 * pair].astype(F32)
            second = src[block, 2 * pair + 1].astype(F32)
            halves = (
                jnp.where(low, first, pltpu.roll(second, SPAN, 1)),
                jnp.where(low, pltpu.roll(first, SPAN, 1), second),
            )
            for half in range(2):
                cols[2 * block + half, :, lanes] = halves[half].astype(BF16)
                rows[2 * block + half, lanes, :] = halves[half].T.astype(BF16)

        outs = ((q_cols_out, q_rows_out), (g_cols_out, g_rows_out))[kind]
        for index, (src, dst) in enumerate(zip((cols, rows), outs)):
            copy = pltpu.make_async_copy(src, dst, out_sem.at[kind, index])
            copy.start()
            own.append(copy)

    near = {}
    self_shift = {}
    for kind in range(2):
        for way in range(2):
            near[way, 1, kind] = hop(0, way, 1, kind)
        self_shift[kind] = shift(0, 0, kind)
    keep(z, 0)
    heads = pl.ds((x * 2 + core) * GROUP, GROUP)
    for kind, (src, dst) in enumerate(((q, q_in), (g, g_in))):
        copy = pltpu.make_async_copy(
            src.at[heads], dst.at[core, :, here], own_sem.at[2 + kind]
        )
        copy.start()
        own.append(copy)
    wide = ([], [])
    relays = []
    for kind, src in enumerate((q, g)):
        relays.append(
            send(
                src.at[pl.ds(lax.rem(x + 2, NX) * 2 * GROUP, 2 * GROUP)], relay.at[kind],
                relay_sem.at[0, kind], relay_sem.at[1, kind], peer(3 if kind else 1, 0),
            )
        )
    for kind, (src, dst) in enumerate(((q, q_in), (g, g_in))):
        for index, (dx, dc) in enumerate(peers):
            if dx == 2:
                continue
            head = lax.rem(x + dx, NX) * 2 + lax.rem(core + dc, 2)
            wide[kind].append(
                send(
                    src.at[pl.ds(head * GROUP, GROUP)],
                    dst.at[core, :, here],
                    x_send.at[2 + kind, index],
                    x_recv.at[2 + kind, index],
                    peer(dx, dc),
                )
            )
    def forward(kind):
        relays[kind].wait_recv()
        from_x = lax.rem(x + (1 if kind else 3), NX)
        there = pl.ds(pl.multiple_of(from_x * 32, 32), 32)
        for index, (dx, dc) in enumerate(peers):
            if dx != 2:
                continue
            head = pl.ds(lax.rem(core + dc, 2) * GROUP, GROUP)
            wide[kind].append(
                send(
                    relay.at[kind, head],
                    (q_in, g_in)[kind].at[core, :, there],
                    x_send.at[2 + kind, index],
                    x_recv.at[2 + kind, index],
                    peer(3 if kind else 1, dc),
                )
            )

    far_shift = {}
    for step in range(1, 4):
        for kind in range(2):
            for way in range(2):
                near[way, step, kind].wait_recv()
                if step < 3 or kind == way:
                    near[way, step + 1, kind] = hop(0, way, step + 1, kind)
                if step == 3 and kind == way:
                    far_shift[way, 4] = shift(way, 4, way)
                if step == 2 or (step == 1 and kind == way):
                    far_shift[way, step, kind] = shift(way, step, kind)
        for way in range(2):
            keep(block_at(0, way, step), 1 + 2 * step + way)
        if step == 1:
            forward(0)
            forward(1)
    hops = {}
    for kind in range(2):
        self_shift[kind].wait_recv()
        hops[1 - kind, 1, kind] = hop(1, 1 - kind, 1, kind)
    keep(NZ + z, 1)
    for kind in range(2):
        for way in range(2):
            far_shift[way, 2, kind].wait_recv()
            hops[way, 3, kind] = hop(1, way, 3, kind)
    for way in range(2):
        keep(block_at(1, way, 2), 9 + way)
    settle(0)
    settle(1)
    for way in range(2):
        near[way, 4, way].wait_recv()
    keep(block_at(0, 0, 4), 2)
    for step in (1, 3):
        for way in range(2):
            for kind in range(2):
                arriving = far_shift if step == 1 and kind == way else hops
                arriving[way, step, kind].wait_recv()
            keep(block_at(1, way, step), 10 + step + way)
    for way in range(2):
        far_shift[way, 4].wait_recv()
    keep(block_at(1, 0, 4), 15)
    for copy in sent + relays:
        copy.wait_send()
    for copy in keeps:
        copy.wait()
    for copy in own[4:]:
        copy.wait()


def bring(q, k, v, g):
    return pl.pallas_call(
        bring_kernel,
        out_shape=(
            jax.ShapeDtypeStruct((4, HD, LANES), BF16),
            jax.ShapeDtypeStruct((4, HD, LANES), BF16),
            jax.ShapeDtypeStruct((4, LANES, HD), BF16),
            jax.ShapeDtypeStruct((4, LANES, HD), BF16),
            jax.ShapeDtypeStruct((2 * NZ, 2, 2 * ROWS, HD), BF16),
        ),
        in_specs=[HBM] * 4,
        out_specs=(HBM,) * 5,
        scratch_shapes=[
            pltpu.VMEM((4, HD, LANES), BF16),
            pltpu.VMEM((4, HD, LANES), BF16),
            pltpu.VMEM((4, LANES, HD), BF16),
            pltpu.VMEM((4, LANES, HD), BF16),
            pltpu.SemaphoreType.DMA((2, 2)),
            pltpu.VMEM((2, GROUP, HD, ROWS), BF16),
            pltpu.VMEM((2, GROUP, HD, ROWS), BF16),
            pltpu.VMEM((2, 2, HD, ROWS), BF16),
            pltpu.VMEM((2 * NZ, 2, 2 * ROWS, HD), BF16),
            pltpu.VMEM((2, 2 * GROUP, HD // NX, ROWS), BF16),
            pltpu.SemaphoreType.DMA((2, 2)),
            pltpu.SemaphoreType.DMA((4,)),
            pltpu.SemaphoreType.DMA((16,)),
            pltpu.SemaphoreType.DMA((4, 8)),
            pltpu.SemaphoreType.DMA((4, 8)),
            pltpu.SemaphoreType.DMA((2, 5, 2)),
            pltpu.SemaphoreType.DMA((2, 5, 2)),
            pltpu.SemaphoreType.DMA((2, 2, 4, 2)),
            pltpu.SemaphoreType.DMA((2, 2, 4, 2)),
        ],
        compiler_params=pltpu.CompilerParams(
            collective_id=0, has_side_effects=True, vmem_limit_bytes=60 << 20
        ),
        name="bring",
    )(q, k, v, g)


def attend_kernel(
    order_in, docs_in, q_cols_in, g_cols_in, q_rows_in, g_rows_in, kv_in, both_out, dkv,
    order, docs, q_cols, g_cols, q_rows, g_rows, both, dq, kv, scores, key_acc, value_acc, out_acc, tops, sums, shift, dots,
    pos_rows, start_rows, item_list, span_list, in_sem, out_sem,
):
    outer = lax.axis_index("outer")
    chip = lax.div(lax.axis_index("inner"), 2)
    loads = [
        pltpu.make_async_copy(order_in, order, in_sem.at[0]),
        pltpu.make_async_copy(docs_in, docs, in_sem.at[1]),
        pltpu.make_async_copy(q_cols_in, q_cols, in_sem.at[2]),
        pltpu.make_async_copy(kv_in.at[:, 0], kv.at[pl.ds(0, 2 * NZ), 0], in_sem.at[3]),
        pltpu.make_async_copy(kv_in.at[:, 1], kv.at[pl.ds(0, 2 * NZ), 1], in_sem.at[4]),
        pltpu.make_async_copy(g_cols_in, g_cols, in_sem.at[5]),
        pltpu.make_async_copy(q_rows_in, q_rows, in_sem.at[6]),
        pltpu.make_async_copy(g_rows_in, g_rows, in_sem.at[7]),
    ]
    for load in loads:
        load.start()
    kv[2 * NZ] = jnp.zeros((2, 4, SPAN, HD), BF16)
    tops[...] = jnp.full_like(tops, NEG)
    sums[...] = jnp.zeros_like(sums)
    loads[0].wait()
    loads[1].wait()
    doc = docs[...]
    starts = [
        jnp.sum(jnp.where(doc < d, 1.0, 0.0)).astype(jnp.int32) for d in range(1, 4)
    ]

    def start_of(position):
        found = jnp.zeros_like(position)
        for start in starts:
            found = jnp.where(position >= start, jnp.maximum(found, start), found)
        return found

    iota_lanes = lax.rem(lax.broadcasted_iota(jnp.int32, (8, ROWS), 1), SPAN)
    lows = []
    highs = []
    for unit in range(4):
        query_span = order[outer * 32 + chip * 4 + unit]
        lows.append(lax.div(start_of(query_span * SPAN), SPAN))
        highs.append(query_span)
        query_pos = query_span * SPAN + iota_lanes
        pos_rows[unit] = query_pos
        start_rows[unit] = start_of(query_pos)

    counts = tuple(jnp.int32(unit * 128) for unit in range(4))
    for group in range(2):
        stored = lax.rem(outer + 4 - group, 4) * 32

        def note(step, counts):
            for part in range(8):
                slot = step * 8 + part
                span = order[stored + slot]
                entry = span * (2 * SPAN) + (group * 32 + slot)
                new = []
                for unit in range(4):
                    span_list[counts[unit]] = entry
                    allowed = (span >= lows[unit]) & (span <= highs[unit])
                    new.append(counts[unit] + jnp.where(allowed, 1, 0))
                counts = tuple(new)
            nothing = jnp.zeros((8, SPAN, HD), F32)
            rows = pl.ds((group * 4 + step) * 8, 8)
            key_acc[rows] = nothing
            value_acc[rows] = nothing
            flat = pl.ds(pl.multiple_of(step * 32, 32), 32)
            for unit in range(2 * group, 2 * group + 2):
                out_acc[unit, flat, :] = jnp.zeros((32, LANES), F32)
                dq[unit, flat, :] = jnp.zeros((32, LANES), F32)
            return counts

        counts = lax.fori_loop(0, 4, note, counts)
    items = jnp.int32(0)
    for unit in range(4):
        for extra in range(ITEM):
            span_list[counts[unit] + extra] = 2 * FAR + SLOTS
        for chunk in range(SLOTS // ITEM):
            item_list[items + chunk] = unit * 128 + chunk * ITEM
        items = items + lax.div(counts[unit] - unit * 128 + ITEM - 1, ITEM)
    blank = 3 * 128 + 72
    for extra in range(ITEM):
        span_list[blank + extra] = 2 * FAR + SLOTS
    for extra in range(4):
        item_list[items + extra] = blank
    steps = lax.div(items + 1, 2)
    long_steps = lax.div(items + 3, 4)

    iota_keys = (
        lax.broadcasted_iota(jnp.int32, (8, 8, ROWS), 0) * 8
        + lax.broadcasted_iota(jnp.int32, (8, 8, ROWS), 1)
    )

    def entries(item):
        first = item_list[item]
        found = [span_list[first + part] for part in range(ITEM)]
        slots = [lax.rem(entry, 2 * SPAN) for entry in found]
        return lax.div(first, 128), slots, [lax.div(a - b, 2) for a, b in zip(found, slots)]

    def spans(slots, kind):
        parts = []
        for slot in slots:
            parts.append(kv[lax.div(slot, 4), kind, lax.rem(slot, 4)])
        return jnp.concatenate(parts, axis=0)

    sides = [pl.ds(side * 256, 256) for side in range(2)]
    loads[2].wait()
    loads[3].wait()

    @functools.partial(lax.fori_loop, 0, long_steps, init_val=0)
    def _(step, _):
        results = []
        for item in [4 * step + part for part in range(4)]:
            unit, slots, bases = entries(item)
            keys = spans(slots, 0)
            biases = []
            for base in bases:
                allowed = (iota_keys <= (pos_rows[unit] - base)[None]) & (
                    iota_keys >= (start_rows[unit] - base)[None]
                )
                biases.append(jnp.where(allowed, 0.0, NEG).reshape(SPAN, ROWS))
            bias = jnp.concatenate(biases, axis=0)
            bias = jnp.concatenate([bias, bias], axis=1)
            for lanes in sides:
                tile = jnp.dot(keys, q_cols[unit, :, lanes], preferred_element_type=F32)
                tile = tile * (SCALE * LOG2E) + bias
                scores[item, :, lanes] = tile
                results.append((unit, lanes, jnp.max(tile.reshape(32, 8, 256), axis=0)))
        for unit, lanes, top in results:
            tops[unit, :, lanes] = jnp.maximum(tops[unit, :, lanes], top)
        return 0

    for unit in range(4):
        shift[unit] = jnp.broadcast_to(jnp.max(tops[unit], axis=0, keepdims=True), (8, LANES))
    loads[4].wait()

    @functools.partial(lax.fori_loop, 0, long_steps, init_val=0)
    def _(step, _):
        results = []
        for item in [4 * step + part for part in range(4)]:
            unit, slots, _ = entries(item)
            values_t = spans(slots, 1).T
            for lanes in sides:
                logits = scores[item, :, lanes].reshape(32, 8, 256)
                probs = jnp.exp2(logits - shift[unit, :, lanes][None])
                part = jnp.dot(
                    values_t, probs.reshape(256, 256).astype(BF16), preferred_element_type=F32
                )
                results.append((unit, lanes, jnp.sum(probs, axis=0), part))
        for unit, lanes, total, part in results:
            sums[unit, :, lanes] += total
            out_acc[unit, :, lanes] += part
        return 0

    for load in loads[5:]:
        load.wait()
    for unit in range(4):
        row_sum = jnp.sum(sums[unit], axis=0, keepdims=True)
        out = (out_acc[unit] * (1.0 / row_sum)).astype(BF16)
        both[unit, 0] = out
        row_dot = jnp.sum(
            out.astype(F32) * g_cols[unit].astype(F32), axis=0, keepdims=True
        )
        dots[unit] = jnp.broadcast_to(row_dot, (8, LANES))
        shift[unit] = shift[unit] + jnp.log(row_sum) * LOG2E

    @functools.partial(lax.fori_loop, 0, steps, init_val=0)
    def _(step, _):
        results = []
        for item in (2 * step, 2 * step + 1):
            unit, slots, _ = entries(item)
            keys_t = spans(slots, 0).T
            values = spans(slots, 1)
            probs_b = []
            score_grads = []
            for lanes in sides:
                logits = scores[item, :, lanes].reshape(32, 8, 256)
                probs = jnp.exp2(logits - shift[unit, :, lanes][None])
                steep = jnp.dot(values, g_cols[unit, :, lanes], preferred_element_type=F32)
                steep = probs * (steep.reshape(32, 8, 256) - dots[unit, :, lanes][None])
                probs_b.append(probs.reshape(256, 256).astype(BF16))
                score_grads.append(steep.reshape(256, 256).astype(BF16))
            probs_b = jnp.concatenate(probs_b, axis=1)
            score_grads = jnp.concatenate(score_grads, axis=1)
            to_values = jnp.dot(probs_b, g_rows[unit], preferred_element_type=F32)
            to_keys = jnp.dot(score_grads, q_rows[unit], preferred_element_type=F32)
            to_query = jnp.dot(keys_t, score_grads, preferred_element_type=F32)
            results.append((slots, unit, to_values, to_keys, to_query))
        for slots, unit, to_values, to_keys, to_query in results:
            dq[unit] += to_query
            for acc, part in ((key_acc, to_keys), (value_acc, to_values)):
                sums_of = [
                    acc[slot] + part[index * SPAN : (index + 1) * SPAN]
                    for index, slot in enumerate(slots)
                ]
                for slot, total in zip(slots, sums_of):
                    acc[slot] = total
        return 0

    for unit in range(4):
        both[unit, 1] = (dq[unit] * SCALE).astype(BF16)
    both_store = pltpu.make_async_copy(both, both_out, out_sem.at[2 * NZ])
    both_store.start()
    stores = [both_store]
    for index in range(2 * NZ):
        for part in range(4):
            kv[index, 0, part] = (key_acc[index * 4 + part] * SCALE).astype(BF16)
            kv[index, 1, part] = value_acc[index * 4 + part].astype(BF16)
        store = pltpu.make_async_copy(kv.at[index], dkv.at[index], out_sem.at[index])
        store.start()
        stores.append(store)
    for store in stores:
        store.wait()


def attend(order, docs, q_cols, g_cols, q_rows, g_rows, kv):
    return pl.pallas_call(
        attend_kernel,
        out_shape=(
            jax.ShapeDtypeStruct((4, 2, HD, LANES), BF16),
            jax.ShapeDtypeStruct((2 * NZ, 2, 4, SPAN, HD), BF16),
        ),
        in_specs=[HBM] * 7,
        out_specs=(HBM,) * 2,
        scratch_shapes=[
            pltpu.SMEM((2 * SLOTS,), jnp.int32),
            pltpu.VMEM((SLOTS, ROWS), jnp.int32),
            pltpu.VMEM((4, HD, LANES), BF16),
            pltpu.VMEM((4, HD, LANES), BF16),
            pltpu.VMEM((4, LANES, HD), BF16),
            pltpu.VMEM((4, LANES, HD), BF16),
            pltpu.VMEM((4, 2, HD, LANES), BF16),
            pltpu.VMEM((4, HD, LANES), F32),
            pltpu.VMEM((2 * NZ + 1, 2, 4, SPAN, HD), BF16),
            pltpu.VMEM((4 * SLOTS // ITEM, ITEM * SPAN, LANES), F32),
            pltpu.VMEM((SLOTS + 1, SPAN, HD), F32),
            pltpu.VMEM((SLOTS + 1, SPAN, HD), F32),
            pltpu.VMEM((4, HD, LANES), F32),
            pltpu.VMEM((4, 8, LANES), F32),
            pltpu.VMEM((4, 8, LANES), F32),
            pltpu.VMEM((4, 8, LANES), F32),
            pltpu.VMEM((4, 8, LANES), F32),
            pltpu.VMEM((4, 8, ROWS), jnp.int32),
            pltpu.VMEM((4, 8, ROWS), jnp.int32),
            pltpu.SMEM((80,), jnp.int32),
            pltpu.SMEM((512,), jnp.int32),
            pltpu.SemaphoreType.DMA((8,)),
            pltpu.SemaphoreType.DMA((2 * NZ + 1,)),
        ],
        compiler_params=pltpu.CompilerParams(vmem_limit_bytes=60 << 20),
        cost_estimate=pl.CostEstimate(
            flops=6 * 2 * 2048 * 2048 * HD, bytes_accessed=12 << 20, transcendentals=2048 * 2048
        ),
        name="attend",
    )(order, docs, q_cols, g_cols, q_rows, g_rows, kv)


def return_kernel(
    both_in, dkv, both_out, dkv_out,
    both, terms, both_rows, order, landed, landed_rows, final, pair_send, pair_recv, own_sem, l_send, l_recv, r_send, r_recv,
):
    x, y, z, core = place()
    sibling = where_is(x, y, z, 1 - core)
    up = where_is(x, y, lax.rem(z + 1, NZ), core)
    down = where_is(x, y, lax.rem(z + NZ - 1, NZ), core)
    later = where_is(x, lax.rem(y + 1, NY), z, core)
    earlier = where_is(x, lax.rem(y + NY - 1, NY), z, core)
    loads = [
        pltpu.make_async_copy(both_in, both, own_sem.at[5]),
        pltpu.make_async_copy(dkv, terms, own_sem.at[4]),
    ]
    for load in loads:
        load.start()
    up_z, down_z = lax.rem(z + 1, NZ), lax.rem(z + NZ - 1, NZ)
    later_y, earlier_y = lax.rem(y + 1, NY), lax.rem(y + NY - 1, NY)
    corners = (where_is(x, earlier_y, up_z, core), where_is(x, earlier_y, down_z, core))
    behind = [where_is(x, later_y, up_z, core), where_is(x, later_y, down_z, core)]
    across = [
        where_is(x, y, up_z, 1 - core),
        where_is(x, y, down_z, 1 - core),
        where_is(x, earlier_y, z, 1 - core),
    ]
    greet(
        [sibling, up, down, later, earlier, *corners, *behind, *across]
        + [where_is(x, later_y, z, 1 - core)]
    )

    ways = (up, down)
    sent = []

    def at(group, distance, way):
        return group * NZ + lax.rem(z + NZ + distance * (-1 if way else 1), NZ)

    def ship(src, index, partner):
        copy = send(src, landed.at[index], l_send.at[index], l_recv.at[index], partner)
        sent.append(copy)
        return copy

    def add(block, kind, *indices):
        total = terms[block, kind].astype(F32)
        for index in indices:
            total = total + landed[index].astype(F32)
        terms[block, kind] = total.astype(BF16)

    mine = pl.ds(pl.multiple_of(core * ROWS, ROWS), ROWS)
    other = pl.ds(pl.multiple_of((1 - core) * ROWS, ROWS), ROWS)

    def deliver(block, kind, index, straight, crossed):
        copies = []
        for half, rows, partner in ((0, mine, straight), (1, other, crossed)):
            copy = send(
                terms.at[block, kind, rows], landed_rows.at[half, index],
                r_send.at[half, index], r_recv.at[half, index], partner,
            )
            sent.append(copy)
            copies.append(copy)
        return copies

    flying = {}
    for way in range(2):
        flying["s", 1, way, way] = ship(dkv.at[at(0, 4, 0), way], 16 + way, ways[way])
    for step, distance in ((0, 3), (1, 1)):
        for kind in range(2):
            for way in range(2):
                if step == 1 and kind == way:
                    continue
                flying["z", step, way, kind] = ship(
                    dkv.at[at(1, distance, way), kind], step * 4 + way * 2 + kind, ways[way]
                )
        if step == 0:
            for kind in range(2):
                flying["y", 4, kind] = ship(dkv.at[at(1, 4, 0), kind], 8 + kind, corners[kind])
    swaps = []
    own = []

    def turn(block, half):
        stacked = both[2 * block + half].reshape(2 * HD, LANES)
        rows = lax.dot_general(
            order[...], stacked, (((1,), (1,)), ((), ())), preferred_element_type=F32
        ).astype(BF16)
        for kind in range(2):
            both_rows[block, kind, half * LANES : (half + 1) * LANES, :] = rows[
                :, kind * HD : (kind + 1) * HD
            ]

    def swap():
        swaps.append(
            send(
                both_rows.at[1 - core], both_out.at[core], pair_send.at[0], pair_recv.at[0], sibling
            )
        )

    def stay():
        copy = pltpu.make_async_copy(both_rows.at[core], both_out.at[core], own_sem.at[0])
        copy.start()
        own.append(copy)

    row = lax.broadcasted_iota(jnp.int32, (LANES, LANES), 0)
    lane = lax.broadcasted_iota(jnp.int32, (LANES, LANES), 1)
    from_lane = lax.rem(row, GROUP) * SPAN + lax.div(row, GROUP)
    order[...] = jnp.where(lane == from_lane, 1.0, 0.0).astype(BF16)
    loads[1].wait()
    for kind in range(2):
        for way in range(2):
            flying["z", 0, way, kind].wait_recv()
            block = at(1, 2, way)
            add(block, kind, way * 2 + kind)
            flying["y", 2, way, kind] = ship(
                terms.at[block, kind], 10 + way * 2 + kind, earlier
            )
    for way in range(2):
        flying["y", 1, way] = ship(dkv.at[at(1, 1, way), way], 30 + way, earlier)
    for way in range(2):
        kind = 1 - way
        flying["s", 2, way, kind] = ship(
            terms.at[at(0, 3, way), kind], 18 + way * 2 + kind, ways[way]
        )
    loads[0].wait()
    turn(1 - core, 0)
    for kind in range(2):
        swaps.append(
            send(
                dkv.at[z, kind, other], landed_rows.at[1, 6 + kind],
                r_send.at[1, 6 + kind], r_recv.at[1, 6 + kind], sibling,
            )
        )
    for way in range(2):
        flying["s", 1, way, way].wait_recv()
        flying["y", 4, way].wait_recv()
        add(at(0, 3, way), way, 16 + way, 8 + way)
        flying["s", 2, way, way] = ship(
            terms.at[at(0, 3, way), way], 18 + way * 2 + way, ways[way]
        )
    for kind in range(2):
        way = 1 - kind
        flying["z", 1, way, kind].wait_recv()
        add(NZ + z, kind, 4 + way * 2 + kind)
        flying["y", 0, kind] = deliver(NZ + z, kind, kind, earlier, across[2])
    turn(1 - core, 1)
    swap()
    for step in (3, 4):
        for turn_of in range(2):
            for way in range(2):
                kind = turn_of if way else 1 - turn_of
                flying["s", step - 1, way, kind].wait_recv()
                indices = [18 + (step - 3) * 4 + way * 2 + kind]
                if step == 3:
                    flying["y", 2, way, kind].wait_recv()
                    indices.append(10 + way * 2 + kind)
                elif kind == way:
                    flying["y", 1, way].wait_recv()
                    indices.append(30 + way)
                block = at(0, 5 - step, way)
                add(block, kind, *indices)
                if step == 3:
                    flying["s", step, way, kind] = ship(
                        terms.at[block, kind], 22 + way * 2 + kind, ways[way]
                    )
                else:
                    flying["s", step, way, kind] = deliver(
                        block, kind, 2 + way * 2 + kind, ways[way], across[way]
                    )
        turn(core, step - 3)
    stay()
    for kind in range(2):
        for half in range(2):
            flying["y", 0, kind][half].wait_recv()
            for way in range(2):
                flying["s", 4, way, kind][half].wait_recv()
            if half:
                swaps[kind].wait_recv()
                total = landed_rows[1, 6 + kind].astype(F32)
            else:
                total = terms[z, kind, mine].astype(F32)
            for index in (kind, 2 + kind, 4 + kind):
                total = total + landed_rows[half, index].astype(F32)
            final[kind, half] = total
        for half in range(2):
            copy = pltpu.make_async_copy(
                final.at[kind, half], dkv_out.at[kind, core if half == 0 else 1 - core],
                own_sem.at[2 + (0, 5)[half] + kind],
            )
            copy.start()
            own.append(copy)
    for copy in sent:
        copy.wait_send()
    for copy in swaps[:2]:
        copy.wait_send()
    swaps[2].wait()
    for copy in own:
        copy.wait()


def give_back(both, dkv):
    return pl.pallas_call(
        return_kernel,
        out_shape=(
            jax.ShapeDtypeStruct((2, 2, ROWS * GROUP, HD), BF16),
            jax.ShapeDtypeStruct((2, 2, ROWS, HD), F32),
        ),
        in_specs=[HBM] * 2,
        out_specs=(HBM,) * 2,
        scratch_shapes=[
            pltpu.VMEM((4, 2, HD, LANES), BF16),
            pltpu.VMEM((2 * NZ, 2, 2 * ROWS, HD), BF16),
            pltpu.VMEM((2, 2, ROWS * GROUP, HD), BF16),
            pltpu.VMEM((LANES, LANES), BF16),
            pltpu.VMEM((32, 2 * ROWS, HD), BF16),
            pltpu.VMEM((2, 8, ROWS, HD), BF16),
            pltpu.VMEM((2, 2, ROWS, HD), F32),
            pltpu.SemaphoreType.DMA((1,)),
            pltpu.SemaphoreType.DMA((1,)),
            pltpu.SemaphoreType.DMA((9,)),
            pltpu.SemaphoreType.DMA((32,)),
            pltpu.SemaphoreType.DMA((32,)),
            pltpu.SemaphoreType.DMA((2, 8)),
            pltpu.SemaphoreType.DMA((2, 8)),
        ],
        compiler_params=pltpu.CompilerParams(
            collective_id=1, has_side_effects=True, vmem_limit_bytes=60 << 20
        ),
        name="give_back",
    )(both, dkv)


def finish_kernel(
    both, dkv, attn_out, dq_out, dk_out, dv_out, halves, attn, dq, parts, dk, dv, sem
):
    loads = [pltpu.make_async_copy(dkv, parts, sem.at[0])]
    for kind in range(2):
        loads.append(
            pltpu.make_async_copy(both.at[:, kind], halves.at[:, kind], sem.at[1 + kind])
        )
    for load in loads:
        load.start()
    stores = []
    loads[0].wait()
    for kind, (rows, dst) in enumerate(((dk, dk_out), (dv, dv_out))):
        for half in range(2):
            rows[pl.ds(half, ROWS, stride=2), :] = parts[kind, half]
        store = pltpu.make_async_copy(rows, dst, sem.at[3 + kind])
        store.start()
        stores.append(store)
    for kind, (joined, dst) in ((1, (dq, dq_out)), (0, (attn, attn_out))):
        loads[1 + kind].wait()
        pair = [halves[half, kind].astype(F32).reshape(ROWS, GROUP, HD) for half in range(2)]
        joined[...] = jnp.concatenate(pair, axis=1).astype(joined.dtype)
        store = pltpu.make_async_copy(joined, dst, sem.at[5 + kind])
        store.start()
        stores.append(store)
    for store in stores:
        store.wait()


def finish(both, dkv):
    return pl.pallas_call(
        finish_kernel,
        out_shape=(
            jax.ShapeDtypeStruct((ROWS, 2 * GROUP, HD), BF16),
            jax.ShapeDtypeStruct((ROWS, 2 * GROUP, HD), F32),
            jax.ShapeDtypeStruct((2 * ROWS, HD), F32),
            jax.ShapeDtypeStruct((2 * ROWS, HD), F32),
        ),
        in_specs=[HBM] * 2,
        out_specs=(HBM,) * 4,
        scratch_shapes=[
            pltpu.VMEM((2, 2, ROWS * GROUP, HD), BF16),
            pltpu.VMEM((ROWS, 2 * GROUP, HD), BF16),
            pltpu.VMEM((ROWS, 2 * GROUP, HD), F32),
            pltpu.VMEM((2, 2, ROWS, HD), F32),
            pltpu.VMEM((2 * ROWS, HD), F32),
            pltpu.VMEM((2 * ROWS, HD), F32),
            pltpu.SemaphoreType.DMA((7,)),
        ],
        compiler_params=pltpu.CompilerParams(vmem_limit_bytes=60 << 20),
        cost_estimate=pl.CostEstimate(flops=0, bytes_accessed=4 << 20, transcendentals=0),
        name="finish",
    )(both, dkv)


def local(queries, keys, values, grad_out, span_order, doc_ids):
    turned = [jnp.transpose(a, (1, 2, 0)) for a in (queries, keys, values, grad_out)]
    q_cols, g_cols, q_rows, g_rows, kv = bring(*turned)
    kv = kv.reshape(2 * NZ, 2, 4, SPAN, HD)
    both, dkv = attend(
        span_order, doc_ids.reshape(SLOTS, ROWS), q_cols, g_cols, q_rows, g_rows, kv
    )
    both, dkv = give_back(both, dkv.reshape(2 * NZ, 2, 2 * ROWS, HD))
    attn, dq, dk, dv = finish(both, dkv)
    return (attn, dq, dk.reshape(ROWS, 2, HD), dv.reshape(ROWS, 2, HD))


def solution(mesh):
    entry = P(("outer", "inner"), None, "head")
    leave = P(("outer", "inner"), "head", None)
    return jax.shard_map(
        local,
        mesh=mesh,
        in_specs=(entry, entry, entry, entry, P(), P()),
        out_specs=(leave, leave, leave, leave),
        check_vma=False,
    )
```

```python
import functools
import math

import jax
import jax.numpy as jnp
from jax import lax
from jax.experimental import pallas as pl
from jax.experimental.pallas import tpu as pltpu
from jax.sharding import PartitionSpec as P

MESH = pl.DeviceIdType.MESH
HBM = pl.BlockSpec(memory_space=pltpu.HBM)
NEG = -1e30
FAR = 1 << 24
NX = 4
NY = 4
NZ = 8
HD = 128
ROWS = 128
SPAN = 64
GROUP = 8
SLOTS = 64
LANES = GROUP * SPAN
SCALE = 1.0 / math.sqrt(HD)
LOG2E = math.log2(math.e)
ITEM = 4
BF16 = jnp.bfloat16
F32 = jnp.float32


def place():
    inner = lax.axis_index("inner")
    return (
        lax.axis_index("head"),
        lax.axis_index("outer"),
        lax.div(inner, 2),
        lax.rem(inner, 2),
    )


def where_is(x, y, z, core):
    return {"head": x, "outer": y, "inner": z * 2 + core}


def greet(partners):
    barrier = pltpu.get_barrier_semaphore()
    for partner in partners:
        pl.semaphore_signal(barrier, inc=1, device_id=partner, device_id_type=MESH)
    pl.semaphore_wait(barrier, len(partners))


def send(src, dst, send_sem, recv_sem, partner):
    copy = pltpu.make_async_remote_copy(
        src_ref=src,
        dst_ref=dst,
        send_sem=send_sem,
        recv_sem=recv_sem,
        device_id=partner,
        device_id_type=MESH,
    )
    copy.start()
    return copy


def bring_kernel(
    q, k, v, g, q_cols_out, g_cols_out, q_rows_out, g_rows_out, kv_out,
    q_cols, g_cols, q_rows, g_rows, out_sem, q_in, g_in, kv_in, ring_kv, relay, relay_sem, own_sem, keep_sem, x_send, x_recv, y_send, y_recv, z_send, z_recv,
):
    x, y, z, core = place()
    peers = [(dx, dc) for dx in range(NX) for dc in range(2) if (dx, dc) != (0, 0)]

    def peer(dx, dc):
        return where_is(lax.rem(x + dx, NX), y, z, lax.rem(core + dc, 2))

    up = where_is(x, y, lax.rem(z + 1, NZ), core)
    down = where_is(x, y, lax.rem(z + NZ - 1, NZ), core)
    later = where_is(x, lax.rem(y + 1, NY), z, core)
    earlier = where_is(x, lax.rem(y + NY - 1, NY), z, core)
    up_z, down_z = lax.rem(z + 1, NZ), lax.rem(z + NZ - 1, NZ)
    later_y, earlier_y = lax.rem(y + 1, NY), lax.rem(y + NY - 1, NY)
    corners = (where_is(x, later_y, up_z, core), where_is(x, later_y, down_z, core))
    behind = [where_is(x, earlier_y, up_z, core), where_is(x, earlier_y, down_z, core)]
    greet([peer(*p) for p in peers] + [up, down, later, earlier, *corners, *behind])

    here = pl.ds(pl.multiple_of(x * 32, 32), 32)
    copies = []
    own = []
    for index, (dx, dc) in enumerate([(0, 0)] + peers):
        head = lax.rem(x + dx, NX) * 2 + lax.rem(core + dc, 2)
        for kind, src in enumerate((k, v)):
            dst = kv_in.at[kind, core, here]
            if index == 0:
                copy = pltpu.make_async_copy(src.at[head], dst, own_sem.at[kind])
                copy.start()
                own.append(copy)
            else:
                copies.append(
                    send(src.at[head], dst, x_send.at[kind, index], x_recv.at[kind, index], peer(dx, dc))
                )
    own[0].wait()
    own[1].wait()
    for copy in copies:
        copy.wait()
    for kind in range(2):
        for block in range(2):
            ring_kv[z, kind, block * ROWS : (block + 1) * ROWS, :] = (
                kv_in[kind, block].astype(F32).T.astype(BF16)
            )
    keeps = []
    sent = []
    ways = (up, down)

    def block_at(group, way, step):
        return group * NZ + lax.rem(z + NZ + step * (1 if way else -1), NZ)

    def keep(block, index):
        copy = pltpu.make_async_copy(ring_kv.at[block], kv_out.at[block], keep_sem.at[index])
        copy.start()
        keeps.append(copy)

    def hop(group, way, step, kind):
        block = block_at(group, way, step - 1)
        copy = send(
            ring_kv.at[block, kind], ring_kv.at[block, kind],
            z_send.at[group, way, step - 1, kind], z_recv.at[group, way, step - 1, kind],
            ways[way],
        )
        sent.append(copy)
        return copy

    def shift(way, step, kind):
        block = block_at(0, way, min(step, 3))
        copy = send(
            ring_kv.at[block, kind], ring_kv.at[NZ + block, kind],
            y_send.at[way, step, kind], y_recv.at[way, step, kind],
            corners[way] if step == 4 else later,
        )
        sent.append(copy)
        return copy

    def settle(kind):
        src, cols, rows = ((q_in, q_cols, q_rows), (g_in, g_cols, g_rows))[kind]
        own[2 + kind].wait()
        for copy in wide[kind]:
            copy.wait()
        low = lax.broadcasted_iota(jnp.int32, (HD, ROWS), 1) < SPAN

        @pl.loop(0, 8)
        def _(index):
            block = lax.div(index, 4)
            pair = lax.rem(index, 4)
            lanes = pl.ds(pl.multiple_of(pair * ROWS, ROWS), ROWS)
            first, second = [
                jnp.concatenate([src[block, a, 2 * pair + b] for a in range(NX)], axis=0).astype(F32)
                for b in range(2)
            ]
            halves = (
                jnp.where(low, first, pltpu.roll(second, SPAN, 1)),
                jnp.where(low, pltpu.roll(first, SPAN, 1), second),
            )
            for half in range(2):
                cols[2 * block + half, :, lanes] = halves[half].astype(BF16)
                rows[2 * block + half, lanes, :] = halves[half].T.astype(BF16)

        outs = ((q_cols_out, q_rows_out), (g_cols_out, g_rows_out))[kind]
        for index, (src, dst) in enumerate(zip((cols, rows), outs)):
            copy = pltpu.make_async_copy(src, dst, out_sem.at[kind, index])
            copy.start()
            own.append(copy)

    near = {}
    self_shift = {}
    for kind in range(2):
        for way in range(2):
            near[way, 1, kind] = hop(0, way, 1, kind)
        self_shift[kind] = shift(0, 0, kind)
    keep(z, 0)
    heads = pl.ds((x * 2 + core) * GROUP, GROUP)
    for kind, (src, dst) in enumerate(((q, q_in), (g, g_in))):
        copy = pltpu.make_async_copy(
            src.at[heads], dst.at[core, x], own_sem.at[2 + kind]
        )
        copy.start()
        own.append(copy)
    wide = ([], [])
    relays = []
    for kind, src in enumerate((q, g)):
        relays.append(
            send(
                src.at[pl.ds(lax.rem(x + 2, NX) * 2 * GROUP, 2 * GROUP)], relay.at[kind],
                relay_sem.at[0, kind], relay_sem.at[1, kind], peer(3 if kind else 1, 0),
            )
        )
    for kind, (src, dst) in enumerate(((q, q_in), (g, g_in))):
        for index, (dx, dc) in enumerate(peers):
            if dx == 2:
                continue
            head = lax.rem(x + dx, NX) * 2 + lax.rem(core + dc, 2)
            wide[kind].append(
                send(
                    src.at[pl.ds(head * GROUP, GROUP)],
                    dst.at[core, x],
                    x_send.at[2 + kind, index],
                    x_recv.at[2 + kind, index],
                    peer(dx, dc),
                )
            )
    def forward(kind):
        relays[kind].wait_recv()
        from_x = lax.rem(x + (1 if kind else 3), NX)
        for index, (dx, dc) in enumerate(peers):
            if dx != 2:
                continue
            head = pl.ds(lax.rem(core + dc, 2) * GROUP, GROUP)
            wide[kind].append(
                send(
                    relay.at[kind, head],
                    (q_in, g_in)[kind].at[core, from_x],
                    x_send.at[2 + kind, index],
                    x_recv.at[2 + kind, index],
                    peer(3 if kind else 1, dc),
                )
            )

    far_shift = {}
    for step in range(1, 4):
        for kind in range(2):
            for way in range(2):
                near[way, step, kind].wait_recv()
                if step < 3 or kind == way:
                    near[way, step + 1, kind] = hop(0, way, step + 1, kind)
                if step == 3 and kind == way:
                    far_shift[way, 4] = shift(way, 4, way)
                if step == 2 or (step == 1 and kind == way):
                    far_shift[way, step, kind] = shift(way, step, kind)
        for way in range(2):
            keep(block_at(0, way, step), 1 + 2 * step + way)
        if step == 1:
            forward(0)
            forward(1)
    hops = {}
    for kind in range(2):
        self_shift[kind].wait_recv()
        hops[1 - kind, 1, kind] = hop(1, 1 - kind, 1, kind)
    keep(NZ + z, 1)
    for kind in range(2):
        for way in range(2):
            far_shift[way, 2, kind].wait_recv()
            hops[way, 3, kind] = hop(1, way, 3, kind)
    for way in range(2):
        keep(block_at(1, way, 2), 9 + way)
    settle(0)
    settle(1)
    for way in range(2):
        near[way, 4, way].wait_recv()
    keep(block_at(0, 0, 4), 2)
    for step in (1, 3):
        for way in range(2):
            for kind in range(2):
                arriving = far_shift if step == 1 and kind == way else hops
                arriving[way, step, kind].wait_recv()
            keep(block_at(1, way, step), 10 + step + way)
    for way in range(2):
        far_shift[way, 4].wait_recv()
    keep(block_at(1, 0, 4), 15)
    for copy in sent + relays:
        copy.wait_send()
    for copy in keeps:
        copy.wait()
    for copy in own[4:]:
        copy.wait()


def bring(q, k, v, g):
    return pl.pallas_call(
        bring_kernel,
        out_shape=(
            jax.ShapeDtypeStruct((4, HD, LANES), BF16),
            jax.ShapeDtypeStruct((4, HD, LANES), BF16),
            jax.ShapeDtypeStruct((4, LANES, HD), BF16),
            jax.ShapeDtypeStruct((4, LANES, HD), BF16),
            jax.ShapeDtypeStruct((2 * NZ, 2, 2 * ROWS, HD), BF16),
        ),
        in_specs=[HBM] * 4,
        out_specs=(HBM,) * 5,
        scratch_shapes=[
            pltpu.VMEM((4, HD, LANES), BF16),
            pltpu.VMEM((4, HD, LANES), BF16),
            pltpu.VMEM((4, LANES, HD), BF16),
            pltpu.VMEM((4, LANES, HD), BF16),
            pltpu.SemaphoreType.DMA((2, 2)),
            pltpu.VMEM((2, NX, GROUP, HD // NX, ROWS), BF16),
            pltpu.VMEM((2, NX, GROUP, HD // NX, ROWS), BF16),
            pltpu.VMEM((2, 2, HD, ROWS), BF16),
            pltpu.VMEM((2 * NZ, 2, 2 * ROWS, HD), BF16),
            pltpu.VMEM((2, 2 * GROUP, HD // NX, ROWS), BF16),
            pltpu.SemaphoreType.DMA((2, 2)),
            pltpu.SemaphoreType.DMA((4,)),
            pltpu.SemaphoreType.DMA((16,)),
            pltpu.SemaphoreType.DMA((4, 8)),
            pltpu.SemaphoreType.DMA((4, 8)),
            pltpu.SemaphoreType.DMA((2, 5, 2)),
            pltpu.SemaphoreType.DMA((2, 5, 2)),
            pltpu.SemaphoreType.DMA((2, 2, 4, 2)),
            pltpu.SemaphoreType.DMA((2, 2, 4, 2)),
        ],
        compiler_params=pltpu.CompilerParams(
            collective_id=0, has_side_effects=True, vmem_limit_bytes=60 << 20
        ),
        name="bring",
    )(q, k, v, g)


def attend_kernel(
    order_in, docs_in, q_cols_in, g_cols_in, q_rows_in, g_rows_in, kv_in, both_out, dkv,
    order, docs, q_cols, g_cols, q_rows, g_rows, both, dq, kv, scores, key_acc, value_acc, out_acc, tops, sums, shift, dots,
    pos_rows, start_rows, item_list, span_list, in_sem, out_sem,
):
    outer = lax.axis_index("outer")
    chip = lax.div(lax.axis_index("inner"), 2)
    loads = [
        pltpu.make_async_copy(order_in, order, in_sem.at[0]),
        pltpu.make_async_copy(docs_in, docs, in_sem.at[1]),
        pltpu.make_async_copy(q_cols_in, q_cols, in_sem.at[2]),
        pltpu.make_async_copy(kv_in.at[:, 0], kv.at[pl.ds(0, 2 * NZ), 0], in_sem.at[3]),
        pltpu.make_async_copy(kv_in.at[:, 1], kv.at[pl.ds(0, 2 * NZ), 1], in_sem.at[4]),
        pltpu.make_async_copy(g_cols_in, g_cols, in_sem.at[5]),
        pltpu.make_async_copy(q_rows_in, q_rows, in_sem.at[6]),
        pltpu.make_async_copy(g_rows_in, g_rows, in_sem.at[7]),
    ]
    for load in loads:
        load.start()
    kv[2 * NZ] = jnp.zeros((2, 4, SPAN, HD), BF16)
    tops[...] = jnp.full_like(tops, NEG)
    sums[...] = jnp.zeros_like(sums)
    loads[0].wait()
    loads[1].wait()
    doc = docs[...]
    starts = [
        jnp.sum(jnp.where(doc < d, 1.0, 0.0)).astype(jnp.int32) for d in range(1, 4)
    ]

    def start_of(position):
        found = jnp.zeros_like(position)
        for start in starts:
            found = jnp.where(position >= start, jnp.maximum(found, start), found)
        return found

    iota_lanes = lax.rem(lax.broadcasted_iota(jnp.int32, (8, ROWS), 1), SPAN)
    lows = []
    highs = []
    for unit in range(4):
        query_span = order[outer * 32 + chip * 4 + unit]
        lows.append(lax.div(start_of(query_span * SPAN), SPAN))
        highs.append(query_span)
        query_pos = query_span * SPAN + iota_lanes
        pos_rows[unit] = query_pos
        start_rows[unit] = start_of(query_pos)

    counts = tuple(jnp.int32(unit * 128) for unit in range(4))
    for group in range(2):
        stored = lax.rem(outer + 4 - group, 4) * 32

        def note(step, counts):
            for part in range(8):
                slot = step * 8 + part
                span = order[stored + slot]
                entry = span * (2 * SPAN) + (group * 32 + slot)
                new = []
                for unit in range(4):
                    span_list[counts[unit]] = entry
                    allowed = (span >= lows[unit]) & (span <= highs[unit])
                    new.append(counts[unit] + jnp.where(allowed, 1, 0))
                counts = tuple(new)
            nothing = jnp.zeros((8, SPAN, HD), F32)
            rows = pl.ds((group * 4 + step) * 8, 8)
            key_acc[rows] = nothing
            value_acc[rows] = nothing
            flat = pl.ds(pl.multiple_of(step * 32, 32), 32)
            for unit in range(2 * group, 2 * group + 2):
                out_acc[unit, flat, :] = jnp.zeros((32, LANES), F32)
                dq[unit, flat, :] = jnp.zeros((32, LANES), F32)
            return counts

        counts = lax.fori_loop(0, 4, note, counts)
    items = jnp.int32(0)
    for unit in range(4):
        for extra in range(ITEM):
            span_list[counts[unit] + extra] = 2 * FAR + SLOTS
        for chunk in range(SLOTS // ITEM):
            item_list[items + chunk] = unit * 128 + chunk * ITEM
        items = items + lax.div(counts[unit] - unit * 128 + ITEM - 1, ITEM)
    blank = 3 * 128 + 72
    for extra in range(ITEM):
        span_list[blank + extra] = 2 * FAR + SLOTS
    for extra in range(4):
        item_list[items + extra] = blank
    steps = lax.div(items + 3, 4)

    iota_keys = (
        lax.broadcasted_iota(jnp.int32, (8, 8, ROWS), 0) * 8
        + lax.broadcasted_iota(jnp.int32, (8, 8, ROWS), 1)
    )

    def entries(item):
        first = item_list[item]
        found = [span_list[first + part] for part in range(ITEM)]
        slots = [lax.rem(entry, 2 * SPAN) for entry in found]
        return lax.div(first, 128), slots, [lax.div(a - b, 2) for a, b in zip(found, slots)]

    def spans(slots, kind):
        parts = []
        for slot in slots:
            parts.append(kv[lax.div(slot, 4), kind, lax.rem(slot, 4)])
        return jnp.concatenate(parts, axis=0)

    sides = [pl.ds(side * 256, 256) for side in range(2)]
    loads[2].wait()
    loads[3].wait()

    @functools.partial(lax.fori_loop, 0, steps, init_val=0)
    def _(step, _):
        results = []
        for item in [4 * step + part for part in range(4)]:
            unit, slots, bases = entries(item)
            keys = spans(slots, 0)
            biases = []
            for base in bases:
                allowed = (iota_keys <= (pos_rows[unit] - base)[None]) & (
                    iota_keys >= (start_rows[unit] - base)[None]
                )
                biases.append(jnp.where(allowed, 0.0, NEG).reshape(SPAN, ROWS))
            bias = jnp.concatenate(biases, axis=0)
            bias = jnp.concatenate([bias, bias], axis=1)
            for lanes in sides:
                tile = jnp.dot(keys, q_cols[unit, :, lanes], preferred_element_type=F32)
                tile = tile * (SCALE * LOG2E) + bias
                scores[item, :, lanes] = tile
                results.append((unit, lanes, jnp.max(tile.reshape(32, 8, 256), axis=0)))
        for unit, lanes, top in results:
            tops[unit, :, lanes] = jnp.maximum(tops[unit, :, lanes], top)
        return 0

    for unit in range(4):
        shift[unit] = jnp.broadcast_to(jnp.max(tops[unit], axis=0, keepdims=True), (8, LANES))
    loads[4].wait()

    @functools.partial(lax.fori_loop, 0, steps, init_val=0)
    def _(step, _):
        results = []
        for item in [4 * step + part for part in range(4)]:
            unit, slots, _ = entries(item)
            values_t = spans(slots, 1).T
            for lanes in sides:
                logits = scores[item, :, lanes].reshape(32, 8, 256)
                probs = jnp.exp2(logits - shift[unit, :, lanes][None])
                part = jnp.dot(
                    values_t, probs.reshape(256, 256).astype(BF16), preferred_element_type=F32
                )
                results.append((unit, lanes, jnp.sum(probs, axis=0), part))
        for unit, lanes, total, part in results:
            sums[unit, :, lanes] += total
            out_acc[unit, :, lanes] += part
        return 0

    for load in loads[5:]:
        load.wait()
    for unit in range(4):
        row_sum = jnp.sum(sums[unit], axis=0, keepdims=True)
        out = (out_acc[unit] * (1.0 / row_sum)).astype(BF16)
        both[unit, 0] = out
        row_dot = jnp.sum(
            out.astype(F32) * g_cols[unit].astype(F32), axis=0, keepdims=True
        )
        dots[unit] = jnp.broadcast_to(row_dot, (8, LANES))
        shift[unit] = shift[unit] + jnp.log(row_sum) * LOG2E

    @functools.partial(lax.fori_loop, 0, steps, init_val=0)
    def _(step, _):
        results = []
        for item in [4 * step + part for part in range(4)]:
            unit, slots, _ = entries(item)
            keys_t = spans(slots, 0).T
            values = spans(slots, 1)
            probs_b = []
            score_grads = []
            for lanes in sides:
                logits = scores[item, :, lanes].reshape(32, 8, 256)
                probs = jnp.exp2(logits - shift[unit, :, lanes][None])
                steep = jnp.dot(values, g_cols[unit, :, lanes], preferred_element_type=F32)
                steep = probs * (steep.reshape(32, 8, 256) - dots[unit, :, lanes][None])
                probs_b.append(probs.reshape(256, 256).astype(BF16))
                score_grads.append(steep.reshape(256, 256).astype(BF16))
            probs_b = jnp.concatenate(probs_b, axis=1)
            score_grads = jnp.concatenate(score_grads, axis=1)
            to_values = jnp.dot(probs_b, g_rows[unit], preferred_element_type=F32)
            to_keys = jnp.dot(score_grads, q_rows[unit], preferred_element_type=F32)
            to_query = jnp.dot(keys_t, score_grads, preferred_element_type=F32)
            results.append((slots, unit, to_values, to_keys, to_query))
        for slots, unit, to_values, to_keys, to_query in results:
            dq[unit] += to_query
            for acc, part in ((key_acc, to_keys), (value_acc, to_values)):
                sums_of = [
                    acc[slot] + part[index * SPAN : (index + 1) * SPAN]
                    for index, slot in enumerate(slots)
                ]
                for slot, total in zip(slots, sums_of):
                    acc[slot] = total
        return 0

    for unit in range(4):
        both[unit, 1] = (dq[unit] * SCALE).astype(BF16)
    both_store = pltpu.make_async_copy(both, both_out, out_sem.at[2 * NZ])
    both_store.start()
    stores = [both_store]
    for index in range(2 * NZ):
        for part in range(4):
            kv[index, 0, part] = (key_acc[index * 4 + part] * SCALE).astype(BF16)
            kv[index, 1, part] = value_acc[index * 4 + part].astype(BF16)
        store = pltpu.make_async_copy(kv.at[index], dkv.at[index], out_sem.at[index])
        store.start()
        stores.append(store)
    for store in stores:
        store.wait()


def attend(order, docs, q_cols, g_cols, q_rows, g_rows, kv):
    return pl.pallas_call(
        attend_kernel,
        out_shape=(
            jax.ShapeDtypeStruct((4, 2, HD, LANES), BF16),
            jax.ShapeDtypeStruct((2 * NZ, 2, 4, SPAN, HD), BF16),
        ),
        in_specs=[HBM] * 7,
        out_specs=(HBM,) * 2,
        scratch_shapes=[
            pltpu.SMEM((2 * SLOTS,), jnp.int32),
            pltpu.VMEM((SLOTS, ROWS), jnp.int32),
            pltpu.VMEM((4, HD, LANES), BF16),
            pltpu.VMEM((4, HD, LANES), BF16),
            pltpu.VMEM((4, LANES, HD), BF16),
            pltpu.VMEM((4, LANES, HD), BF16),
            pltpu.VMEM((4, 2, HD, LANES), BF16),
            pltpu.VMEM((4, HD, LANES), F32),
            pltpu.VMEM((2 * NZ + 1, 2, 4, SPAN, HD), BF16),
            pltpu.VMEM((4 * SLOTS // ITEM, ITEM * SPAN, LANES), F32),
            pltpu.VMEM((SLOTS + 1, SPAN, HD), F32),
            pltpu.VMEM((SLOTS + 1, SPAN, HD), F32),
            pltpu.VMEM((4, HD, LANES), F32),
            pltpu.VMEM((4, 8, LANES), F32),
            pltpu.VMEM((4, 8, LANES), F32),
            pltpu.VMEM((4, 8, LANES), F32),
            pltpu.VMEM((4, 8, LANES), F32),
            pltpu.VMEM((4, 8, ROWS), jnp.int32),
            pltpu.VMEM((4, 8, ROWS), jnp.int32),
            pltpu.SMEM((80,), jnp.int32),
            pltpu.SMEM((512,), jnp.int32),
            pltpu.SemaphoreType.DMA((8,)),
            pltpu.SemaphoreType.DMA((2 * NZ + 1,)),
        ],
        compiler_params=pltpu.CompilerParams(vmem_limit_bytes=60 << 20),
        cost_estimate=pl.CostEstimate(
            flops=6 * 2 * 2048 * 2048 * HD, bytes_accessed=12 << 20, transcendentals=2048 * 2048
        ),
        name="attend",
    )(order, docs, q_cols, g_cols, q_rows, g_rows, kv)


def return_kernel(
    both_in, dkv, both_out, dkv_out,
    both, terms, both_rows, order, landed, landed_rows, final, pair_send, pair_recv, own_sem, l_send, l_recv, r_send, r_recv,
):
    x, y, z, core = place()
    sibling = where_is(x, y, z, 1 - core)
    up = where_is(x, y, lax.rem(z + 1, NZ), core)
    down = where_is(x, y, lax.rem(z + NZ - 1, NZ), core)
    later = where_is(x, lax.rem(y + 1, NY), z, core)
    earlier = where_is(x, lax.rem(y + NY - 1, NY), z, core)
    loads = [
        pltpu.make_async_copy(both_in, both, own_sem.at[5]),
        pltpu.make_async_copy(dkv, terms, own_sem.at[4]),
    ]
    for load in loads:
        load.start()
    up_z, down_z = lax.rem(z + 1, NZ), lax.rem(z + NZ - 1, NZ)
    later_y, earlier_y = lax.rem(y + 1, NY), lax.rem(y + NY - 1, NY)
    corners = (where_is(x, earlier_y, up_z, core), where_is(x, earlier_y, down_z, core))
    behind = [where_is(x, later_y, up_z, core), where_is(x, later_y, down_z, core)]
    across = [
        where_is(x, y, up_z, 1 - core),
        where_is(x, y, down_z, 1 - core),
        where_is(x, earlier_y, z, 1 - core),
    ]
    greet(
        [sibling, up, down, later, earlier, *corners, *behind, *across]
        + [where_is(x, later_y, z, 1 - core)]
    )

    ways = (up, down)
    sent = []

    def at(group, distance, way):
        return group * NZ + lax.rem(z + NZ + distance * (-1 if way else 1), NZ)

    def ship(src, index, partner):
        copy = send(src, landed.at[index], l_send.at[index], l_recv.at[index], partner)
        sent.append(copy)
        return copy

    def add(block, kind, *indices):
        total = terms[block, kind].astype(F32)
        for index in indices:
            total = total + landed[index].astype(F32)
        terms[block, kind] = total.astype(BF16)

    mine = pl.ds(pl.multiple_of(core * ROWS, ROWS), ROWS)
    other = pl.ds(pl.multiple_of((1 - core) * ROWS, ROWS), ROWS)

    def deliver(block, kind, index, straight, crossed):
        copies = []
        for half, rows, partner in ((0, mine, straight), (1, other, crossed)):
            copy = send(
                terms.at[block, kind, rows], landed_rows.at[half, index],
                r_send.at[half, index], r_recv.at[half, index], partner,
            )
            sent.append(copy)
            copies.append(copy)
        return copies

    flying = {}
    for way in range(2):
        flying["s", 1, way, way] = ship(dkv.at[at(0, 4, 0), way], 16 + way, ways[way])
    for step, distance in ((0, 3), (1, 1)):
        for kind in range(2):
            for way in range(2):
                if step == 1 and kind == way:
                    continue
                flying["z", step, way, kind] = ship(
                    dkv.at[at(1, distance, way), kind], step * 4 + way * 2 + kind, ways[way]
                )
        if step == 0:
            for kind in range(2):
                flying["y", 4, kind] = ship(dkv.at[at(1, 4, 0), kind], 8 + kind, corners[kind])
    swaps = []
    own = []

    def turn(block, half):
        stacked = both[2 * block + half].reshape(2 * HD, LANES)
        rows = lax.dot_general(
            order[...], stacked, (((1,), (1,)), ((), ())), preferred_element_type=F32
        ).astype(BF16)
        for kind in range(2):
            both_rows[block, kind, half * LANES : (half + 1) * LANES, :] = rows[
                :, kind * HD : (kind + 1) * HD
            ]

    def swap():
        swaps.append(
            send(
                both_rows.at[1 - core], both_out.at[core], pair_send.at[0], pair_recv.at[0], sibling
            )
        )

    def stay():
        copy = pltpu.make_async_copy(both_rows.at[core], both_out.at[core], own_sem.at[0])
        copy.start()
        own.append(copy)

    row = lax.broadcasted_iota(jnp.int32, (LANES, LANES), 0)
    lane = lax.broadcasted_iota(jnp.int32, (LANES, LANES), 1)
    from_lane = lax.rem(row, GROUP) * SPAN + lax.div(row, GROUP)
    order[...] = jnp.where(lane == from_lane, 1.0, 0.0).astype(BF16)
    loads[1].wait()
    for kind in range(2):
        for way in range(2):
            flying["z", 0, way, kind].wait_recv()
            block = at(1, 2, way)
            add(block, kind, way * 2 + kind)
            flying["y", 2, way, kind] = ship(
                terms.at[block, kind], 10 + way * 2 + kind, earlier
            )
    for way in range(2):
        flying["y", 1, way] = ship(dkv.at[at(1, 1, way), way], 30 + way, earlier)
    for way in range(2):
        kind = 1 - way
        flying["s", 2, way, kind] = ship(
            terms.at[at(0, 3, way), kind], 18 + way * 2 + kind, ways[way]
        )
    loads[0].wait()
    turn(1 - core, 0)
    for kind in range(2):
        swaps.append(
            send(
                dkv.at[z, kind, other], landed_rows.at[1, 6 + kind],
                r_send.at[1, 6 + kind], r_recv.at[1, 6 + kind], sibling,
            )
        )
    for way in range(2):
        flying["s", 1, way, way].wait_recv()
        flying["y", 4, way].wait_recv()
        add(at(0, 3, way), way, 16 + way, 8 + way)
        flying["s", 2, way, way] = ship(
            terms.at[at(0, 3, way), way], 18 + way * 2 + way, ways[way]
        )
    for kind in range(2):
        way = 1 - kind
        flying["z", 1, way, kind].wait_recv()
        add(NZ + z, kind, 4 + way * 2 + kind)
        flying["y", 0, kind] = deliver(NZ + z, kind, kind, earlier, across[2])
    turn(1 - core, 1)
    swap()
    for step in (3, 4):
        for turn_of in range(2):
            for way in range(2):
                kind = turn_of if way else 1 - turn_of
                flying["s", step - 1, way, kind].wait_recv()
                indices = [18 + (step - 3) * 4 + way * 2 + kind]
                if step == 3:
                    flying["y", 2, way, kind].wait_recv()
                    indices.append(10 + way * 2 + kind)
                elif kind == way:
                    flying["y", 1, way].wait_recv()
                    indices.append(30 + way)
                block = at(0, 5 - step, way)
                add(block, kind, *indices)
                if step == 3:
                    flying["s", step, way, kind] = ship(
                        terms.at[block, kind], 22 + way * 2 + kind, ways[way]
                    )
                else:
                    flying["s", step, way, kind] = deliver(
                        block, kind, 2 + way * 2 + kind, ways[way], across[way]
                    )
        turn(core, step - 3)
    stay()
    for kind in range(2):
        for half in range(2):
            flying["y", 0, kind][half].wait_recv()
            for way in range(2):
                flying["s", 4, way, kind][half].wait_recv()
            if half:
                swaps[kind].wait_recv()
                total = landed_rows[1, 6 + kind].astype(F32)
            else:
                total = terms[z, kind, mine].astype(F32)
            for index in (kind, 2 + kind, 4 + kind):
                total = total + landed_rows[half, index].astype(F32)
            final[kind, half] = total
        for half in range(2):
            copy = pltpu.make_async_copy(
                final.at[kind, half], dkv_out.at[kind, core if half == 0 else 1 - core],
                own_sem.at[2 + (0, 5)[half] + kind],
            )
            copy.start()
            own.append(copy)
    for copy in sent:
        copy.wait_send()
    for copy in swaps[:2]:
        copy.wait_send()
    swaps[2].wait()
    for copy in own:
        copy.wait()


def give_back(both, dkv):
    return pl.pallas_call(
        return_kernel,
        out_shape=(
            jax.ShapeDtypeStruct((2, 2, ROWS * GROUP, HD), BF16),
            jax.ShapeDtypeStruct((2, 2, ROWS, HD), F32),
        ),
        in_specs=[HBM] * 2,
        out_specs=(HBM,) * 2,
        scratch_shapes=[
            pltpu.VMEM((4, 2, HD, LANES), BF16),
            pltpu.VMEM((2 * NZ, 2, 2 * ROWS, HD), BF16),
            pltpu.VMEM((2, 2, ROWS * GROUP, HD), BF16),
            pltpu.VMEM((LANES, LANES), BF16),
            pltpu.VMEM((32, 2 * ROWS, HD), BF16),
            pltpu.VMEM((2, 8, ROWS, HD), BF16),
            pltpu.VMEM((2, 2, ROWS, HD), F32),
            pltpu.SemaphoreType.DMA((1,)),
            pltpu.SemaphoreType.DMA((1,)),
            pltpu.SemaphoreType.DMA((9,)),
            pltpu.SemaphoreType.DMA((32,)),
            pltpu.SemaphoreType.DMA((32,)),
            pltpu.SemaphoreType.DMA((2, 8)),
            pltpu.SemaphoreType.DMA((2, 8)),
        ],
        compiler_params=pltpu.CompilerParams(
            collective_id=1, has_side_effects=True, vmem_limit_bytes=60 << 20
        ),
        name="give_back",
    )(both, dkv)


def finish_kernel(
    both, dkv, attn_out, dq_out, dk_out, dv_out, halves, attn, dq, parts, dk, dv, sem
):
    loads = [pltpu.make_async_copy(dkv, parts, sem.at[0])]
    for kind in range(2):
        loads.append(
            pltpu.make_async_copy(both.at[:, kind], halves.at[:, kind], sem.at[1 + kind])
        )
    for load in loads:
        load.start()
    stores = []
    loads[0].wait()
    for kind, (rows, dst) in enumerate(((dk, dk_out), (dv, dv_out))):
        for half in range(2):
            rows[pl.ds(half, ROWS, stride=2), :] = parts[kind, half]
        store = pltpu.make_async_copy(rows, dst, sem.at[3 + kind])
        store.start()
        stores.append(store)
    for kind, (joined, dst) in ((1, (dq, dq_out)), (0, (attn, attn_out))):
        loads[1 + kind].wait()
        pair = [halves[half, kind].astype(F32).reshape(ROWS, GROUP, HD) for half in range(2)]
        joined[...] = jnp.concatenate(pair, axis=1).astype(joined.dtype)
        store = pltpu.make_async_copy(joined, dst, sem.at[5 + kind])
        store.start()
        stores.append(store)
    for store in stores:
        store.wait()


def finish(both, dkv):
    return pl.pallas_call(
        finish_kernel,
        out_shape=(
            jax.ShapeDtypeStruct((ROWS, 2 * GROUP, HD), BF16),
            jax.ShapeDtypeStruct((ROWS, 2 * GROUP, HD), F32),
            jax.ShapeDtypeStruct((2 * ROWS, HD), F32),
            jax.ShapeDtypeStruct((2 * ROWS, HD), F32),
        ),
        in_specs=[HBM] * 2,
        out_specs=(HBM,) * 4,
        scratch_shapes=[
            pltpu.VMEM((2, 2, ROWS * GROUP, HD), BF16),
            pltpu.VMEM((ROWS, 2 * GROUP, HD), BF16),
            pltpu.VMEM((ROWS, 2 * GROUP, HD), F32),
            pltpu.VMEM((2, 2, ROWS, HD), F32),
            pltpu.VMEM((2 * ROWS, HD), F32),
            pltpu.VMEM((2 * ROWS, HD), F32),
            pltpu.SemaphoreType.DMA((7,)),
        ],
        compiler_params=pltpu.CompilerParams(vmem_limit_bytes=60 << 20),
        cost_estimate=pl.CostEstimate(flops=0, bytes_accessed=4 << 20, transcendentals=0),
        name="finish",
    )(both, dkv)


def local(queries, keys, values, grad_out, span_order, doc_ids):
    turned = [jnp.transpose(a, (1, 2, 0)) for a in (queries, keys, values, grad_out)]
    q_cols, g_cols, q_rows, g_rows, kv = bring(*turned)
    kv = kv.reshape(2 * NZ, 2, 4, SPAN, HD)
    both, dkv = attend(
        span_order, doc_ids.reshape(SLOTS, ROWS), q_cols, g_cols, q_rows, g_rows, kv
    )
    both, dkv = give_back(both, dkv.reshape(2 * NZ, 2, 2 * ROWS, HD))
    attn, dq, dk, dv = finish(both, dkv)
    return (attn, dq, dk.reshape(ROWS, 2, HD), dv.reshape(ROWS, 2, HD))


def solution(mesh):
    entry = P(("outer", "inner"), None, "head")
    leave = P(("outer", "inner"), "head", None)
    return jax.shard_map(
        local,
        mesh=mesh,
        in_specs=(entry, entry, entry, entry, P(), P()),
        out_specs=(leave, leave, leave, leave),
        check_vma=False,
    )
```

```python
import functools
import math

import jax
import jax.numpy as jnp
from jax import lax
from jax.experimental import pallas as pl
from jax.experimental.pallas import tpu as pltpu
from jax.sharding import PartitionSpec as P

MESH = pl.DeviceIdType.MESH
HBM = pl.BlockSpec(memory_space=pltpu.HBM)
NEG = -1e30
FAR = 1 << 24
NX = 4
NY = 4
NZ = 8
HD = 128
ROWS = 128
SPAN = 64
GROUP = 8
SLOTS = 64
LANES = GROUP * SPAN
SCALE = 1.0 / math.sqrt(HD)
LOG2E = math.log2(math.e)
ITEM = 4
BF16 = jnp.bfloat16
F32 = jnp.float32


def place():
    inner = lax.axis_index("inner")
    return (
        lax.axis_index("head"),
        lax.axis_index("outer"),
        lax.div(inner, 2),
        lax.rem(inner, 2),
    )


def where_is(x, y, z, core):
    return {"head": x, "outer": y, "inner": z * 2 + core}


def greet(partners):
    barrier = pltpu.get_barrier_semaphore()
    for partner in partners:
        pl.semaphore_signal(barrier, inc=1, device_id=partner, device_id_type=MESH)
    pl.semaphore_wait(barrier, len(partners))


def send(src, dst, send_sem, recv_sem, partner):
    copy = pltpu.make_async_remote_copy(
        src_ref=src,
        dst_ref=dst,
        send_sem=send_sem,
        recv_sem=recv_sem,
        device_id=partner,
        device_id_type=MESH,
    )
    copy.start()
    return copy


def bring_kernel(
    q, k, v, g, q_cols_out, g_cols_out, q_rows_out, g_rows_out, kv_out,
    q_cols, g_cols, q_rows, g_rows, out_sem, q_in, g_in, kv_in, ring_kv, own_sem, keep_sem, x_send, x_recv, y_send, y_recv, z_send, z_recv,
):
    x, y, z, core = place()
    peers = [(dx, dc) for dx in range(NX) for dc in range(2) if (dx, dc) != (0, 0)]

    def peer(dx, dc):
        return where_is(lax.rem(x + dx, NX), y, z, lax.rem(core + dc, 2))

    up = where_is(x, y, lax.rem(z + 1, NZ), core)
    down = where_is(x, y, lax.rem(z + NZ - 1, NZ), core)
    later = where_is(x, lax.rem(y + 1, NY), z, core)
    earlier = where_is(x, lax.rem(y + NY - 1, NY), z, core)
    up_z, down_z = lax.rem(z + 1, NZ), lax.rem(z + NZ - 1, NZ)
    later_y, earlier_y = lax.rem(y + 1, NY), lax.rem(y + NY - 1, NY)
    corners = (where_is(x, later_y, up_z, core), where_is(x, later_y, down_z, core))
    behind = [where_is(x, earlier_y, up_z, core), where_is(x, earlier_y, down_z, core)]
    greet([peer(*p) for p in peers] + [up, down, later, earlier, *corners, *behind])

    here = pl.ds(pl.multiple_of(x * 32, 32), 32)
    copies = []
    own = []
    for index, (dx, dc) in enumerate([(0, 0)] + peers):
        head = lax.rem(x + dx, NX) * 2 + lax.rem(core + dc, 2)
        for kind, src in enumerate((k, v)):
            dst = kv_in.at[kind, core, here]
            if index == 0:
                copy = pltpu.make_async_copy(src.at[head], dst, own_sem.at[kind])
                copy.start()
                own.append(copy)
            else:
                copies.append(
                    send(src.at[head], dst, x_send.at[kind, index], x_recv.at[kind, index], peer(dx, dc))
                )
    own[0].wait()
    own[1].wait()
    for copy in copies:
        copy.wait()
    for kind in range(2):
        for block in range(2):
            ring_kv[z, kind, block * ROWS : (block + 1) * ROWS, :] = (
                kv_in[kind, block].astype(F32).T.astype(BF16)
            )
    keeps = []
    sent = []
    ways = (up, down)

    def block_at(group, way, step):
        return group * NZ + lax.rem(z + NZ + step * (1 if way else -1), NZ)

    def keep(block, index):
        copy = pltpu.make_async_copy(ring_kv.at[block], kv_out.at[block], keep_sem.at[index])
        copy.start()
        keeps.append(copy)

    def hop(group, way, step, kind):
        block = block_at(group, way, step - 1)
        copy = send(
            ring_kv.at[block, kind], ring_kv.at[block, kind],
            z_send.at[group, way, step - 1, kind], z_recv.at[group, way, step - 1, kind],
            ways[way],
        )
        sent.append(copy)
        return copy

    def shift(way, step, kind):
        block = block_at(0, way, min(step, 3))
        copy = send(
            ring_kv.at[block, kind], ring_kv.at[NZ + block, kind],
            y_send.at[way, step, kind], y_recv.at[way, step, kind],
            corners[way] if step == 4 else later,
        )
        sent.append(copy)
        return copy

    def settle(kind):
        src, cols, rows = ((q_in, q_cols, q_rows), (g_in, g_cols, g_rows))[kind]
        own[2 + kind].wait()
        for copy in wide[kind]:
            copy.wait()
        low = lax.broadcasted_iota(jnp.int32, (HD, ROWS), 1) < SPAN

        @pl.loop(0, 8)
        def _(index):
            block = lax.div(index, 4)
            pair = lax.rem(index, 4)
            lanes = pl.ds(pl.multiple_of(pair * ROWS, ROWS), ROWS)
            first, second = [
                jnp.concatenate([src[block, a, 2 * pair + b] for a in range(NX)], axis=0).astype(F32)
                for b in range(2)
            ]
            halves = (
                jnp.where(low, first, pltpu.roll(second, SPAN, 1)),
                jnp.where(low, pltpu.roll(first, SPAN, 1), second),
            )
            for half in range(2):
                cols[2 * block + half, :, lanes] = halves[half].astype(BF16)
                rows[2 * block + half, lanes, :] = halves[half].T.astype(BF16)

        outs = ((q_cols_out, q_rows_out), (g_cols_out, g_rows_out))[kind]
        for index, (src, dst) in enumerate(zip((cols, rows), outs)):
            copy = pltpu.make_async_copy(src, dst, out_sem.at[kind, index])
            copy.start()
            own.append(copy)

    near = {}
    self_shift = {}
    for kind in range(2):
        for way in range(2):
            near[way, 1, kind] = hop(0, way, 1, kind)
        self_shift[kind] = shift(0, 0, kind)
    keep(z, 0)
    heads = pl.ds((x * 2 + core) * GROUP, GROUP)
    for kind, (src, dst) in enumerate(((q, q_in), (g, g_in))):
        copy = pltpu.make_async_copy(
            src.at[heads], dst.at[core, x], own_sem.at[2 + kind]
        )
        copy.start()
        own.append(copy)
    wide = ([], [])

    def spread(kind, *offsets):
        src, dst = ((q, q_in), (g, g_in))[kind]
        for index, (dx, dc) in enumerate(peers):
            if dx not in offsets:
                continue
            head = lax.rem(x + dx, NX) * 2 + lax.rem(core + dc, 2)
            wide[kind].append(
                send(
                    src.at[pl.ds(head * GROUP, GROUP)],
                    dst.at[core, x],
                    x_send.at[2 + kind, index],
                    x_recv.at[2 + kind, index],
                    peer(dx, dc),
                )
            )

    spread(0, 2)
    spread(0, 0, 1)
    far_shift = {}
    for step in range(1, 4):
        for kind in range(2):
            for way in range(2):
                near[way, step, kind].wait_recv()
                if step < 3 or kind == way:
                    near[way, step + 1, kind] = hop(0, way, step + 1, kind)
                if step == 3 and kind == way:
                    far_shift[way, 4] = shift(way, 4, way)
                if step == 2 or (step == 1 and kind == way):
                    far_shift[way, step, kind] = shift(way, step, kind)
        for way in range(2):
            keep(block_at(0, way, step), 1 + 2 * step + way)
        if step == 1:
            spread(0, 3)
            spread(1, 2)
        elif step == 2:
            spread(1, 0, 1, 3)
    hops = {}
    for kind in range(2):
        self_shift[kind].wait_recv()
        hops[1 - kind, 1, kind] = hop(1, 1 - kind, 1, kind)
    keep(NZ + z, 1)
    for kind in range(2):
        for way in range(2):
            far_shift[way, 2, kind].wait_recv()
            hops[way, 3, kind] = hop(1, way, 3, kind)
    for way in range(2):
        keep(block_at(1, way, 2), 9 + way)
    settle(0)
    settle(1)
    for way in range(2):
        near[way, 4, way].wait_recv()
    keep(block_at(0, 0, 4), 2)
    for step in (1, 3):
        for way in range(2):
            for kind in range(2):
                arriving = far_shift if step == 1 and kind == way else hops
                arriving[way, step, kind].wait_recv()
            keep(block_at(1, way, step), 10 + step + way)
    for way in range(2):
        far_shift[way, 4].wait_recv()
    keep(block_at(1, 0, 4), 15)
    for copy in sent:
        copy.wait_send()
    for copy in keeps:
        copy.wait()
    for copy in own[4:]:
        copy.wait()


def bring(q, k, v, g):
    return pl.pallas_call(
        bring_kernel,
        out_shape=(
            jax.ShapeDtypeStruct((4, HD, LANES), BF16),
            jax.ShapeDtypeStruct((4, HD, LANES), BF16),
            jax.ShapeDtypeStruct((4, LANES, HD), BF16),
            jax.ShapeDtypeStruct((4, LANES, HD), BF16),
            jax.ShapeDtypeStruct((2 * NZ, 2, 2 * ROWS, HD), BF16),
        ),
        in_specs=[HBM] * 4,
        out_specs=(HBM,) * 5,
        scratch_shapes=[
            pltpu.VMEM((4, HD, LANES), BF16),
            pltpu.VMEM((4, HD, LANES), BF16),
            pltpu.VMEM((4, LANES, HD), BF16),
            pltpu.VMEM((4, LANES, HD), BF16),
            pltpu.SemaphoreType.DMA((2, 2)),
            pltpu.VMEM((2, NX, GROUP, HD // NX, ROWS), BF16),
            pltpu.VMEM((2, NX, GROUP, HD // NX, ROWS), BF16),
            pltpu.VMEM((2, 2, HD, ROWS), BF16),
            pltpu.VMEM((2 * NZ, 2, 2 * ROWS, HD), BF16),
            pltpu.SemaphoreType.DMA((4,)),
            pltpu.SemaphoreType.DMA((16,)),
            pltpu.SemaphoreType.DMA((4, 8)),
            pltpu.SemaphoreType.DMA((4, 8)),
            pltpu.SemaphoreType.DMA((2, 5, 2)),
            pltpu.SemaphoreType.DMA((2, 5, 2)),
            pltpu.SemaphoreType.DMA((2, 2, 4, 2)),
            pltpu.SemaphoreType.DMA((2, 2, 4, 2)),
        ],
        compiler_params=pltpu.CompilerParams(
            collective_id=0, has_side_effects=True, vmem_limit_bytes=60 << 20
        ),
        name="bring",
    )(q, k, v, g)


def attend_kernel(
    order_in, docs_in, q_cols_in, g_cols_in, q_rows_in, g_rows_in, kv_in, both_out, dkv,
    order, docs, q_cols, g_cols, q_rows, g_rows, both, dq, kv, scores, key_acc, value_acc, out_acc, tops, sums, shift, dots,
    pos_rows, start_rows, item_list, span_list, in_sem, out_sem,
):
    outer = lax.axis_index("outer")
    chip = lax.div(lax.axis_index("inner"), 2)
    loads = [
        pltpu.make_async_copy(order_in, order, in_sem.at[0]),
        pltpu.make_async_copy(docs_in, docs, in_sem.at[1]),
        pltpu.make_async_copy(q_cols_in, q_cols, in_sem.at[2]),
        pltpu.make_async_copy(kv_in.at[:, 0], kv.at[pl.ds(0, 2 * NZ), 0], in_sem.at[3]),
        pltpu.make_async_copy(kv_in.at[:, 1], kv.at[pl.ds(0, 2 * NZ), 1], in_sem.at[4]),
        pltpu.make_async_copy(g_cols_in, g_cols, in_sem.at[5]),
        pltpu.make_async_copy(q_rows_in, q_rows, in_sem.at[6]),
        pltpu.make_async_copy(g_rows_in, g_rows, in_sem.at[7]),
    ]
    for load in loads:
        load.start()
    kv[2 * NZ] = jnp.zeros((2, 4, SPAN, HD), BF16)
    tops[...] = jnp.full_like(tops, NEG)
    sums[...] = jnp.zeros_like(sums)
    loads[0].wait()
    loads[1].wait()
    doc = docs[...]
    starts = [
        jnp.sum(jnp.where(doc < d, 1.0, 0.0)).astype(jnp.int32) for d in range(1, 4)
    ]

    def start_of(position):
        found = jnp.zeros_like(position)
        for start in starts:
            found = jnp.where(position >= start, jnp.maximum(found, start), found)
        return found

    iota_lanes = lax.rem(lax.broadcasted_iota(jnp.int32, (8, ROWS), 1), SPAN)
    lows = []
    highs = []
    for unit in range(4):
        query_span = order[outer * 32 + chip * 4 + unit]
        lows.append(lax.div(start_of(query_span * SPAN), SPAN))
        highs.append(query_span)
        query_pos = query_span * SPAN + iota_lanes
        pos_rows[unit] = query_pos
        start_rows[unit] = start_of(query_pos)

    counts = tuple(jnp.int32(unit * 128) for unit in range(4))
    for group in range(2):
        stored = lax.rem(outer + 4 - group, 4) * 32

        def note(step, counts):
            for part in range(8):
                slot = step * 8 + part
                span = order[stored + slot]
                entry = span * (2 * SPAN) + (group * 32 + slot)
                new = []
                for unit in range(4):
                    span_list[counts[unit]] = entry
                    allowed = (span >= lows[unit]) & (span <= highs[unit])
                    new.append(counts[unit] + jnp.where(allowed, 1, 0))
                counts = tuple(new)
            nothing = jnp.zeros((8, SPAN, HD), F32)
            rows = pl.ds((group * 4 + step) * 8, 8)
            key_acc[rows] = nothing
            value_acc[rows] = nothing
            flat = pl.ds(pl.multiple_of(step * 32, 32), 32)
            for unit in range(2 * group, 2 * group + 2):
                out_acc[unit, flat, :] = jnp.zeros((32, LANES), F32)
                dq[unit, flat, :] = jnp.zeros((32, LANES), F32)
            return counts

        counts = lax.fori_loop(0, 4, note, counts)
    items = jnp.int32(0)
    for unit in range(4):
        for extra in range(ITEM):
            span_list[counts[unit] + extra] = 2 * FAR + SLOTS
        for chunk in range(SLOTS // ITEM):
            item_list[items + chunk] = unit * 128 + chunk * ITEM
        items = items + lax.div(counts[unit] - unit * 128 + ITEM - 1, ITEM)
    blank = 3 * 128 + 72
    for extra in range(ITEM):
        span_list[blank + extra] = 2 * FAR + SLOTS
    for extra in range(4):
        item_list[items + extra] = blank
    steps = lax.div(items + 3, 4)

    iota_keys = (
        lax.broadcasted_iota(jnp.int32, (8, 8, ROWS), 0) * 8
        + lax.broadcasted_iota(jnp.int32, (8, 8, ROWS), 1)
    )

    def entries(item):
        first = item_list[item]
        found = [span_list[first + part] for part in range(ITEM)]
        slots = [lax.rem(entry, 2 * SPAN) for entry in found]
        return lax.div(first, 128), slots, [lax.div(a - b, 2) for a, b in zip(found, slots)]

    def spans(slots, kind):
        parts = []
        for slot in slots:
            parts.append(kv[lax.div(slot, 4), kind, lax.rem(slot, 4)])
        return jnp.concatenate(parts, axis=0)

    sides = [pl.ds(side * 256, 256) for side in range(2)]
    loads[2].wait()
    loads[3].wait()

    @functools.partial(lax.fori_loop, 0, steps, init_val=0)
    def _(step, _):
        results = []
        for item in [4 * step + part for part in range(4)]:
            unit, slots, bases = entries(item)
            keys = spans(slots, 0)
            biases = []
            for base in bases:
                allowed = (iota_keys <= (pos_rows[unit] - base)[None]) & (
                    iota_keys >= (start_rows[unit] - base)[None]
                )
                biases.append(jnp.where(allowed, 0.0, NEG).reshape(SPAN, ROWS))
            bias = jnp.concatenate(biases, axis=0)
            bias = jnp.concatenate([bias, bias], axis=1)
            for lanes in sides:
                tile = jnp.dot(keys, q_cols[unit, :, lanes], preferred_element_type=F32)
                tile = tile * (SCALE * LOG2E) + bias
                scores[item, :, lanes] = tile
                results.append((unit, lanes, jnp.max(tile.reshape(32, 8, 256), axis=0)))
        for unit, lanes, top in results:
            tops[unit, :, lanes] = jnp.maximum(tops[unit, :, lanes], top)
        return 0

    for unit in range(4):
        shift[unit] = jnp.broadcast_to(jnp.max(tops[unit], axis=0, keepdims=True), (8, LANES))
    loads[4].wait()

    @functools.partial(lax.fori_loop, 0, steps, init_val=0)
    def _(step, _):
        results = []
        for item in [4 * step + part for part in range(4)]:
            unit, slots, _ = entries(item)
            values_t = spans(slots, 1).T
            for lanes in sides:
                logits = scores[item, :, lanes].reshape(32, 8, 256)
                probs = jnp.exp2(logits - shift[unit, :, lanes][None])
                part = jnp.dot(
                    values_t, probs.reshape(256, 256).astype(BF16), preferred_element_type=F32
                )
                results.append((unit, lanes, jnp.sum(probs, axis=0), part))
        for unit, lanes, total, part in results:
            sums[unit, :, lanes] += total
            out_acc[unit, :, lanes] += part
        return 0

    for load in loads[5:]:
        load.wait()
    for unit in range(4):
        row_sum = jnp.sum(sums[unit], axis=0, keepdims=True)
        out = (out_acc[unit] * (1.0 / row_sum)).astype(BF16)
        both[unit, 0] = out
        row_dot = jnp.sum(
            out.astype(F32) * g_cols[unit].astype(F32), axis=0, keepdims=True
        )
        dots[unit] = jnp.broadcast_to(row_dot, (8, LANES))
        shift[unit] = shift[unit] + jnp.log(row_sum) * LOG2E

    @functools.partial(lax.fori_loop, 0, steps, init_val=0)
    def _(step, _):
        results = []
        for item in [4 * step + part for part in range(4)]:
            unit, slots, _ = entries(item)
            keys_t = spans(slots, 0).T
            values = spans(slots, 1)
            probs_b = []
            score_grads = []
            for lanes in sides:
                logits = scores[item, :, lanes].reshape(32, 8, 256)
                probs = jnp.exp2(logits - shift[unit, :, lanes][None])
                steep = jnp.dot(values, g_cols[unit, :, lanes], preferred_element_type=F32)
                steep = probs * (steep.reshape(32, 8, 256) - dots[unit, :, lanes][None])
                probs_b.append(probs.reshape(256, 256).astype(BF16))
                score_grads.append(steep.reshape(256, 256).astype(BF16))
            probs_b = jnp.concatenate(probs_b, axis=1)
            score_grads = jnp.concatenate(score_grads, axis=1)
            to_values = jnp.dot(probs_b, g_rows[unit], preferred_element_type=F32)
            to_keys = jnp.dot(score_grads, q_rows[unit], preferred_element_type=F32)
            to_query = jnp.dot(keys_t, score_grads, preferred_element_type=F32)
            results.append((slots, unit, to_values, to_keys, to_query))
        for slots, unit, to_values, to_keys, to_query in results:
            dq[unit] += to_query
            for acc, part in ((key_acc, to_keys), (value_acc, to_values)):
                sums_of = [
                    acc[slot] + part[index * SPAN : (index + 1) * SPAN]
                    for index, slot in enumerate(slots)
                ]
                for slot, total in zip(slots, sums_of):
                    acc[slot] = total
        return 0

    for unit in range(4):
        both[unit, 1] = (dq[unit] * SCALE).astype(BF16)
    both_store = pltpu.make_async_copy(both, both_out, out_sem.at[2 * NZ])
    both_store.start()
    stores = [both_store]
    for index in range(2 * NZ):
        for part in range(4):
            kv[index, 0, part] = (key_acc[index * 4 + part] * SCALE).astype(BF16)
            kv[index, 1, part] = value_acc[index * 4 + part].astype(BF16)
        store = pltpu.make_async_copy(kv.at[index], dkv.at[index], out_sem.at[index])
        store.start()
        stores.append(store)
    for store in stores:
        store.wait()


def attend(order, docs, q_cols, g_cols, q_rows, g_rows, kv):
    return pl.pallas_call(
        attend_kernel,
        out_shape=(
            jax.ShapeDtypeStruct((4, 2, HD, LANES), BF16),
            jax.ShapeDtypeStruct((2 * NZ, 2, 4, SPAN, HD), BF16),
        ),
        in_specs=[HBM] * 7,
        out_specs=(HBM,) * 2,
        scratch_shapes=[
            pltpu.SMEM((2 * SLOTS,), jnp.int32),
            pltpu.VMEM((SLOTS, ROWS), jnp.int32),
            pltpu.VMEM((4, HD, LANES), BF16),
            pltpu.VMEM((4, HD, LANES), BF16),
            pltpu.VMEM((4, LANES, HD), BF16),
            pltpu.VMEM((4, LANES, HD), BF16),
            pltpu.VMEM((4, 2, HD, LANES), BF16),
            pltpu.VMEM((4, HD, LANES), F32),
            pltpu.VMEM((2 * NZ + 1, 2, 4, SPAN, HD), BF16),
            pltpu.VMEM((4 * SLOTS // ITEM, ITEM * SPAN, LANES), F32),
            pltpu.VMEM((SLOTS + 1, SPAN, HD), F32),
            pltpu.VMEM((SLOTS + 1, SPAN, HD), F32),
            pltpu.VMEM((4, HD, LANES), F32),
            pltpu.VMEM((4, 8, LANES), F32),
            pltpu.VMEM((4, 8, LANES), F32),
            pltpu.VMEM((4, 8, LANES), F32),
            pltpu.VMEM((4, 8, LANES), F32),
            pltpu.VMEM((4, 8, ROWS), jnp.int32),
            pltpu.VMEM((4, 8, ROWS), jnp.int32),
            pltpu.SMEM((80,), jnp.int32),
            pltpu.SMEM((512,), jnp.int32),
            pltpu.SemaphoreType.DMA((8,)),
            pltpu.SemaphoreType.DMA((2 * NZ + 1,)),
        ],
        compiler_params=pltpu.CompilerParams(vmem_limit_bytes=60 << 20),
        cost_estimate=pl.CostEstimate(
            flops=6 * 2 * 2048 * 2048 * HD, bytes_accessed=12 << 20, transcendentals=2048 * 2048
        ),
        name="attend",
    )(order, docs, q_cols, g_cols, q_rows, g_rows, kv)


def return_kernel(
    both_in, dkv, both_out, dkv_out,
    both, terms, both_rows, order, landed, landed_rows, final, pair_send, pair_recv, own_sem, l_send, l_recv, r_send, r_recv,
):
    x, y, z, core = place()
    sibling = where_is(x, y, z, 1 - core)
    up = where_is(x, y, lax.rem(z + 1, NZ), core)
    down = where_is(x, y, lax.rem(z + NZ - 1, NZ), core)
    later = where_is(x, lax.rem(y + 1, NY), z, core)
    earlier = where_is(x, lax.rem(y + NY - 1, NY), z, core)
    loads = [
        pltpu.make_async_copy(both_in, both, own_sem.at[5]),
        pltpu.make_async_copy(dkv, terms, own_sem.at[4]),
    ]
    for load in loads:
        load.start()
    up_z, down_z = lax.rem(z + 1, NZ), lax.rem(z + NZ - 1, NZ)
    later_y, earlier_y = lax.rem(y + 1, NY), lax.rem(y + NY - 1, NY)
    corners = (where_is(x, earlier_y, up_z, core), where_is(x, earlier_y, down_z, core))
    behind = [where_is(x, later_y, up_z, core), where_is(x, later_y, down_z, core)]
    across = [
        where_is(x, y, up_z, 1 - core),
        where_is(x, y, down_z, 1 - core),
        where_is(x, earlier_y, z, 1 - core),
    ]
    greet(
        [sibling, up, down, later, earlier, *corners, *behind, *across]
        + [where_is(x, later_y, z, 1 - core)]
    )

    ways = (up, down)
    sent = []

    def at(group, distance, way):
        return group * NZ + lax.rem(z + NZ + distance * (-1 if way else 1), NZ)

    def ship(src, index, partner):
        copy = send(src, landed.at[index], l_send.at[index], l_recv.at[index], partner)
        sent.append(copy)
        return copy

    def add(block, kind, *indices):
        total = terms[block, kind].astype(F32)
        for index in indices:
            total = total + landed[index].astype(F32)
        terms[block, kind] = total.astype(BF16)

    mine = pl.ds(pl.multiple_of(core * ROWS, ROWS), ROWS)
    other = pl.ds(pl.multiple_of((1 - core) * ROWS, ROWS), ROWS)

    def deliver(block, kind, index, straight, crossed):
        copies = []
        for half, rows, partner in ((0, mine, straight), (1, other, crossed)):
            copy = send(
                terms.at[block, kind, rows], landed_rows.at[half, index],
                r_send.at[half, index], r_recv.at[half, index], partner,
            )
            sent.append(copy)
            copies.append(copy)
        return copies

    flying = {}
    for way in range(2):
        flying["s", 1, way, way] = ship(dkv.at[at(0, 4, 0), way], 16 + way, ways[way])
    for step, distance in ((0, 3), (1, 1)):
        for kind in range(2):
            for way in range(2):
                if step == 1 and kind == way:
                    continue
                flying["z", step, way, kind] = ship(
                    dkv.at[at(1, distance, way), kind], step * 4 + way * 2 + kind, ways[way]
                )
        if step == 0:
            for kind in range(2):
                flying["y", 4, kind] = ship(dkv.at[at(1, 4, 0), kind], 8 + kind, corners[kind])
    swaps = []
    own = []

    def turn(block, half):
        stacked = both[2 * block + half].reshape(2 * HD, LANES)
        rows = lax.dot_general(
            order[...], stacked, (((1,), (1,)), ((), ())), preferred_element_type=F32
        ).astype(BF16)
        for kind in range(2):
            both_rows[block, kind, half * LANES : (half + 1) * LANES, :] = rows[
                :, kind * HD : (kind + 1) * HD
            ]

    def swap():
        swaps.append(
            send(
                both_rows.at[1 - core], both_out.at[core], pair_send.at[0], pair_recv.at[0], sibling
            )
        )

    def stay():
        copy = pltpu.make_async_copy(both_rows.at[core], both_out.at[core], own_sem.at[0])
        copy.start()
        own.append(copy)

    row = lax.broadcasted_iota(jnp.int32, (LANES, LANES), 0)
    lane = lax.broadcasted_iota(jnp.int32, (LANES, LANES), 1)
    from_lane = lax.rem(row, GROUP) * SPAN + lax.div(row, GROUP)
    order[...] = jnp.where(lane == from_lane, 1.0, 0.0).astype(BF16)
    loads[1].wait()
    for kind in range(2):
        for way in range(2):
            flying["z", 0, way, kind].wait_recv()
            block = at(1, 2, way)
            add(block, kind, way * 2 + kind)
            flying["y", 2, way, kind] = ship(
                terms.at[block, kind], 10 + way * 2 + kind, earlier
            )
    for way in range(2):
        flying["y", 1, way] = ship(dkv.at[at(1, 1, way), way], 30 + way, earlier)
    for way in range(2):
        kind = 1 - way
        flying["s", 2, way, kind] = ship(
            terms.at[at(0, 3, way), kind], 18 + way * 2 + kind, ways[way]
        )
    loads[0].wait()
    turn(1 - core, 0)
    for kind in range(2):
        swaps.append(
            send(
                dkv.at[z, kind, other], landed_rows.at[1, 6 + kind],
                r_send.at[1, 6 + kind], r_recv.at[1, 6 + kind], sibling,
            )
        )
    for way in range(2):
        flying["s", 1, way, way].wait_recv()
        flying["y", 4, way].wait_recv()
        add(at(0, 3, way), way, 16 + way, 8 + way)
        flying["s", 2, way, way] = ship(
            terms.at[at(0, 3, way), way], 18 + way * 2 + way, ways[way]
        )
    for kind in range(2):
        way = 1 - kind
        flying["z", 1, way, kind].wait_recv()
        add(NZ + z, kind, 4 + way * 2 + kind)
        flying["y", 0, kind] = deliver(NZ + z, kind, kind, earlier, across[2])
    turn(1 - core, 1)
    for step in (3, 4):
        for turn_of in range(2):
            for way in range(2):
                kind = turn_of if way else 1 - turn_of
                flying["s", step - 1, way, kind].wait_recv()
                indices = [18 + (step - 3) * 4 + way * 2 + kind]
                if step == 3:
                    flying["y", 2, way, kind].wait_recv()
                    indices.append(10 + way * 2 + kind)
                elif kind == way:
                    flying["y", 1, way].wait_recv()
                    indices.append(30 + way)
                block = at(0, 5 - step, way)
                add(block, kind, *indices)
                if step == 3:
                    flying["s", step, way, kind] = ship(
                        terms.at[block, kind], 22 + way * 2 + kind, ways[way]
                    )
                else:
                    flying["s", step, way, kind] = deliver(
                        block, kind, 2 + way * 2 + kind, ways[way], across[way]
                    )
        if step == 3:
            turn(core, 0)
        else:
            swap()
            turn(core, 1)
            stay()
    for kind in range(2):
        for half in range(2):
            flying["y", 0, kind][half].wait_recv()
            for way in range(2):
                flying["s", 4, way, kind][half].wait_recv()
            if half:
                swaps[kind].wait_recv()
                total = landed_rows[1, 6 + kind].astype(F32)
            else:
                total = terms[z, kind, mine].astype(F32)
            for index in (kind, 2 + kind, 4 + kind):
                total = total + landed_rows[half, index].astype(F32)
            final[kind, half] = total
        for half in range(2):
            copy = pltpu.make_async_copy(
                final.at[kind, half], dkv_out.at[kind, core if half == 0 else 1 - core],
                own_sem.at[2 + (0, 5)[half] + kind],
            )
            copy.start()
            own.append(copy)
    for copy in sent:
        copy.wait_send()
    for copy in swaps[:2]:
        copy.wait_send()
    swaps[2].wait()
    for copy in own:
        copy.wait()


def give_back(both, dkv):
    return pl.pallas_call(
        return_kernel,
        out_shape=(
            jax.ShapeDtypeStruct((2, 2, ROWS * GROUP, HD), BF16),
            jax.ShapeDtypeStruct((2, 2, ROWS, HD), F32),
        ),
        in_specs=[HBM] * 2,
        out_specs=(HBM,) * 2,
        scratch_shapes=[
            pltpu.VMEM((4, 2, HD, LANES), BF16),
            pltpu.VMEM((2 * NZ, 2, 2 * ROWS, HD), BF16),
            pltpu.VMEM((2, 2, ROWS * GROUP, HD), BF16),
            pltpu.VMEM((LANES, LANES), BF16),
            pltpu.VMEM((32, 2 * ROWS, HD), BF16),
            pltpu.VMEM((2, 8, ROWS, HD), BF16),
            pltpu.VMEM((2, 2, ROWS, HD), F32),
            pltpu.SemaphoreType.DMA((1,)),
            pltpu.SemaphoreType.DMA((1,)),
            pltpu.SemaphoreType.DMA((9,)),
            pltpu.SemaphoreType.DMA((32,)),
            pltpu.SemaphoreType.DMA((32,)),
            pltpu.SemaphoreType.DMA((2, 8)),
            pltpu.SemaphoreType.DMA((2, 8)),
        ],
        compiler_params=pltpu.CompilerParams(
            collective_id=1, has_side_effects=True, vmem_limit_bytes=60 << 20
        ),
        name="give_back",
    )(both, dkv)


def finish_kernel(
    both, dkv, attn_out, dq_out, dk_out, dv_out, halves, attn, dq, parts, dk, dv, sem
):
    loads = [pltpu.make_async_copy(dkv, parts, sem.at[0])]
    for kind in range(2):
        loads.append(
            pltpu.make_async_copy(both.at[:, kind], halves.at[:, kind], sem.at[1 + kind])
        )
    for load in loads:
        load.start()
    stores = []
    loads[0].wait()
    for kind, (rows, dst) in enumerate(((dk, dk_out), (dv, dv_out))):
        for half in range(2):
            rows[pl.ds(half, ROWS, stride=2), :] = parts[kind, half]
        store = pltpu.make_async_copy(rows, dst, sem.at[3 + kind])
        store.start()
        stores.append(store)
    for kind, (joined, dst) in ((1, (dq, dq_out)), (0, (attn, attn_out))):
        loads[1 + kind].wait()
        pair = [halves[half, kind].astype(F32).reshape(ROWS, GROUP, HD) for half in range(2)]
        joined[...] = jnp.concatenate(pair, axis=1).astype(joined.dtype)
        store = pltpu.make_async_copy(joined, dst, sem.at[5 + kind])
        store.start()
        stores.append(store)
    for store in stores:
        store.wait()


def finish(both, dkv):
    return pl.pallas_call(
        finish_kernel,
        out_shape=(
            jax.ShapeDtypeStruct((ROWS, 2 * GROUP, HD), BF16),
            jax.ShapeDtypeStruct((ROWS, 2 * GROUP, HD), F32),
            jax.ShapeDtypeStruct((2 * ROWS, HD), F32),
            jax.ShapeDtypeStruct((2 * ROWS, HD), F32),
        ),
        in_specs=[HBM] * 2,
        out_specs=(HBM,) * 4,
        scratch_shapes=[
            pltpu.VMEM((2, 2, ROWS * GROUP, HD), BF16),
            pltpu.VMEM((ROWS, 2 * GROUP, HD), BF16),
            pltpu.VMEM((ROWS, 2 * GROUP, HD), F32),
            pltpu.VMEM((2, 2, ROWS, HD), F32),
            pltpu.VMEM((2 * ROWS, HD), F32),
            pltpu.VMEM((2 * ROWS, HD), F32),
            pltpu.SemaphoreType.DMA((7,)),
        ],
        compiler_params=pltpu.CompilerParams(vmem_limit_bytes=60 << 20),
        cost_estimate=pl.CostEstimate(flops=0, bytes_accessed=4 << 20, transcendentals=0),
        name="finish",
    )(both, dkv)


def local(queries, keys, values, grad_out, span_order, doc_ids):
    turned = [jnp.transpose(a, (1, 2, 0)) for a in (queries, keys, values, grad_out)]
    q_cols, g_cols, q_rows, g_rows, kv = bring(*turned)
    kv = kv.reshape(2 * NZ, 2, 4, SPAN, HD)
    both, dkv = attend(
        span_order, doc_ids.reshape(SLOTS, ROWS), q_cols, g_cols, q_rows, g_rows, kv
    )
    both, dkv = give_back(both, dkv.reshape(2 * NZ, 2, 2 * ROWS, HD))
    attn, dq, dk, dv = finish(both, dkv)
    return (attn, dq, dk.reshape(ROWS, 2, HD), dv.reshape(ROWS, 2, HD))


def solution(mesh):
    entry = P(("outer", "inner"), None, "head")
    leave = P(("outer", "inner"), "head", None)
    return jax.shard_map(
        local,
        mesh=mesh,
        in_specs=(entry, entry, entry, entry, P(), P()),
        out_specs=(leave, leave, leave, leave),
        check_vma=False,
    )
```

```python
import functools
import math

import jax
import jax.numpy as jnp
from jax import lax
from jax.experimental import pallas as pl
from jax.experimental.pallas import tpu as pltpu
from jax.sharding import PartitionSpec as P

MESH = pl.DeviceIdType.MESH
HBM = pl.BlockSpec(memory_space=pltpu.HBM)
NEG = -1e30
FAR = 1 << 24
NX = 4
NY = 4
NZ = 8
HD = 128
ROWS = 128
SPAN = 64
GROUP = 8
SLOTS = 64
LANES = GROUP * SPAN
SCALE = 1.0 / math.sqrt(HD)
LOG2E = math.log2(math.e)
ITEM = 4
BF16 = jnp.bfloat16
F32 = jnp.float32


def place():
    inner = lax.axis_index("inner")
    return (
        lax.axis_index("head"),
        lax.axis_index("outer"),
        lax.div(inner, 2),
        lax.rem(inner, 2),
    )


def where_is(x, y, z, core):
    return {"head": x, "outer": y, "inner": z * 2 + core}


def greet(partners, meanwhile):
    barrier = pltpu.get_barrier_semaphore()
    for partner in partners:
        pl.semaphore_signal(barrier, inc=1, device_id=partner, device_id_type=MESH)
    meanwhile()
    pl.semaphore_wait(barrier, len(partners))


def send(src, dst, send_sem, recv_sem, partner):
    copy = pltpu.make_async_remote_copy(
        src_ref=src,
        dst_ref=dst,
        send_sem=send_sem,
        recv_sem=recv_sem,
        device_id=partner,
        device_id_type=MESH,
    )
    copy.start()
    return copy


def bring_kernel(
    q, k, v, g, q_cols_out, g_cols_out, q_rows_out, g_rows_out, kv_out,
    q_cols, g_cols, q_rows, g_rows, out_sem, swap, q_in, g_in, kv_in, ring_kv, own_sem, keep_sem, x_send, x_recv, y_send, y_recv, z_send, z_recv,
):
    x, y, z, core = place()
    peers = [(dx, dc) for dx in range(NX) for dc in range(2) if (dx, dc) != (0, 0)]

    def peer(dx, dc):
        return where_is(lax.rem(x + dx, NX), y, z, lax.rem(core + dc, 2))

    up = where_is(x, y, lax.rem(z + 1, NZ), core)
    down = where_is(x, y, lax.rem(z + NZ - 1, NZ), core)
    later = where_is(x, lax.rem(y + 1, NY), z, core)
    earlier = where_is(x, lax.rem(y + NY - 1, NY), z, core)
    up_z, down_z = lax.rem(z + 1, NZ), lax.rem(z + NZ - 1, NZ)
    later_y, earlier_y = lax.rem(y + 1, NY), lax.rem(y + NY - 1, NY)
    corners = (where_is(x, later_y, up_z, core), where_is(x, later_y, down_z, core))
    behind = [where_is(x, earlier_y, up_z, core), where_is(x, earlier_y, down_z, core)]
    def prepare():
        row = lax.broadcasted_iota(jnp.int32, (2 * ROWS, 2 * ROWS), 0)
        lane = lax.broadcasted_iota(jnp.int32, (2 * ROWS, 2 * ROWS), 1)
        middle = (row >= SPAN) & (row < 3 * SPAN)
        swapped = jnp.where(row < ROWS, row + SPAN, row - SPAN)
        swap[...] = jnp.where(lane == jnp.where(middle, swapped, row), 1.0, 0.0).astype(BF16)

    greet([peer(*p) for p in peers] + [up, down, later, earlier, *corners, *behind], prepare)

    here = pl.ds(pl.multiple_of(x * 32, 32), 32)
    copies = []
    own = []
    for index, (dx, dc) in enumerate([(0, 0)] + peers):
        head = lax.rem(x + dx, NX) * 2 + lax.rem(core + dc, 2)
        for kind, src in enumerate((k, v)):
            dst = kv_in.at[kind, core, here]
            if index == 0:
                copy = pltpu.make_async_copy(src.at[head], dst, own_sem.at[kind])
                copy.start()
                own.append(copy)
            else:
                copies.append(
                    send(src.at[head], dst, x_send.at[kind, index], x_recv.at[kind, index], peer(dx, dc))
                )
    own[0].wait()
    own[1].wait()
    for copy in copies:
        copy.wait()
    for kind in range(2):
        for block in range(2):
            ring_kv[z, kind, block * ROWS : (block + 1) * ROWS, :] = (
                kv_in[kind, block].astype(F32).T.astype(BF16)
            )
    keeps = []
    sent = []
    ways = (up, down)

    def block_at(group, way, step):
        return group * NZ + lax.rem(z + NZ + step * (1 if way else -1), NZ)

    def keep(block, index):
        copy = pltpu.make_async_copy(ring_kv.at[block], kv_out.at[block], keep_sem.at[index])
        copy.start()
        keeps.append(copy)

    def hop(group, way, step, kind):
        block = block_at(group, way, step - 1)
        copy = send(
            ring_kv.at[block, kind], ring_kv.at[block, kind],
            z_send.at[group, way, step - 1, kind], z_recv.at[group, way, step - 1, kind],
            ways[way],
        )
        sent.append(copy)
        return copy

    def shift(way, step, kind):
        block = block_at(0, way, min(step, 3))
        copy = send(
            ring_kv.at[block, kind], ring_kv.at[NZ + block, kind],
            y_send.at[way, step, kind], y_recv.at[way, step, kind],
            corners[way] if step == 4 else later,
        )
        sent.append(copy)
        return copy

    def settle(kind):
        src, cols, rows = ((q_in, q_cols, q_rows), (g_in, g_cols, g_rows))[kind]
        own[2 + kind].wait()
        for copy in wide[kind]:
            copy.wait()
        for block in range(2):
            for pair in range(4):
                lanes = pl.ds(pair * ROWS, ROWS)
                both = jnp.concatenate(
                    [
                        jnp.concatenate([src[block, a, 2 * pair + b] for a in range(NX)], axis=0)
                        for b in range(2)
                    ],
                    axis=1,
                )
                across = jnp.dot(both, swap[...], preferred_element_type=F32).astype(BF16)
                along = lax.dot_general(
                    swap[...], both, (((1,), (1,)), ((), ())), preferred_element_type=F32
                ).astype(BF16)
                for half in range(2):
                    part = slice(half * ROWS, (half + 1) * ROWS)
                    cols[2 * block + half, :, lanes] = across[:, part]
                    rows[2 * block + half, lanes, :] = along[part]

        outs = ((q_cols_out, q_rows_out), (g_cols_out, g_rows_out))[kind]
        for index, (src, dst) in enumerate(zip((cols, rows), outs)):
            copy = pltpu.make_async_copy(src, dst, out_sem.at[kind, index])
            copy.start()
            own.append(copy)

    near = {}
    self_shift = {}
    for kind in range(2):
        for way in range(2):
            near[way, 1, kind] = hop(0, way, 1, kind)
        self_shift[kind] = shift(0, 0, kind)
    keep(z, 0)
    heads = pl.ds((x * 2 + core) * GROUP, GROUP)
    for kind, (src, dst) in enumerate(((q, q_in), (g, g_in))):
        copy = pltpu.make_async_copy(
            src.at[heads], dst.at[core, x], own_sem.at[2 + kind]
        )
        copy.start()
        own.append(copy)
    wide = ([], [])

    def spread(kind, *offsets):
        src, dst = ((q, q_in), (g, g_in))[kind]
        for index, (dx, dc) in enumerate(peers):
            if dx not in offsets:
                continue
            head = lax.rem(x + dx, NX) * 2 + lax.rem(core + dc, 2)
            wide[kind].append(
                send(
                    src.at[pl.ds(head * GROUP, GROUP)],
                    dst.at[core, x],
                    x_send.at[2 + kind, index],
                    x_recv.at[2 + kind, index],
                    peer(dx, dc),
                )
            )

    spread(0, 2)
    spread(0, 0, 1)
    far_shift = {}
    for step in range(1, 4):
        for kind in range(2):
            for way in range(2):
                near[way, step, kind].wait_recv()
                if step < 3 or kind == way:
                    near[way, step + 1, kind] = hop(0, way, step + 1, kind)
                if step == 3 and kind == way:
                    far_shift[way, 4] = shift(way, 4, way)
                if step == 2 or (step == 1 and kind == way):
                    far_shift[way, step, kind] = shift(way, step, kind)
        for way in range(2):
            keep(block_at(0, way, step), 1 + 2 * step + way)
        if step == 1:
            spread(0, 3)
            spread(1, 2)
        elif step == 2:
            spread(1, 0, 1, 3)
    hops = {}
    for kind in range(2):
        self_shift[kind].wait_recv()
        hops[1 - kind, 1, kind] = hop(1, 1 - kind, 1, kind)
    keep(NZ + z, 1)
    for kind in range(2):
        for way in range(2):
            far_shift[way, 2, kind].wait_recv()
            hops[way, 3, kind] = hop(1, way, 3, kind)
    for way in range(2):
        keep(block_at(1, way, 2), 9 + way)
    settle(0)
    settle(1)
    for way in range(2):
        near[way, 4, way].wait_recv()
    keep(block_at(0, 0, 4), 2)
    for step in (1, 3):
        for way in range(2):
            for kind in range(2):
                arriving = far_shift if step == 1 and kind == way else hops
                arriving[way, step, kind].wait_recv()
            keep(block_at(1, way, step), 10 + step + way)
    for way in range(2):
        far_shift[way, 4].wait_recv()
    keep(block_at(1, 0, 4), 15)
    for copy in sent:
        copy.wait_send()
    for copy in keeps:
        copy.wait()
    for copy in own[4:]:
        copy.wait()


def bring(q, k, v, g):
    return pl.pallas_call(
        bring_kernel,
        out_shape=(
            jax.ShapeDtypeStruct((4, HD, LANES), BF16),
            jax.ShapeDtypeStruct((4, HD, LANES), BF16),
            jax.ShapeDtypeStruct((4, LANES, HD), BF16),
            jax.ShapeDtypeStruct((4, LANES, HD), BF16),
            jax.ShapeDtypeStruct((2 * NZ, 2, 2 * ROWS, HD), BF16),
        ),
        in_specs=[HBM] * 4,
        out_specs=(HBM,) * 5,
        scratch_shapes=[
            pltpu.VMEM((4, HD, LANES), BF16),
            pltpu.VMEM((4, HD, LANES), BF16),
            pltpu.VMEM((4, LANES, HD), BF16),
            pltpu.VMEM((4, LANES, HD), BF16),
            pltpu.SemaphoreType.DMA((2, 2)),
            pltpu.VMEM((2 * ROWS, 2 * ROWS), BF16),
            pltpu.VMEM((2, NX, GROUP, HD // NX, ROWS), BF16),
            pltpu.VMEM((2, NX, GROUP, HD // NX, ROWS), BF16),
            pltpu.VMEM((2, 2, HD, ROWS), BF16),
            pltpu.VMEM((2 * NZ, 2, 2 * ROWS, HD), BF16),
            pltpu.SemaphoreType.DMA((4,)),
            pltpu.SemaphoreType.DMA((16,)),
            pltpu.SemaphoreType.DMA((4, 8)),
            pltpu.SemaphoreType.DMA((4, 8)),
            pltpu.SemaphoreType.DMA((2, 5, 2)),
            pltpu.SemaphoreType.DMA((2, 5, 2)),
            pltpu.SemaphoreType.DMA((2, 2, 4, 2)),
            pltpu.SemaphoreType.DMA((2, 2, 4, 2)),
        ],
        compiler_params=pltpu.CompilerParams(
            collective_id=0, has_side_effects=True, vmem_limit_bytes=60 << 20
        ),
        name="bring",
    )(q, k, v, g)


def attend_kernel(
    order_in, docs_in, q_cols_in, g_cols_in, q_rows_in, g_rows_in, kv_in, both_out, dkv,
    order, docs, q_cols, g_cols, q_rows, g_rows, both, dq, kv, scores, key_acc, value_acc, out_acc, tops, sums, shift, dots,
    pos_rows, start_rows, item_list, span_list, in_sem, out_sem,
):
    outer = lax.axis_index("outer")
    chip = lax.div(lax.axis_index("inner"), 2)
    loads = [
        pltpu.make_async_copy(order_in, order, in_sem.at[0]),
        pltpu.make_async_copy(docs_in, docs, in_sem.at[1]),
        pltpu.make_async_copy(q_cols_in, q_cols, in_sem.at[2]),
        pltpu.make_async_copy(kv_in.at[:, 0], kv.at[pl.ds(0, 2 * NZ), 0], in_sem.at[3]),
        pltpu.make_async_copy(kv_in.at[:, 1], kv.at[pl.ds(0, 2 * NZ), 1], in_sem.at[4]),
        pltpu.make_async_copy(g_cols_in, g_cols, in_sem.at[5]),
        pltpu.make_async_copy(q_rows_in, q_rows, in_sem.at[6]),
        pltpu.make_async_copy(g_rows_in, g_rows, in_sem.at[7]),
    ]
    for load in loads:
        load.start()
    kv[2 * NZ] = jnp.zeros((2, 4, SPAN, HD), BF16)
    tops[...] = jnp.full_like(tops, NEG)
    sums[...] = jnp.zeros_like(sums)
    loads[0].wait()
    loads[1].wait()
    doc = docs[...]
    starts = [
        jnp.sum(jnp.where(doc < d, 1.0, 0.0)).astype(jnp.int32) for d in range(1, 4)
    ]

    def start_of(position):
        found = jnp.zeros_like(position)
        for start in starts:
            found = jnp.where(position >= start, jnp.maximum(found, start), found)
        return found

    iota_lanes = lax.rem(lax.broadcasted_iota(jnp.int32, (8, ROWS), 1), SPAN)
    lows = []
    highs = []
    for unit in range(4):
        query_span = order[outer * 32 + chip * 4 + unit]
        lows.append(lax.div(start_of(query_span * SPAN), SPAN))
        highs.append(query_span)
        query_pos = query_span * SPAN + iota_lanes
        pos_rows[unit] = query_pos
        start_rows[unit] = start_of(query_pos)

    counts = tuple(jnp.int32(unit * 128) for unit in range(4))
    for group in range(2):
        stored = lax.rem(outer + 4 - group, 4) * 32

        def note(step, counts):
            for part in range(8):
                slot = step * 8 + part
                span = order[stored + slot]
                entry = span * (2 * SPAN) + (group * 32 + slot)
                new = []
                for unit in range(4):
                    span_list[counts[unit]] = entry
                    allowed = (span >= lows[unit]) & (span <= highs[unit])
                    new.append(counts[unit] + jnp.where(allowed, 1, 0))
                counts = tuple(new)
            nothing = jnp.zeros((8, SPAN, HD), F32)
            rows = pl.ds((group * 4 + step) * 8, 8)
            key_acc[rows] = nothing
            value_acc[rows] = nothing
            flat = pl.ds(pl.multiple_of(step * 32, 32), 32)
            for unit in range(2 * group, 2 * group + 2):
                out_acc[unit, flat, :] = jnp.zeros((32, LANES), F32)
                dq[unit, flat, :] = jnp.zeros((32, LANES), F32)
            return counts

        counts = lax.fori_loop(0, 4, note, counts)
    items = jnp.int32(0)
    for unit in range(4):
        for extra in range(ITEM):
            span_list[counts[unit] + extra] = 2 * FAR + SLOTS
        for chunk in range(SLOTS // ITEM):
            item_list[items + chunk] = unit * 128 + chunk * ITEM
        items = items + lax.div(counts[unit] - unit * 128 + ITEM - 1, ITEM)
    blank = 3 * 128 + 72
    for extra in range(ITEM):
        span_list[blank + extra] = 2 * FAR + SLOTS
    for extra in range(4):
        item_list[items + extra] = blank
    steps = lax.div(items + 3, 4)

    iota_keys = (
        lax.broadcasted_iota(jnp.int32, (8, 8, ROWS), 0) * 8
        + lax.broadcasted_iota(jnp.int32, (8, 8, ROWS), 1)
    )

    def entries(item):
        first = item_list[item]
        found = [span_list[first + part] for part in range(ITEM)]
        slots = [lax.rem(entry, 2 * SPAN) for entry in found]
        return lax.div(first, 128), slots, [lax.div(a - b, 2) for a, b in zip(found, slots)]

    def spans(slots, kind):
        parts = []
        for slot in slots:
            parts.append(kv[lax.div(slot, 4), kind, lax.rem(slot, 4)])
        return jnp.concatenate(parts, axis=0)

    sides = [pl.ds(side * 256, 256) for side in range(2)]
    loads[2].wait()
    loads[3].wait()

    @functools.partial(lax.fori_loop, 0, steps, init_val=0)
    def _(step, _):
        results = []
        for item in [4 * step + part for part in range(4)]:
            unit, slots, bases = entries(item)
            keys = spans(slots, 0)
            biases = []
            for base in bases:
                allowed = (iota_keys <= (pos_rows[unit] - base)[None]) & (
                    iota_keys >= (start_rows[unit] - base)[None]
                )
                biases.append(jnp.where(allowed, 0.0, NEG).reshape(SPAN, ROWS))
            bias = jnp.concatenate(biases, axis=0)
            bias = jnp.concatenate([bias, bias], axis=1)
            for lanes in sides:
                tile = jnp.dot(keys, q_cols[unit, :, lanes], preferred_element_type=F32)
                tile = tile * (SCALE * LOG2E) + bias
                scores[item, :, lanes] = tile
                results.append((unit, lanes, jnp.max(tile.reshape(32, 8, 256), axis=0)))
        for unit, lanes, top in results:
            tops[unit, :, lanes] = jnp.maximum(tops[unit, :, lanes], top)
        return 0

    for unit in range(4):
        shift[unit] = jnp.broadcast_to(jnp.max(tops[unit], axis=0, keepdims=True), (8, LANES))
    loads[4].wait()

    @functools.partial(lax.fori_loop, 0, steps, init_val=0)
    def _(step, _):
        results = []
        for item in [4 * step + part for part in range(4)]:
            unit, slots, _ = entries(item)
            values_t = spans(slots, 1).T
            for lanes in sides:
                logits = scores[item, :, lanes].reshape(32, 8, 256)
                probs = jnp.exp2(logits - shift[unit, :, lanes][None])
                part = jnp.dot(
                    values_t, probs.reshape(256, 256).astype(BF16), preferred_element_type=F32
                )
                results.append((unit, lanes, jnp.sum(probs, axis=0), part))
        for unit, lanes, total, part in results:
            sums[unit, :, lanes] += total
            out_acc[unit, :, lanes] += part
        return 0

    for load in loads[5:]:
        load.wait()
    for unit in range(4):
        row_sum = jnp.sum(sums[unit], axis=0, keepdims=True)
        out = (out_acc[unit] * (1.0 / row_sum)).astype(BF16)
        both[unit, 0] = out
        row_dot = jnp.sum(
            out.astype(F32) * g_cols[unit].astype(F32), axis=0, keepdims=True
        )
        dots[unit] = jnp.broadcast_to(row_dot, (8, LANES))
        shift[unit] = shift[unit] + jnp.log(row_sum) * LOG2E

    @functools.partial(lax.fori_loop, 0, steps, init_val=0)
    def _(step, _):
        results = []
        for item in [4 * step + part for part in range(4)]:
            unit, slots, _ = entries(item)
            keys_t = spans(slots, 0).T
            values = spans(slots, 1)
            probs_b = []
            score_grads = []
            for lanes in sides:
                logits = scores[item, :, lanes].reshape(32, 8, 256)
                probs = jnp.exp2(logits - shift[unit, :, lanes][None])
                steep = jnp.dot(values, g_cols[unit, :, lanes], preferred_element_type=F32)
                steep = probs * (steep.reshape(32, 8, 256) - dots[unit, :, lanes][None])
                probs_b.append(probs.reshape(256, 256).astype(BF16))
                score_grads.append(steep.reshape(256, 256).astype(BF16))
            probs_b = jnp.concatenate(probs_b, axis=1)
            score_grads = jnp.concatenate(score_grads, axis=1)
            to_values = jnp.dot(probs_b, g_rows[unit], preferred_element_type=F32)
            to_keys = jnp.dot(score_grads, q_rows[unit], preferred_element_type=F32)
            to_query = jnp.dot(keys_t, score_grads, preferred_element_type=F32)
            results.append((slots, unit, to_values, to_keys, to_query))
        for slots, unit, to_values, to_keys, to_query in results:
            dq[unit] += to_query
            for acc, part in ((key_acc, to_keys), (value_acc, to_values)):
                sums_of = [
                    acc[slot] + part[index * SPAN : (index + 1) * SPAN]
                    for index, slot in enumerate(slots)
                ]
                for slot, total in zip(slots, sums_of):
                    acc[slot] = total
        return 0

    for unit in range(4):
        both[unit, 1] = (dq[unit] * SCALE).astype(BF16)
    both_store = pltpu.make_async_copy(both, both_out, out_sem.at[2 * NZ])
    both_store.start()
    stores = [both_store]
    for index in range(2 * NZ):
        for part in range(4):
            kv[index, 0, part] = (key_acc[index * 4 + part] * SCALE).astype(BF16)
            kv[index, 1, part] = value_acc[index * 4 + part].astype(BF16)
        store = pltpu.make_async_copy(kv.at[index], dkv.at[index], out_sem.at[index])
        store.start()
        stores.append(store)
    for store in stores:
        store.wait()


def attend(order, docs, q_cols, g_cols, q_rows, g_rows, kv):
    return pl.pallas_call(
        attend_kernel,
        out_shape=(
            jax.ShapeDtypeStruct((4, 2, HD, LANES), BF16),
            jax.ShapeDtypeStruct((2 * NZ, 2, 4, SPAN, HD), BF16),
        ),
        in_specs=[HBM] * 7,
        out_specs=(HBM,) * 2,
        scratch_shapes=[
            pltpu.SMEM((2 * SLOTS,), jnp.int32),
            pltpu.VMEM((SLOTS, ROWS), jnp.int32),
            pltpu.VMEM((4, HD, LANES), BF16),
            pltpu.VMEM((4, HD, LANES), BF16),
            pltpu.VMEM((4, LANES, HD), BF16),
            pltpu.VMEM((4, LANES, HD), BF16),
            pltpu.VMEM((4, 2, HD, LANES), BF16),
            pltpu.VMEM((4, HD, LANES), F32),
            pltpu.VMEM((2 * NZ + 1, 2, 4, SPAN, HD), BF16),
            pltpu.VMEM((4 * SLOTS // ITEM, ITEM * SPAN, LANES), F32),
            pltpu.VMEM((SLOTS + 1, SPAN, HD), F32),
            pltpu.VMEM((SLOTS + 1, SPAN, HD), F32),
            pltpu.VMEM((4, HD, LANES), F32),
            pltpu.VMEM((4, 8, LANES), F32),
            pltpu.VMEM((4, 8, LANES), F32),
            pltpu.VMEM((4, 8, LANES), F32),
            pltpu.VMEM((4, 8, LANES), F32),
            pltpu.VMEM((4, 8, ROWS), jnp.int32),
            pltpu.VMEM((4, 8, ROWS), jnp.int32),
            pltpu.SMEM((80,), jnp.int32),
            pltpu.SMEM((512,), jnp.int32),
            pltpu.SemaphoreType.DMA((8,)),
            pltpu.SemaphoreType.DMA((2 * NZ + 1,)),
        ],
        compiler_params=pltpu.CompilerParams(vmem_limit_bytes=60 << 20),
        cost_estimate=pl.CostEstimate(
            flops=6 * 2 * 2048 * 2048 * HD, bytes_accessed=12 << 20, transcendentals=2048 * 2048
        ),
        name="attend",
    )(order, docs, q_cols, g_cols, q_rows, g_rows, kv)


def return_kernel(
    both_in, dkv, both_out, dkv_out,
    both, terms, both_rows, order, landed, landed_rows, final, pair_send, pair_recv, own_sem, l_send, l_recv, r_send, r_recv,
):
    x, y, z, core = place()
    sibling = where_is(x, y, z, 1 - core)
    up = where_is(x, y, lax.rem(z + 1, NZ), core)
    down = where_is(x, y, lax.rem(z + NZ - 1, NZ), core)
    later = where_is(x, lax.rem(y + 1, NY), z, core)
    earlier = where_is(x, lax.rem(y + NY - 1, NY), z, core)
    loads = [
        pltpu.make_async_copy(both_in, both, own_sem.at[5]),
        pltpu.make_async_copy(dkv, terms, own_sem.at[4]),
    ]
    for load in loads:
        load.start()
    up_z, down_z = lax.rem(z + 1, NZ), lax.rem(z + NZ - 1, NZ)
    later_y, earlier_y = lax.rem(y + 1, NY), lax.rem(y + NY - 1, NY)
    corners = (where_is(x, earlier_y, up_z, core), where_is(x, earlier_y, down_z, core))
    behind = [where_is(x, later_y, up_z, core), where_is(x, later_y, down_z, core)]
    across = [
        where_is(x, y, up_z, 1 - core),
        where_is(x, y, down_z, 1 - core),
        where_is(x, earlier_y, z, 1 - core),
    ]
    def prepare():
        row = lax.broadcasted_iota(jnp.int32, (LANES, LANES), 0)
        lane = lax.broadcasted_iota(jnp.int32, (LANES, LANES), 1)
        from_lane = (row & (GROUP - 1)) * SPAN + (row >> 3)
        order[...] = jnp.where(lane == from_lane, 1.0, 0.0).astype(BF16)

    greet(
        [sibling, up, down, later, earlier, *corners, *behind, *across]
        + [where_is(x, later_y, z, 1 - core)],
        prepare,
    )

    ways = (up, down)
    sent = []

    def at(group, distance, way):
        return group * NZ + lax.rem(z + NZ + distance * (-1 if way else 1), NZ)

    def ship(src, index, partner):
        copy = send(src, landed.at[index], l_send.at[index], l_recv.at[index], partner)
        sent.append(copy)
        return copy

    def add(block, kind, *indices):
        total = terms[block, kind].astype(F32)
        for index in indices:
            total = total + landed[index].astype(F32)
        terms[block, kind] = total.astype(BF16)

    mine = pl.ds(pl.multiple_of(core * ROWS, ROWS), ROWS)
    other = pl.ds(pl.multiple_of((1 - core) * ROWS, ROWS), ROWS)

    def deliver(block, kind, index, straight, crossed):
        copies = []
        for half, rows, partner in ((0, mine, straight), (1, other, crossed)):
            copy = send(
                terms.at[block, kind, rows], landed_rows.at[half, index],
                r_send.at[half, index], r_recv.at[half, index], partner,
            )
            sent.append(copy)
            copies.append(copy)
        return copies

    flying = {}
    for way in range(2):
        flying["s", 1, way, way] = ship(dkv.at[at(0, 4, 0), way], 16 + way, ways[way])
    for step, distance in ((0, 3), (1, 1)):
        for kind in range(2):
            for way in range(2):
                if step == 1 and kind == way:
                    continue
                flying["z", step, way, kind] = ship(
                    dkv.at[at(1, distance, way), kind], step * 4 + way * 2 + kind, ways[way]
                )
        if step == 0:
            for kind in range(2):
                flying["y", 4, kind] = ship(dkv.at[at(1, 4, 0), kind], 8 + kind, corners[kind])
    swaps = []
    own = []

    def turn(block, half):
        stacked = both[2 * block + half].reshape(2 * HD, LANES)
        rows = lax.dot_general(
            order[...], stacked, (((1,), (1,)), ((), ())), preferred_element_type=F32
        ).astype(BF16)
        for kind in range(2):
            both_rows[block, kind, half * LANES : (half + 1) * LANES, :] = rows[
                :, kind * HD : (kind + 1) * HD
            ]

    def swap():
        swaps.append(
            send(
                both_rows.at[1 - core], both_out.at[core], pair_send.at[0], pair_recv.at[0], sibling
            )
        )

    def stay():
        copy = pltpu.make_async_copy(both_rows.at[core], both_out.at[core], own_sem.at[0])
        copy.start()
        own.append(copy)

    loads[1].wait()
    for kind in range(2):
        for way in range(2):
            flying["z", 0, way, kind].wait_recv()
            block = at(1, 2, way)
            add(block, kind, way * 2 + kind)
            flying["y", 2, way, kind] = ship(
                terms.at[block, kind], 10 + way * 2 + kind, earlier
            )
    for way in range(2):
        flying["y", 1, way] = ship(dkv.at[at(1, 1, way), way], 30 + way, earlier)
    for way in range(2):
        kind = 1 - way
        flying["s", 2, way, kind] = ship(
            terms.at[at(0, 3, way), kind], 18 + way * 2 + kind, ways[way]
        )
    loads[0].wait()
    turn(1 - core, 0)
    for kind in range(2):
        swaps.append(
            send(
                dkv.at[z, kind, other], landed_rows.at[1, 6 + kind],
                r_send.at[1, 6 + kind], r_recv.at[1, 6 + kind], sibling,
            )
        )
    for way in range(2):
        flying["s", 1, way, way].wait_recv()
        flying["y", 4, way].wait_recv()
        add(at(0, 3, way), way, 16 + way, 8 + way)
        flying["s", 2, way, way] = ship(
            terms.at[at(0, 3, way), way], 18 + way * 2 + way, ways[way]
        )
    for kind in range(2):
        way = 1 - kind
        flying["z", 1, way, kind].wait_recv()
        add(NZ + z, kind, 4 + way * 2 + kind)
        flying["y", 0, kind] = deliver(NZ + z, kind, kind, earlier, across[2])
    turn(1 - core, 1)
    for step in (3, 4):
        for turn_of in range(2):
            for way in range(2):
                kind = turn_of if way else 1 - turn_of
                flying["s", step - 1, way, kind].wait_recv()
                indices = [18 + (step - 3) * 4 + way * 2 + kind]
                if step == 3:
                    flying["y", 2, way, kind].wait_recv()
                    indices.append(10 + way * 2 + kind)
                elif kind == way:
                    flying["y", 1, way].wait_recv()
                    indices.append(30 + way)
                block = at(0, 5 - step, way)
                add(block, kind, *indices)
                if step == 3:
                    flying["s", step, way, kind] = ship(
                        terms.at[block, kind], 22 + way * 2 + kind, ways[way]
                    )
                else:
                    flying["s", step, way, kind] = deliver(
                        block, kind, 2 + way * 2 + kind, ways[way], across[way]
                    )
        if step == 3:
            turn(core, 0)
        else:
            swap()
            turn(core, 1)
            stay()
    for kind in range(2):
        for half in range(2):
            flying["y", 0, kind][half].wait_recv()
            for way in range(2):
                flying["s", 4, way, kind][half].wait_recv()
            if half:
                swaps[kind].wait_recv()
                total = landed_rows[1, 6 + kind].astype(F32)
            else:
                total = terms[z, kind, mine].astype(F32)
            for index in (kind, 2 + kind, 4 + kind):
                total = total + landed_rows[half, index].astype(F32)
            final[kind, half] = total
        for half in range(2):
            copy = pltpu.make_async_copy(
                final.at[kind, half], dkv_out.at[kind, core if half == 0 else 1 - core],
                own_sem.at[2 + (0, 5)[half] + kind],
            )
            copy.start()
            own.append(copy)
    for copy in sent:
        copy.wait_send()
    for copy in swaps[:2]:
        copy.wait_send()
    swaps[2].wait()
    for copy in own:
        copy.wait()


def give_back(both, dkv):
    return pl.pallas_call(
        return_kernel,
        out_shape=(
            jax.ShapeDtypeStruct((2, 2, ROWS * GROUP, HD), BF16),
            jax.ShapeDtypeStruct((2, 2, ROWS, HD), F32),
        ),
        in_specs=[HBM] * 2,
        out_specs=(HBM,) * 2,
        scratch_shapes=[
            pltpu.VMEM((4, 2, HD, LANES), BF16),
            pltpu.VMEM((2 * NZ, 2, 2 * ROWS, HD), BF16),
            pltpu.VMEM((2, 2, ROWS * GROUP, HD), BF16),
            pltpu.VMEM((LANES, LANES), BF16),
            pltpu.VMEM((32, 2 * ROWS, HD), BF16),
            pltpu.VMEM((2, 8, ROWS, HD), BF16),
            pltpu.VMEM((2, 2, ROWS, HD), F32),
            pltpu.SemaphoreType.DMA((1,)),
            pltpu.SemaphoreType.DMA((1,)),
            pltpu.SemaphoreType.DMA((9,)),
            pltpu.SemaphoreType.DMA((32,)),
            pltpu.SemaphoreType.DMA((32,)),
            pltpu.SemaphoreType.DMA((2, 8)),
            pltpu.SemaphoreType.DMA((2, 8)),
        ],
        compiler_params=pltpu.CompilerParams(
            collective_id=1, has_side_effects=True, vmem_limit_bytes=60 << 20
        ),
        name="give_back",
    )(both, dkv)


def finish_kernel(
    both, dkv, attn_out, dq_out, dk_out, dv_out, halves, attn, dq, parts, dk, dv, sem
):
    loads = [pltpu.make_async_copy(dkv, parts, sem.at[0])]
    for kind in range(2):
        loads.append(
            pltpu.make_async_copy(both.at[:, kind], halves.at[:, kind], sem.at[1 + kind])
        )
    for load in loads:
        load.start()
    stores = []
    loads[0].wait()
    for kind, (rows, dst) in enumerate(((dk, dk_out), (dv, dv_out))):
        for half in range(2):
            rows[pl.ds(half, ROWS, stride=2), :] = parts[kind, half]
        store = pltpu.make_async_copy(rows, dst, sem.at[3 + kind])
        store.start()
        stores.append(store)
    for kind, (joined, dst) in ((1, (dq, dq_out)), (0, (attn, attn_out))):
        loads[1 + kind].wait()
        pair = [halves[half, kind].astype(F32).reshape(ROWS, GROUP, HD) for half in range(2)]
        joined[...] = jnp.concatenate(pair, axis=1).astype(joined.dtype)
        store = pltpu.make_async_copy(joined, dst, sem.at[5 + kind])
        store.start()
        stores.append(store)
    for store in stores:
        store.wait()


def finish(both, dkv):
    return pl.pallas_call(
        finish_kernel,
        out_shape=(
            jax.ShapeDtypeStruct((ROWS, 2 * GROUP, HD), BF16),
            jax.ShapeDtypeStruct((ROWS, 2 * GROUP, HD), F32),
            jax.ShapeDtypeStruct((2 * ROWS, HD), F32),
            jax.ShapeDtypeStruct((2 * ROWS, HD), F32),
        ),
        in_specs=[HBM] * 2,
        out_specs=(HBM,) * 4,
        scratch_shapes=[
            pltpu.VMEM((2, 2, ROWS * GROUP, HD), BF16),
            pltpu.VMEM((ROWS, 2 * GROUP, HD), BF16),
            pltpu.VMEM((ROWS, 2 * GROUP, HD), F32),
            pltpu.VMEM((2, 2, ROWS, HD), F32),
            pltpu.VMEM((2 * ROWS, HD), F32),
            pltpu.VMEM((2 * ROWS, HD), F32),
            pltpu.SemaphoreType.DMA((7,)),
        ],
        compiler_params=pltpu.CompilerParams(vmem_limit_bytes=60 << 20),
        cost_estimate=pl.CostEstimate(flops=0, bytes_accessed=4 << 20, transcendentals=0),
        name="finish",
    )(both, dkv)


def local(queries, keys, values, grad_out, span_order, doc_ids):
    turned = [jnp.transpose(a, (1, 2, 0)) for a in (queries, keys, values, grad_out)]
    q_cols, g_cols, q_rows, g_rows, kv = bring(*turned)
    kv = kv.reshape(2 * NZ, 2, 4, SPAN, HD)
    both, dkv = attend(
        span_order, doc_ids.reshape(SLOTS, ROWS), q_cols, g_cols, q_rows, g_rows, kv
    )
    both, dkv = give_back(both, dkv.reshape(2 * NZ, 2, 2 * ROWS, HD))
    attn, dq, dk, dv = finish(both, dkv)
    return (attn, dq, dk.reshape(ROWS, 2, HD), dv.reshape(ROWS, 2, HD))


def solution(mesh):
    entry = P(("outer", "inner"), None, "head")
    leave = P(("outer", "inner"), "head", None)
    return jax.shard_map(
        local,
        mesh=mesh,
        in_specs=(entry, entry, entry, entry, P(), P()),
        out_specs=(leave, leave, leave, leave),
        check_vma=False,
    )
```

```python
import functools
import math

import jax
import jax.numpy as jnp
from jax import lax
from jax.experimental import pallas as pl
from jax.experimental.pallas import tpu as pltpu
from jax.sharding import PartitionSpec as P

MESH = pl.DeviceIdType.MESH
HBM = pl.BlockSpec(memory_space=pltpu.HBM)
NEG = -1e30
FAR = 1 << 24
NX = 4
NY = 4
NZ = 8
HD = 128
ROWS = 128
SPAN = 64
GROUP = 8
SLOTS = 64
LANES = GROUP * SPAN
SCALE = 1.0 / math.sqrt(HD)
LOG2E = math.log2(math.e)
ITEM = 4
BF16 = jnp.bfloat16
F32 = jnp.float32


def place():
    inner = lax.axis_index("inner")
    return (
        lax.axis_index("head"),
        lax.axis_index("outer"),
        lax.div(inner, 2),
        lax.rem(inner, 2),
    )


def where_is(x, y, z, core):
    return {"head": x, "outer": y, "inner": z * 2 + core}


def greet(partners):
    barrier = pltpu.get_barrier_semaphore()
    for partner in partners:
        pl.semaphore_signal(barrier, inc=1, device_id=partner, device_id_type=MESH)
    pl.semaphore_wait(barrier, len(partners))


def send(src, dst, send_sem, recv_sem, partner):
    copy = pltpu.make_async_remote_copy(
        src_ref=src,
        dst_ref=dst,
        send_sem=send_sem,
        recv_sem=recv_sem,
        device_id=partner,
        device_id_type=MESH,
    )
    copy.start()
    return copy


def bring_kernel(
    q, k, v, g, q_cols_out, g_cols_out, q_rows_out, g_rows_out, kv_out,
    q_cols, g_cols, q_rows, g_rows, out_sem, q_in, g_in, kv_in, ring_kv, relay, relay_sem, own_sem, keep_sem, x_send, x_recv, y_send, y_recv, z_send, z_recv,
):
    x, y, z, core = place()
    peers = [(dx, dc) for dx in range(NX) for dc in range(2) if (dx, dc) != (0, 0)]

    def peer(dx, dc):
        return where_is(lax.rem(x + dx, NX), y, z, lax.rem(core + dc, 2))

    up = where_is(x, y, lax.rem(z + 1, NZ), core)
    down = where_is(x, y, lax.rem(z + NZ - 1, NZ), core)
    later = where_is(x, lax.rem(y + 1, NY), z, core)
    earlier = where_is(x, lax.rem(y + NY - 1, NY), z, core)
    up_z, down_z = lax.rem(z + 1, NZ), lax.rem(z + NZ - 1, NZ)
    later_y, earlier_y = lax.rem(y + 1, NY), lax.rem(y + NY - 1, NY)
    corners = (where_is(x, later_y, up_z, core), where_is(x, later_y, down_z, core))
    behind = [where_is(x, earlier_y, up_z, core), where_is(x, earlier_y, down_z, core)]
    greet([peer(*p) for p in peers] + [up, down, later, earlier, *corners, *behind])

    here = pl.ds(pl.multiple_of(x * 32, 32), 32)
    copies = []
    own = []
    for index, (dx, dc) in enumerate([(0, 0)] + peers):
        head = lax.rem(x + dx, NX) * 2 + lax.rem(core + dc, 2)
        for kind, src in enumerate((k, v)):
            dst = kv_in.at[kind, core, here]
            if index == 0:
                copy = pltpu.make_async_copy(src.at[head], dst, own_sem.at[kind])
                copy.start()
                own.append(copy)
            else:
                copies.append(
                    send(src.at[head], dst, x_send.at[kind, index], x_recv.at[kind, index], peer(dx, dc))
                )
    own[0].wait()
    own[1].wait()
    for copy in copies:
        copy.wait()
    for kind in range(2):
        for block in range(2):
            ring_kv[z, kind, block * ROWS : (block + 1) * ROWS, :] = (
                kv_in[kind, block].astype(F32).T.astype(BF16)
            )
    keeps = []
    sent = []
    ways = (up, down)

    def block_at(group, way, step):
        return group * NZ + lax.rem(z + NZ + step * (1 if way else -1), NZ)

    def keep(block, index):
        copy = pltpu.make_async_copy(ring_kv.at[block], kv_out.at[block], keep_sem.at[index])
        copy.start()
        keeps.append(copy)

    def hop(group, way, step, kind):
        block = block_at(group, way, step - 1)
        copy = send(
            ring_kv.at[block, kind], ring_kv.at[block, kind],
            z_send.at[group, way, step - 1, kind], z_recv.at[group, way, step - 1, kind],
            ways[way],
        )
        sent.append(copy)
        return copy

    def shift(way, step, kind):
        block = block_at(0, way, min(step, 3))
        copy = send(
            ring_kv.at[block, kind], ring_kv.at[NZ + block, kind],
            y_send.at[way, step, kind], y_recv.at[way, step, kind],
            corners[way] if step == 4 else later,
        )
        sent.append(copy)
        return copy

    def settle(kind):
        src, cols, rows = ((q_in, q_cols, q_rows), (g_in, g_cols, g_rows))[kind]
        own[2 + kind].wait()
        for copy in wide[kind]:
            copy.wait()
        low = lax.broadcasted_iota(jnp.int32, (HD, ROWS), 1) < SPAN

        @pl.loop(0, 8)
        def _(index):
            block = lax.div(index, 4)
            pair = lax.rem(index, 4)
            lanes = pl.ds(pl.multiple_of(pair * ROWS, ROWS), ROWS)
            first = src[block, 2 * pair].astype(F32)
            second = src[block, 2 * pair + 1].astype(F32)
            halves = (
                jnp.where(low, first, pltpu.roll(second, SPAN, 1)),
                jnp.where(low, pltpu.roll(first, SPAN, 1), second),
            )
            for half in range(2):
                cols[2 * block + half, :, lanes] = halves[half].astype(BF16)
                rows[2 * block + half, lanes, :] = halves[half].T.astype(BF16)

        outs = ((q_cols_out, q_rows_out), (g_cols_out, g_rows_out))[kind]
        for index, (src, dst) in enumerate(zip((cols, rows), outs)):
            copy = pltpu.make_async_copy(src, dst, out_sem.at[kind, index])
            copy.start()
            own.append(copy)

    near = {}
    self_shift = {}
    for kind in range(2):
        for way in range(2):
            near[way, 1, kind] = hop(0, way, 1, kind)
        self_shift[kind] = shift(0, 0, kind)
    keep(z, 0)
    heads = pl.ds((x * 2 + core) * GROUP, GROUP)
    for kind, (src, dst) in enumerate(((q, q_in), (g, g_in))):
        copy = pltpu.make_async_copy(
            src.at[heads], dst.at[core, :, here], own_sem.at[2 + kind]
        )
        copy.start()
        own.append(copy)
    wide = ([], [])
    relays = []
    for kind, src in enumerate((q, g)):
        relays.append(
            send(
                src.at[pl.ds(lax.rem(x + 2, NX) * 2 * GROUP, 2 * GROUP)], relay.at[kind],
                relay_sem.at[0, kind], relay_sem.at[1, kind], peer(3 if kind else 1, 0),
            )
        )
    for kind, (src, dst) in enumerate(((q, q_in), (g, g_in))):
        for index, (dx, dc) in enumerate(peers):
            if dx == 2:
                continue
            head = lax.rem(x + dx, NX) * 2 + lax.rem(core + dc, 2)
            wide[kind].append(
                send(
                    src.at[pl.ds(head * GROUP, GROUP)],
                    dst.at[core, :, here],
                    x_send.at[2 + kind, index],
                    x_recv.at[2 + kind, index],
                    peer(dx, dc),
                )
            )
    def forward(kind):
        relays[kind].wait_recv()
        from_x = lax.rem(x + (1 if kind else 3), NX)
        there = pl.ds(pl.multiple_of(from_x * 32, 32), 32)
        for index, (dx, dc) in enumerate(peers):
            if dx != 2:
                continue
            head = pl.ds(lax.rem(core + dc, 2) * GROUP, GROUP)
            wide[kind].append(
                send(
                    relay.at[kind, head],
                    (q_in, g_in)[kind].at[core, :, there],
                    x_send.at[2 + kind, index],
                    x_recv.at[2 + kind, index],
                    peer(3 if kind else 1, dc),
                )
            )

    far_shift = {}
    for step in range(1, 4):
        for kind in range(2):
            for way in range(2):
                near[way, step, kind].wait_recv()
                if step < 3 or kind == way:
                    near[way, step + 1, kind] = hop(0, way, step + 1, kind)
                if step == 3 and kind == way:
                    far_shift[way, 4] = shift(way, 4, way)
                if step == 2 or (step == 1 and kind == way):
                    far_shift[way, step, kind] = shift(way, step, kind)
        for way in range(2):
            keep(block_at(0, way, step), 1 + 2 * step + way)
        if step == 1:
            forward(0)
            forward(1)
    hops = {}
    for kind in range(2):
        self_shift[kind].wait_recv()
        hops[1 - kind, 1, kind] = hop(1, 1 - kind, 1, kind)
    keep(NZ + z, 1)
    for kind in range(2):
        for way in range(2):
            far_shift[way, 2, kind].wait_recv()
            hops[way, 3, kind] = hop(1, way, 3, kind)
    for way in range(2):
        keep(block_at(1, way, 2), 9 + way)
    settle(0)
    settle(1)
    for way in range(2):
        near[way, 4, way].wait_recv()
    keep(block_at(0, 0, 4), 2)
    for step in (1, 3):
        for way in range(2):
            for kind in range(2):
                arriving = far_shift if step == 1 and kind == way else hops
                arriving[way, step, kind].wait_recv()
            keep(block_at(1, way, step), 10 + step + way)
    for way in range(2):
        far_shift[way, 4].wait_recv()
    keep(block_at(1, 0, 4), 15)
    for copy in sent + relays:
        copy.wait_send()
    for copy in keeps:
        copy.wait()
    for copy in own[4:]:
        copy.wait()


def bring(q, k, v, g):
    return pl.pallas_call(
        bring_kernel,
        out_shape=(
            jax.ShapeDtypeStruct((4, HD, LANES), BF16),
            jax.ShapeDtypeStruct((4, HD, LANES), BF16),
            jax.ShapeDtypeStruct((4, LANES, HD), BF16),
            jax.ShapeDtypeStruct((4, LANES, HD), BF16),
            jax.ShapeDtypeStruct((2 * NZ, 2, 2 * ROWS, HD), BF16),
        ),
        in_specs=[HBM] * 4,
        out_specs=(HBM,) * 5,
        scratch_shapes=[
            pltpu.VMEM((4, HD, LANES), BF16),
            pltpu.VMEM((4, HD, LANES), BF16),
            pltpu.VMEM((4, LANES, HD), BF16),
            pltpu.VMEM((4, LANES, HD), BF16),
            pltpu.SemaphoreType.DMA((2, 2)),
            pltpu.VMEM((2, GROUP, HD, ROWS), BF16),
            pltpu.VMEM((2, GROUP, HD, ROWS), BF16),
            pltpu.VMEM((2, 2, HD, ROWS), BF16),
            pltpu.VMEM((2 * NZ, 2, 2 * ROWS, HD), BF16),
            pltpu.VMEM((2, 2 * GROUP, HD // NX, ROWS), BF16),
            pltpu.SemaphoreType.DMA((2, 2)),
            pltpu.SemaphoreType.DMA((4,)),
            pltpu.SemaphoreType.DMA((16,)),
            pltpu.SemaphoreType.DMA((4, 8)),
            pltpu.SemaphoreType.DMA((4, 8)),
            pltpu.SemaphoreType.DMA((2, 5, 2)),
            pltpu.SemaphoreType.DMA((2, 5, 2)),
            pltpu.SemaphoreType.DMA((2, 2, 4, 2)),
            pltpu.SemaphoreType.DMA((2, 2, 4, 2)),
        ],
        compiler_params=pltpu.CompilerParams(
            collective_id=0, has_side_effects=True, vmem_limit_bytes=60 << 20
        ),
        name="bring",
    )(q, k, v, g)


def attend_kernel(
    order_in, docs_in, q_cols_in, g_cols_in, q_rows_in, g_rows_in, kv_in, attn_out, dq_out, dkv,
    order, docs, q_cols, g_cols, q_rows, g_rows, attn, dq, kv, scores, key_acc, value_acc, out_acc, tops, sums, shift, dots,
    pos_rows, start_rows, item_list, span_list, in_sem, out_sem,
):
    outer = lax.axis_index("outer")
    chip = lax.div(lax.axis_index("inner"), 2)
    loads = [
        pltpu.make_async_copy(order_in, order, in_sem.at[0]),
        pltpu.make_async_copy(docs_in, docs, in_sem.at[1]),
        pltpu.make_async_copy(q_cols_in, q_cols, in_sem.at[2]),
        pltpu.make_async_copy(kv_in.at[:, 0], kv.at[pl.ds(0, 2 * NZ), 0], in_sem.at[3]),
        pltpu.make_async_copy(kv_in.at[:, 1], kv.at[pl.ds(0, 2 * NZ), 1], in_sem.at[4]),
        pltpu.make_async_copy(g_cols_in, g_cols, in_sem.at[5]),
        pltpu.make_async_copy(q_rows_in, q_rows, in_sem.at[6]),
        pltpu.make_async_copy(g_rows_in, g_rows, in_sem.at[7]),
    ]
    for load in loads:
        load.start()
    kv[2 * NZ] = jnp.zeros((2, 4, SPAN, HD), BF16)
    tops[...] = jnp.full_like(tops, NEG)
    sums[...] = jnp.zeros_like(sums)
    loads[0].wait()
    loads[1].wait()
    doc = docs[...]
    starts = [
        jnp.sum(jnp.where(doc < d, 1.0, 0.0)).astype(jnp.int32) for d in range(1, 4)
    ]

    def start_of(position):
        found = jnp.zeros_like(position)
        for start in starts:
            found = jnp.where(position >= start, jnp.maximum(found, start), found)
        return found

    iota_lanes = lax.rem(lax.broadcasted_iota(jnp.int32, (8, ROWS), 1), SPAN)
    lows = []
    highs = []
    for unit in range(4):
        query_span = order[outer * 32 + chip * 4 + unit]
        lows.append(lax.div(start_of(query_span * SPAN), SPAN))
        highs.append(query_span)
        query_pos = query_span * SPAN + iota_lanes
        pos_rows[unit] = query_pos
        start_rows[unit] = start_of(query_pos)

    counts = tuple(jnp.int32(unit * 128) for unit in range(4))
    for group in range(2):
        stored = lax.rem(outer + 4 - group, 4) * 32

        def note(step, counts):
            for part in range(8):
                slot = step * 8 + part
                span = order[stored + slot]
                entry = span * (2 * SPAN) + (group * 32 + slot)
                new = []
                for unit in range(4):
                    span_list[counts[unit]] = entry
                    allowed = (span >= lows[unit]) & (span <= highs[unit])
                    new.append(counts[unit] + jnp.where(allowed, 1, 0))
                counts = tuple(new)
            nothing = jnp.zeros((8, SPAN, HD), F32)
            rows = pl.ds((group * 4 + step) * 8, 8)
            key_acc[rows] = nothing
            value_acc[rows] = nothing
            flat = pl.ds(pl.multiple_of(step * 32, 32), 32)
            for unit in range(2 * group, 2 * group + 2):
                out_acc[unit, flat, :] = jnp.zeros((32, LANES), F32)
                dq[unit, flat, :] = jnp.zeros((32, LANES), F32)
            return counts

        counts = lax.fori_loop(0, 4, note, counts)
    items = jnp.int32(0)
    for unit in range(4):
        for extra in range(ITEM):
            span_list[counts[unit] + extra] = 2 * FAR + SLOTS
        for chunk in range(SLOTS // ITEM):
            item_list[items + chunk] = unit * 128 + chunk * ITEM
        items = items + lax.div(counts[unit] - unit * 128 + ITEM - 1, ITEM)
    blank = 3 * 128 + 72
    for extra in range(ITEM):
        span_list[blank + extra] = 2 * FAR + SLOTS
    for extra in range(4):
        item_list[items + extra] = blank
    steps = lax.div(items + 3, 4)

    iota_keys = (
        lax.broadcasted_iota(jnp.int32, (8, 8, ROWS), 0) * 8
        + lax.broadcasted_iota(jnp.int32, (8, 8, ROWS), 1)
    )

    def entries(item):
        first = item_list[item]
        found = [span_list[first + part] for part in range(ITEM)]
        slots = [lax.rem(entry, 2 * SPAN) for entry in found]
        return lax.div(first, 128), slots, [lax.div(a - b, 2) for a, b in zip(found, slots)]

    def spans(slots, kind):
        parts = []
        for slot in slots:
            parts.append(kv[lax.div(slot, 4), kind, lax.rem(slot, 4)])
        return jnp.concatenate(parts, axis=0)

    sides = [pl.ds(side * 256, 256) for side in range(2)]
    loads[2].wait()
    loads[3].wait()

    @functools.partial(lax.fori_loop, 0, steps, init_val=0)
    def _(step, _):
        results = []
        for item in [4 * step + part for part in range(4)]:
            unit, slots, bases = entries(item)
            keys = spans(slots, 0)
            biases = []
            for base in bases:
                allowed = (iota_keys <= (pos_rows[unit] - base)[None]) & (
                    iota_keys >= (start_rows[unit] - base)[None]
                )
                biases.append(jnp.where(allowed, 0.0, NEG).reshape(SPAN, ROWS))
            bias = jnp.concatenate(biases, axis=0)
            bias = jnp.concatenate([bias, bias], axis=1)
            for lanes in sides:
                tile = jnp.dot(keys, q_cols[unit, :, lanes], preferred_element_type=F32)
                tile = tile * (SCALE * LOG2E) + bias
                scores[item, :, lanes] = tile
                results.append((unit, lanes, jnp.max(tile.reshape(32, 8, 256), axis=0)))
        for unit, lanes, top in results:
            tops[unit, :, lanes] = jnp.maximum(tops[unit, :, lanes], top)
        return 0

    for unit in range(4):
        shift[unit] = jnp.broadcast_to(jnp.max(tops[unit], axis=0, keepdims=True), (8, LANES))
    loads[4].wait()

    @functools.partial(lax.fori_loop, 0, steps, init_val=0)
    def _(step, _):
        results = []
        for item in [4 * step + part for part in range(4)]:
            unit, slots, _ = entries(item)
            values_t = spans(slots, 1).T
            for lanes in sides:
                logits = scores[item, :, lanes].reshape(32, 8, 256)
                probs = jnp.exp2(logits - shift[unit, :, lanes][None])
                part = jnp.dot(
                    values_t, probs.reshape(256, 256).astype(BF16), preferred_element_type=F32
                )
                results.append((unit, lanes, jnp.sum(probs, axis=0), part))
        for unit, lanes, total, part in results:
            sums[unit, :, lanes] += total
            out_acc[unit, :, lanes] += part
        return 0

    for load in loads[5:]:
        load.wait()
    for unit in range(4):
        row_sum = jnp.sum(sums[unit], axis=0, keepdims=True)
        out = (out_acc[unit] * (1.0 / row_sum)).astype(BF16)
        attn[unit] = out
        row_dot = jnp.sum(
            out.astype(F32) * g_cols[unit].astype(F32), axis=0, keepdims=True
        )
        dots[unit] = jnp.broadcast_to(row_dot, (8, LANES))
        shift[unit] = shift[unit] + jnp.log(row_sum) * LOG2E
    attn_store = pltpu.make_async_copy(attn, attn_out, out_sem.at[2 * NZ])
    attn_store.start()

    @functools.partial(lax.fori_loop, 0, steps, init_val=0)
    def _(step, _):
        results = []
        for item in [4 * step + part for part in range(4)]:
            unit, slots, _ = entries(item)
            keys_t = spans(slots, 0).T
            values = spans(slots, 1)
            probs_b = []
            score_grads = []
            for lanes in sides:
                logits = scores[item, :, lanes].reshape(32, 8, 256)
                probs = jnp.exp2(logits - shift[unit, :, lanes][None])
                steep = jnp.dot(values, g_cols[unit, :, lanes], preferred_element_type=F32)
                steep = probs * (steep.reshape(32, 8, 256) - dots[unit, :, lanes][None])
                probs_b.append(probs.reshape(256, 256).astype(BF16))
                score_grads.append(steep.reshape(256, 256).astype(BF16))
            probs_b = jnp.concatenate(probs_b, axis=1)
            score_grads = jnp.concatenate(score_grads, axis=1)
            to_values = jnp.dot(probs_b, g_rows[unit], preferred_element_type=F32)
            to_keys = jnp.dot(score_grads, q_rows[unit], preferred_element_type=F32)
            to_query = jnp.dot(keys_t, score_grads, preferred_element_type=F32)
            results.append((slots, unit, to_values, to_keys, to_query))
        for slots, unit, to_values, to_keys, to_query in results:
            dq[unit] += to_query
            for acc, part in ((key_acc, to_keys), (value_acc, to_values)):
                sums_of = [
                    acc[slot] + part[index * SPAN : (index + 1) * SPAN]
                    for index, slot in enumerate(slots)
                ]
                for slot, total in zip(slots, sums_of):
                    acc[slot] = total
        return 0

    dq_store = pltpu.make_async_copy(dq, dq_out, out_sem.at[2 * NZ + 1])
    dq_store.start()
    stores = [attn_store, dq_store]
    for index in range(2 * NZ):
        for part in range(4):
            kv[index, 0, part] = (key_acc[index * 4 + part] * SCALE).astype(BF16)
            kv[index, 1, part] = value_acc[index * 4 + part].astype(BF16)
        store = pltpu.make_async_copy(kv.at[index], dkv.at[index], out_sem.at[index])
        store.start()
        stores.append(store)
    for store in stores:
        store.wait()


def attend(order, docs, q_cols, g_cols, q_rows, g_rows, kv):
    return pl.pallas_call(
        attend_kernel,
        out_shape=(
            jax.ShapeDtypeStruct((4, HD, LANES), BF16),
            jax.ShapeDtypeStruct((4, HD, LANES), F32),
            jax.ShapeDtypeStruct((2 * NZ, 2, 4, SPAN, HD), BF16),
        ),
        in_specs=[HBM] * 7,
        out_specs=(HBM,) * 3,
        scratch_shapes=[
            pltpu.SMEM((2 * SLOTS,), jnp.int32),
            pltpu.VMEM((SLOTS, ROWS), jnp.int32),
            pltpu.VMEM((4, HD, LANES), BF16),
            pltpu.VMEM((4, HD, LANES), BF16),
            pltpu.VMEM((4, LANES, HD), BF16),
            pltpu.VMEM((4, LANES, HD), BF16),
            pltpu.VMEM((4, HD, LANES), BF16),
            pltpu.VMEM((4, HD, LANES), F32),
            pltpu.VMEM((2 * NZ + 1, 2, 4, SPAN, HD), BF16),
            pltpu.VMEM((4 * SLOTS // ITEM, ITEM * SPAN, LANES), F32),
            pltpu.VMEM((SLOTS + 1, SPAN, HD), F32),
            pltpu.VMEM((SLOTS + 1, SPAN, HD), F32),
            pltpu.VMEM((4, HD, LANES), F32),
            pltpu.VMEM((4, 8, LANES), F32),
            pltpu.VMEM((4, 8, LANES), F32),
            pltpu.VMEM((4, 8, LANES), F32),
            pltpu.VMEM((4, 8, LANES), F32),
            pltpu.VMEM((4, 8, ROWS), jnp.int32),
            pltpu.VMEM((4, 8, ROWS), jnp.int32),
            pltpu.SMEM((80,), jnp.int32),
            pltpu.SMEM((512,), jnp.int32),
            pltpu.SemaphoreType.DMA((8,)),
            pltpu.SemaphoreType.DMA((2 * NZ + 2,)),
        ],
        compiler_params=pltpu.CompilerParams(vmem_limit_bytes=60 << 20),
        cost_estimate=pl.CostEstimate(
            flops=6 * 2 * 2048 * 2048 * HD, bytes_accessed=12 << 20, transcendentals=2048 * 2048
        ),
        name="attend",
    )(order, docs, q_cols, g_cols, q_rows, g_rows, kv)


def return_kernel(
    attn_in, dq_in, dkv, attn_out, dq_out, dkv_out,
    attn, dq, terms, attn_rows, dq_rows, rows_tmp, landed, final, pair_send, pair_recv, own_sem, l_send, l_recv,
):
    x, y, z, core = place()
    sibling = where_is(x, y, z, 1 - core)
    up = where_is(x, y, lax.rem(z + 1, NZ), core)
    down = where_is(x, y, lax.rem(z + NZ - 1, NZ), core)
    later = where_is(x, lax.rem(y + 1, NY), z, core)
    earlier = where_is(x, lax.rem(y + NY - 1, NY), z, core)
    loads = [
        pltpu.make_async_copy(attn_in, attn, own_sem.at[5]),
        pltpu.make_async_copy(dq_in, dq, own_sem.at[6]),
        pltpu.make_async_copy(dkv, terms, own_sem.at[4]),
    ]
    for load in loads:
        load.start()
    greet([sibling, up, down, later, earlier])

    ways = (up, down)
    sent = []

    def at(group, distance, way):
        return group * NZ + lax.rem(z + NZ + distance * (-1 if way else 1), NZ)

    def ship(src, index, partner):
        copy = send(src, landed.at[index], l_send.at[index], l_recv.at[index], partner)
        sent.append(copy)
        return copy

    def add(block, kind, *indices):
        total = terms[block, kind].astype(F32)
        for index in indices:
            total = total + landed[index].astype(F32)
        terms[block, kind] = total.astype(BF16)

    flying = {}
    for step, distance in ((0, 3), (1, 1)):
        for kind in range(2):
            for way in range(2):
                if step == 1 and kind == way:
                    continue
                flying["z", step, way, kind] = ship(
                    dkv.at[at(1, distance, way), kind], step * 4 + way * 2 + kind, ways[way]
                )
        if step == 0:
            for kind in range(2):
                flying["y", 4, kind] = ship(dkv.at[at(1, 4, 0), kind], 8 + kind, earlier)
    swaps = []
    own = []

    def turn(block):
        for half in range(2):
            unit = 2 * block + half
            rows = pl.ds(half * LANES, LANES)
            for source, scale, target in ((attn, None, rows_tmp), (dq, SCALE, dq_rows.at[block, rows])):
                for pair in range(4):
                    tile = source[unit, :, pair * ROWS : (pair + 1) * ROWS].astype(F32)
                    tile = tile.T if scale is None else (tile * scale).T
                    for part in range(2):
                        target[pl.ds(2 * pair + part, SPAN, stride=GROUP), :] = tile[
                            part * SPAN : (part + 1) * SPAN
                        ]
                if scale is None:
                    attn_rows[block, rows, :] = rows_tmp[...].astype(BF16)

    def swap():
        turn(1 - core)
        for kind, (src, dst) in enumerate(((attn_rows, attn_out), (dq_rows, dq_out))):
            swaps.append(
                send(src.at[1 - core], dst.at[core], pair_send.at[kind], pair_recv.at[kind], sibling)
            )

    def stay():
        turn(core)
        for kind, (src, dst) in enumerate(((attn_rows, attn_out), (dq_rows, dq_out))):
            copy = pltpu.make_async_copy(src.at[core], dst.at[core], own_sem.at[kind])
            copy.start()
            own.append(copy)

    loads[2].wait()
    for kind in range(2):
        for way in range(2):
            flying["z", 0, way, kind].wait_recv()
            block = at(1, 2, way)
            add(block, kind, way * 2 + kind)
            flying["y", 2, way, kind] = ship(
                terms.at[block, kind], 10 + way * 2 + kind, earlier
            )
    for way in range(2):
        flying["y", 1, way] = ship(dkv.at[at(1, 1, way), way], 30 + way, earlier)
    for way in range(2):
        flying["y", 4, way].wait_recv()
        block = at(0, 4, 0)
        add(block, way, 8 + way)
        flying["s", 1, way, way] = ship(terms.at[block, way], 16 + way, ways[way])
    for way in range(2):
        kind = 1 - way
        flying["s", 2, way, kind] = ship(
            terms.at[at(0, 3, way), kind], 18 + way * 2 + kind, ways[way]
        )
    loads[0].wait()
    loads[1].wait()
    swap()
    for way in range(2):
        flying["s", 1, way, way].wait_recv()
        add(at(0, 3, way), way, 16 + way)
        flying["s", 2, way, way] = ship(
            terms.at[at(0, 3, way), way], 18 + way * 2 + way, ways[way]
        )
    for kind in range(2):
        way = 1 - kind
        flying["z", 1, way, kind].wait_recv()
        add(NZ + z, kind, 4 + way * 2 + kind)
        flying["y", 0, kind] = ship(terms.at[NZ + z, kind], 14 + kind, earlier)
    for step in (3, 4):
        for turn_of in range(2):
            for way in range(2):
                kind = turn_of if way else 1 - turn_of
                flying["s", step - 1, way, kind].wait_recv()
                indices = [18 + (step - 3) * 4 + way * 2 + kind]
                if step == 3:
                    flying["y", 2, way, kind].wait_recv()
                    indices.append(10 + way * 2 + kind)
                elif kind == way:
                    flying["y", 1, way].wait_recv()
                    indices.append(30 + way)
                block = at(0, 5 - step, way)
                add(block, kind, *indices)
                flying["s", step, way, kind] = ship(
                    terms.at[block, kind], 18 + (step - 2) * 4 + way * 2 + kind, ways[way]
                )
        if step == 3:
            stay()
    for kind in range(2):
        flying["y", 0, kind].wait_recv()
        for way in range(2):
            flying["s", 4, way, kind].wait_recv()
        total = terms[z, kind].astype(F32)
        for index in (14 + kind, 26 + kind, 28 + kind):
            total = total + landed[index].astype(F32)
        final[kind] = total
    mine = pl.ds(pl.multiple_of(core * ROWS, ROWS), ROWS)
    other = pl.ds(pl.multiple_of((1 - core) * ROWS, ROWS), ROWS)
    for kind in range(2):
        swaps.append(
            send(
                final.at[kind, other], dkv_out.at[kind, core],
                pair_send.at[2 + kind], pair_recv.at[2 + kind], sibling,
            )
        )
        copy = pltpu.make_async_copy(
            final.at[kind, mine], dkv_out.at[kind, core], own_sem.at[2 + kind]
        )
        copy.start()
        own.append(copy)
    for copy in sent:
        copy.wait_send()
    for copy in swaps:
        copy.wait()
    for copy in own:
        copy.wait()


def give_back(attn, dq, dkv):
    return pl.pallas_call(
        return_kernel,
        out_shape=(
            jax.ShapeDtypeStruct((2, ROWS * GROUP, HD), BF16),
            jax.ShapeDtypeStruct((2, ROWS * GROUP, HD), F32),
            jax.ShapeDtypeStruct((2, 2, ROWS, HD), F32),
        ),
        in_specs=[HBM] * 3,
        out_specs=(HBM,) * 3,
        scratch_shapes=[
            pltpu.VMEM((4, HD, LANES), BF16),
            pltpu.VMEM((4, HD, LANES), F32),
            pltpu.VMEM((2 * NZ, 2, 2 * ROWS, HD), BF16),
            pltpu.VMEM((2, ROWS * GROUP, HD), BF16),
            pltpu.VMEM((2, ROWS * GROUP, HD), F32),
            pltpu.VMEM((LANES, HD), F32),
            pltpu.VMEM((32, 2 * ROWS, HD), BF16),
            pltpu.VMEM((2, 2 * ROWS, HD), F32),
            pltpu.SemaphoreType.DMA((4,)),
            pltpu.SemaphoreType.DMA((4,)),
            pltpu.SemaphoreType.DMA((7,)),
            pltpu.SemaphoreType.DMA((32,)),
            pltpu.SemaphoreType.DMA((32,)),
        ],
        compiler_params=pltpu.CompilerParams(
            collective_id=1, has_side_effects=True, vmem_limit_bytes=60 << 20
        ),
        name="give_back",
    )(attn, dq, dkv)


def finish_kernel(
    attn, dq, dkv, attn_out, dq_out, dk_out, dv_out, halves, joined, wide, wide_joined, parts, dk, dv, sem
):
    loads = [
        pltpu.make_async_copy(dkv, parts, sem.at[0]),
        pltpu.make_async_copy(attn, halves, sem.at[1]),
        pltpu.make_async_copy(dq, wide, sem.at[2]),
    ]
    for load in loads:
        load.start()
    stores = []
    loads[0].wait()
    for kind, (rows, dst) in enumerate(((dk, dk_out), (dv, dv_out))):
        for half in range(2):
            rows[pl.ds(half, ROWS, stride=2), :] = parts[kind, half]
        store = pltpu.make_async_copy(rows, dst, sem.at[4 + kind])
        store.start()
        stores.append(store)
    loads[1].wait()
    both = [halves[half].astype(F32).reshape(ROWS, GROUP, HD) for half in range(2)]
    joined[...] = jnp.concatenate(both, axis=1).astype(BF16)
    store = pltpu.make_async_copy(joined, attn_out, sem.at[6])
    store.start()
    stores.append(store)
    loads[2].wait()
    wide_joined[...] = jnp.concatenate(
        [wide[half].reshape(ROWS, GROUP, HD) for half in range(2)], axis=1
    )
    store = pltpu.make_async_copy(wide_joined, dq_out, sem.at[3])
    store.start()
    stores.append(store)
    for store in stores:
        store.wait()


def finish(attn, dq, dkv):
    return pl.pallas_call(
        finish_kernel,
        out_shape=(
            jax.ShapeDtypeStruct((ROWS, 2 * GROUP, HD), BF16),
            jax.ShapeDtypeStruct((ROWS, 2 * GROUP, HD), F32),
            jax.ShapeDtypeStruct((2 * ROWS, HD), F32),
            jax.ShapeDtypeStruct((2 * ROWS, HD), F32),
        ),
        in_specs=[HBM] * 3,
        out_specs=(HBM,) * 4,
        scratch_shapes=[
            pltpu.VMEM((2, ROWS * GROUP, HD), BF16),
            pltpu.VMEM((ROWS, 2 * GROUP, HD), BF16),
            pltpu.VMEM((2, ROWS * GROUP, HD), F32),
            pltpu.VMEM((ROWS, 2 * GROUP, HD), F32),
            pltpu.VMEM((2, 2, ROWS, HD), F32),
            pltpu.VMEM((2 * ROWS, HD), F32),
            pltpu.VMEM((2 * ROWS, HD), F32),
            pltpu.SemaphoreType.DMA((7,)),
        ],
        compiler_params=pltpu.CompilerParams(vmem_limit_bytes=60 << 20),
        cost_estimate=pl.CostEstimate(flops=0, bytes_accessed=4 << 20, transcendentals=0),
        name="finish",
    )(attn, dq, dkv)


def local(queries, keys, values, grad_out, span_order, doc_ids):
    turned = [jnp.transpose(a, (1, 2, 0)) for a in (queries, keys, values, grad_out)]
    q_cols, g_cols, q_rows, g_rows, kv = bring(*turned)
    kv = kv.reshape(2 * NZ, 2, 4, SPAN, HD)
    attn, dq, dkv = attend(
        span_order, doc_ids.reshape(SLOTS, ROWS), q_cols, g_cols, q_rows, g_rows, kv
    )
    attn, dq, dkv = give_back(attn, dq, dkv.reshape(2 * NZ, 2, 2 * ROWS, HD))
    attn, dq, dk, dv = finish(attn, dq, dkv)
    return (attn, dq, dk.reshape(ROWS, 2, HD), dv.reshape(ROWS, 2, HD))


def solution(mesh):
    entry = P(("outer", "inner"), None, "head")
    leave = P(("outer", "inner"), "head", None)
    return jax.shard_map(
        local,
        mesh=mesh,
        in_specs=(entry, entry, entry, entry, P(), P()),
        out_specs=(leave, leave, leave, leave),
        check_vma=False,
    )
```

```python
import functools
import math

import jax
import jax.numpy as jnp
from jax import lax
from jax.experimental import pallas as pl
from jax.experimental.pallas import tpu as pltpu
from jax.sharding import PartitionSpec as P

MESH = pl.DeviceIdType.MESH
HBM = pl.BlockSpec(memory_space=pltpu.HBM)
NEG = -1e30
FAR = 1 << 24
NX = 4
NY = 4
NZ = 8
HD = 128
ROWS = 128
SPAN = 64
GROUP = 8
SLOTS = 64
LANES = GROUP * SPAN
SCALE = 1.0 / math.sqrt(HD)
LOG2E = math.log2(math.e)
ITEM = 4
BF16 = jnp.bfloat16
F32 = jnp.float32


def place():
    inner = lax.axis_index("inner")
    return (
        lax.axis_index("head"),
        lax.axis_index("outer"),
        lax.div(inner, 2),
        lax.rem(inner, 2),
    )


def where_is(x, y, z, core):
    return {"head": x, "outer": y, "inner": z * 2 + core}


def greet(partners):
    barrier = pltpu.get_barrier_semaphore()
    for partner in partners:
        pl.semaphore_signal(barrier, inc=1, device_id=partner, device_id_type=MESH)
    pl.semaphore_wait(barrier, len(partners))


def send(src, dst, send_sem, recv_sem, partner):
    copy = pltpu.make_async_remote_copy(
        src_ref=src,
        dst_ref=dst,
        send_sem=send_sem,
        recv_sem=recv_sem,
        device_id=partner,
        device_id_type=MESH,
    )
    copy.start()
    return copy


def bring_kernel(
    q, k, v, g, q_cols_out, g_cols_out, q_rows_out, g_rows_out, kv_out,
    q_cols, g_cols, q_rows, g_rows, out_sem, q_in, g_in, kv_in, ring_kv, relay, relay_sem, own_sem, keep_sem, x_send, x_recv, y_send, y_recv, z_send, z_recv,
):
    x, y, z, core = place()
    peers = [(dx, dc) for dx in range(NX) for dc in range(2) if (dx, dc) != (0, 0)]

    def peer(dx, dc):
        return where_is(lax.rem(x + dx, NX), y, z, lax.rem(core + dc, 2))

    up = where_is(x, y, lax.rem(z + 1, NZ), core)
    down = where_is(x, y, lax.rem(z + NZ - 1, NZ), core)
    later = where_is(x, lax.rem(y + 1, NY), z, core)
    earlier = where_is(x, lax.rem(y + NY - 1, NY), z, core)
    up_z, down_z = lax.rem(z + 1, NZ), lax.rem(z + NZ - 1, NZ)
    later_y, earlier_y = lax.rem(y + 1, NY), lax.rem(y + NY - 1, NY)
    corners = (where_is(x, later_y, up_z, core), where_is(x, later_y, down_z, core))
    behind = [where_is(x, earlier_y, up_z, core), where_is(x, earlier_y, down_z, core)]
    greet([peer(*p) for p in peers] + [up, down, later, earlier, *corners, *behind])

    here = pl.ds(pl.multiple_of(x * 32, 32), 32)
    copies = []
    own = []
    for index, (dx, dc) in enumerate([(0, 0)] + peers):
        head = lax.rem(x + dx, NX) * 2 + lax.rem(core + dc, 2)
        for kind, src in enumerate((k, v)):
            dst = kv_in.at[kind, core, here]
            if index == 0:
                copy = pltpu.make_async_copy(src.at[head], dst, own_sem.at[kind])
                copy.start()
                own.append(copy)
            else:
                copies.append(
                    send(src.at[head], dst, x_send.at[kind, index], x_recv.at[kind, index], peer(dx, dc))
                )
    own[0].wait()
    own[1].wait()
    for copy in copies:
        copy.wait()
    for kind in range(2):
        for block in range(2):
            ring_kv[z, kind, block * ROWS : (block + 1) * ROWS, :] = (
                kv_in[kind, block].astype(F32).T.astype(BF16)
            )
    keeps = []
    sent = []
    ways = (up, down)

    def block_at(group, way, step):
        return group * NZ + lax.rem(z + NZ + step * (1 if way else -1), NZ)

    def keep(block, index):
        copy = pltpu.make_async_copy(ring_kv.at[block], kv_out.at[block], keep_sem.at[index])
        copy.start()
        keeps.append(copy)

    def hop(group, way, step, kind):
        block = block_at(group, way, step - 1)
        copy = send(
            ring_kv.at[block, kind], ring_kv.at[block, kind],
            z_send.at[group, way, step - 1, kind], z_recv.at[group, way, step - 1, kind],
            ways[way],
        )
        sent.append(copy)
        return copy

    def shift(way, step, kind):
        block = block_at(0, way, min(step, 3))
        copy = send(
            ring_kv.at[block, kind], ring_kv.at[NZ + block, kind],
            y_send.at[way, step, kind], y_recv.at[way, step, kind],
            corners[way] if step == 4 else later,
        )
        sent.append(copy)
        return copy

    def settle(kind):
        src, cols, rows = ((q_in, q_cols, q_rows), (g_in, g_cols, g_rows))[kind]
        own[2 + kind].wait()
        for copy in wide[kind]:
            copy.wait()
        low = lax.broadcasted_iota(jnp.int32, (HD, ROWS), 1) < SPAN

        @pl.loop(0, 8)
        def _(index):
            block = lax.div(index, 4)
            pair = lax.rem(index, 4)
            lanes = pl.ds(pl.multiple_of(pair * ROWS, ROWS), ROWS)
            first = src[block, 2 * pair].astype(F32)
            second = src[block, 2 * pair + 1].astype(F32)
            halves = (
                jnp.where(low, first, pltpu.roll(second, SPAN, 1)),
                jnp.where(low, pltpu.roll(first, SPAN, 1), second),
            )
            for half in range(2):
                cols[2 * block + half, :, lanes] = halves[half].astype(BF16)
                rows[2 * block + half, lanes, :] = halves[half].T.astype(BF16)

        outs = ((q_cols_out, q_rows_out), (g_cols_out, g_rows_out))[kind]
        for index, (src, dst) in enumerate(zip((cols, rows), outs)):
            copy = pltpu.make_async_copy(src, dst, out_sem.at[kind, index])
            copy.start()
            own.append(copy)

    near = {}
    self_shift = {}
    for kind in range(2):
        for way in range(2):
            near[way, 1, kind] = hop(0, way, 1, kind)
        self_shift[kind] = shift(0, 0, kind)
    keep(z, 0)
    heads = pl.ds((x * 2 + core) * GROUP, GROUP)
    for kind, (src, dst) in enumerate(((q, q_in), (g, g_in))):
        copy = pltpu.make_async_copy(
            src.at[heads], dst.at[core, :, here], own_sem.at[2 + kind]
        )
        copy.start()
        own.append(copy)
    wide = ([], [])
    relays = []
    for kind, src in enumerate((q, g)):
        relays.append(
            send(
                src.at[pl.ds(lax.rem(x + 2, NX) * 2 * GROUP, 2 * GROUP)], relay.at[kind],
                relay_sem.at[0, kind], relay_sem.at[1, kind], peer(3 if kind else 1, 0),
            )
        )
    for kind, (src, dst) in enumerate(((q, q_in), (g, g_in))):
        for index, (dx, dc) in enumerate(peers):
            if dx == 2:
                continue
            head = lax.rem(x + dx, NX) * 2 + lax.rem(core + dc, 2)
            wide[kind].append(
                send(
                    src.at[pl.ds(head * GROUP, GROUP)],
                    dst.at[core, :, here],
                    x_send.at[2 + kind, index],
                    x_recv.at[2 + kind, index],
                    peer(dx, dc),
                )
            )
    def forward(kind):
        relays[kind].wait_recv()
        from_x = lax.rem(x + (1 if kind else 3), NX)
        there = pl.ds(pl.multiple_of(from_x * 32, 32), 32)
        for index, (dx, dc) in enumerate(peers):
            if dx != 2:
                continue
            head = pl.ds(lax.rem(core + dc, 2) * GROUP, GROUP)
            wide[kind].append(
                send(
                    relay.at[kind, head],
                    (q_in, g_in)[kind].at[core, :, there],
                    x_send.at[2 + kind, index],
                    x_recv.at[2 + kind, index],
                    peer(3 if kind else 1, dc),
                )
            )

    far_shift = {}
    for step in range(1, 4):
        for kind in range(2):
            for way in range(2):
                near[way, step, kind].wait_recv()
                if step < 3 or kind == way:
                    near[way, step + 1, kind] = hop(0, way, step + 1, kind)
                if step == 3 and kind == way:
                    far_shift[way, 4] = shift(way, 4, way)
                if step == 2 or (step == 1 and kind == way):
                    far_shift[way, step, kind] = shift(way, step, kind)
        for way in range(2):
            keep(block_at(0, way, step), 1 + 2 * step + way)
        if step == 1:
            forward(0)
            forward(1)
    hops = {}
    for kind in range(2):
        self_shift[kind].wait_recv()
        hops[1 - kind, 1, kind] = hop(1, 1 - kind, 1, kind)
    keep(NZ + z, 1)
    for kind in range(2):
        for way in range(2):
            far_shift[way, 2, kind].wait_recv()
            hops[way, 3, kind] = hop(1, way, 3, kind)
    for way in range(2):
        keep(block_at(1, way, 2), 9 + way)
    settle(0)
    settle(1)
    for way in range(2):
        near[way, 4, way].wait_recv()
    keep(block_at(0, 0, 4), 2)
    for step in (1, 3):
        for way in range(2):
            for kind in range(2):
                arriving = far_shift if step == 1 and kind == way else hops
                arriving[way, step, kind].wait_recv()
            keep(block_at(1, way, step), 10 + step + way)
    for way in range(2):
        far_shift[way, 4].wait_recv()
    keep(block_at(1, 0, 4), 15)
    for copy in sent + relays:
        copy.wait_send()
    for copy in keeps:
        copy.wait()
    for copy in own[4:]:
        copy.wait()


def bring(q, k, v, g):
    return pl.pallas_call(
        bring_kernel,
        out_shape=(
            jax.ShapeDtypeStruct((4, HD, LANES), BF16),
            jax.ShapeDtypeStruct((4, HD, LANES), BF16),
            jax.ShapeDtypeStruct((4, LANES, HD), BF16),
            jax.ShapeDtypeStruct((4, LANES, HD), BF16),
            jax.ShapeDtypeStruct((2 * NZ, 2, 2 * ROWS, HD), BF16),
        ),
        in_specs=[HBM] * 4,
        out_specs=(HBM,) * 5,
        scratch_shapes=[
            pltpu.VMEM((4, HD, LANES), BF16),
            pltpu.VMEM((4, HD, LANES), BF16),
            pltpu.VMEM((4, LANES, HD), BF16),
            pltpu.VMEM((4, LANES, HD), BF16),
            pltpu.SemaphoreType.DMA((2, 2)),
            pltpu.VMEM((2, GROUP, HD, ROWS), BF16),
            pltpu.VMEM((2, GROUP, HD, ROWS), BF16),
            pltpu.VMEM((2, 2, HD, ROWS), BF16),
            pltpu.VMEM((2 * NZ, 2, 2 * ROWS, HD), BF16),
            pltpu.VMEM((2, 2 * GROUP, HD // NX, ROWS), BF16),
            pltpu.SemaphoreType.DMA((2, 2)),
            pltpu.SemaphoreType.DMA((4,)),
            pltpu.SemaphoreType.DMA((16,)),
            pltpu.SemaphoreType.DMA((4, 8)),
            pltpu.SemaphoreType.DMA((4, 8)),
            pltpu.SemaphoreType.DMA((2, 5, 2)),
            pltpu.SemaphoreType.DMA((2, 5, 2)),
            pltpu.SemaphoreType.DMA((2, 2, 4, 2)),
            pltpu.SemaphoreType.DMA((2, 2, 4, 2)),
        ],
        compiler_params=pltpu.CompilerParams(
            collective_id=0, has_side_effects=True, vmem_limit_bytes=60 << 20
        ),
        name="bring",
    )(q, k, v, g)


def attend_kernel(
    order_in, docs_in, q_cols_in, g_cols_in, q_rows_in, g_rows_in, kv_in, attn_out, dq_out, dkv,
    order, docs, q_cols, g_cols, q_rows, g_rows, attn, dq, dq_b, kv, scores, key_acc, value_acc, out_acc, tops, sums, shift, dots,
    pos_rows, start_rows, item_list, span_list, in_sem, out_sem,
):
    outer = lax.axis_index("outer")
    chip = lax.div(lax.axis_index("inner"), 2)
    loads = [
        pltpu.make_async_copy(order_in, order, in_sem.at[0]),
        pltpu.make_async_copy(docs_in, docs, in_sem.at[1]),
        pltpu.make_async_copy(q_cols_in, q_cols, in_sem.at[2]),
        pltpu.make_async_copy(kv_in.at[:, 0], kv.at[pl.ds(0, 2 * NZ), 0], in_sem.at[3]),
        pltpu.make_async_copy(kv_in.at[:, 1], kv.at[pl.ds(0, 2 * NZ), 1], in_sem.at[4]),
        pltpu.make_async_copy(g_cols_in, g_cols, in_sem.at[5]),
        pltpu.make_async_copy(q_rows_in, q_rows, in_sem.at[6]),
        pltpu.make_async_copy(g_rows_in, g_rows, in_sem.at[7]),
    ]
    for load in loads:
        load.start()
    kv[2 * NZ] = jnp.zeros((2, 4, SPAN, HD), BF16)
    tops[...] = jnp.full_like(tops, NEG)
    sums[...] = jnp.zeros_like(sums)
    loads[0].wait()
    loads[1].wait()
    doc = docs[...]
    starts = [
        jnp.sum(jnp.where(doc < d, 1.0, 0.0)).astype(jnp.int32) for d in range(1, 4)
    ]

    def start_of(position):
        found = jnp.zeros_like(position)
        for start in starts:
            found = jnp.where(position >= start, jnp.maximum(found, start), found)
        return found

    iota_lanes = lax.rem(lax.broadcasted_iota(jnp.int32, (8, ROWS), 1), SPAN)
    lows = []
    highs = []
    for unit in range(4):
        query_span = order[outer * 32 + chip * 4 + unit]
        lows.append(lax.div(start_of(query_span * SPAN), SPAN))
        highs.append(query_span)
        query_pos = query_span * SPAN + iota_lanes
        pos_rows[unit] = query_pos
        start_rows[unit] = start_of(query_pos)

    counts = tuple(jnp.int32(unit * 128) for unit in range(4))
    for group in range(2):
        stored = lax.rem(outer + 4 - group, 4) * 32

        def note(step, counts):
            for part in range(8):
                slot = step * 8 + part
                span = order[stored + slot]
                entry = span * (2 * SPAN) + (group * 32 + slot)
                new = []
                for unit in range(4):
                    span_list[counts[unit]] = entry
                    allowed = (span >= lows[unit]) & (span <= highs[unit])
                    new.append(counts[unit] + jnp.where(allowed, 1, 0))
                counts = tuple(new)
            nothing = jnp.zeros((8, SPAN, HD), F32)
            rows = pl.ds((group * 4 + step) * 8, 8)
            key_acc[rows] = nothing
            value_acc[rows] = nothing
            flat = pl.ds(pl.multiple_of(step * 32, 32), 32)
            for unit in range(2 * group, 2 * group + 2):
                out_acc[unit, flat, :] = jnp.zeros((32, LANES), F32)
                dq[unit, flat, :] = jnp.zeros((32, LANES), F32)
            return counts

        counts = lax.fori_loop(0, 4, note, counts)
    items = jnp.int32(0)
    for unit in range(4):
        for extra in range(ITEM):
            span_list[counts[unit] + extra] = 2 * FAR + SLOTS
        for chunk in range(SLOTS // ITEM):
            item_list[items + chunk] = unit * 128 + chunk * ITEM
        items = items + lax.div(counts[unit] - unit * 128 + ITEM - 1, ITEM)
    blank = 3 * 128 + 72
    for extra in range(ITEM):
        span_list[blank + extra] = 2 * FAR + SLOTS
    for extra in range(4):
        item_list[items + extra] = blank
    steps = lax.div(items + 3, 4)

    iota_keys = (
        lax.broadcasted_iota(jnp.int32, (8, 8, ROWS), 0) * 8
        + lax.broadcasted_iota(jnp.int32, (8, 8, ROWS), 1)
    )

    def entries(item):
        first = item_list[item]
        found = [span_list[first + part] for part in range(ITEM)]
        slots = [lax.rem(entry, 2 * SPAN) for entry in found]
        return lax.div(first, 128), slots, [lax.div(a - b, 2) for a, b in zip(found, slots)]

    def spans(slots, kind):
        parts = []
        for slot in slots:
            parts.append(kv[lax.div(slot, 4), kind, lax.rem(slot, 4)])
        return jnp.concatenate(parts, axis=0)

    sides = [pl.ds(side * 256, 256) for side in range(2)]
    loads[2].wait()
    loads[3].wait()

    @functools.partial(lax.fori_loop, 0, steps, init_val=0)
    def _(step, _):
        results = []
        for item in [4 * step + part for part in range(4)]:
            unit, slots, bases = entries(item)
            keys = spans(slots, 0)
            biases = []
            for base in bases:
                allowed = (iota_keys <= (pos_rows[unit] - base)[None]) & (
                    iota_keys >= (start_rows[unit] - base)[None]
                )
                biases.append(jnp.where(allowed, 0.0, NEG).reshape(SPAN, ROWS))
            bias = jnp.concatenate(biases, axis=0)
            bias = jnp.concatenate([bias, bias], axis=1)
            for lanes in sides:
                tile = jnp.dot(keys, q_cols[unit, :, lanes], preferred_element_type=F32)
                tile = tile * (SCALE * LOG2E) + bias
                scores[item, :, lanes] = tile
                results.append((unit, lanes, jnp.max(tile.reshape(32, 8, 256), axis=0)))
        for unit, lanes, top in results:
            tops[unit, :, lanes] = jnp.maximum(tops[unit, :, lanes], top)
        return 0

    for unit in range(4):
        shift[unit] = jnp.broadcast_to(jnp.max(tops[unit], axis=0, keepdims=True), (8, LANES))
    loads[4].wait()

    @functools.partial(lax.fori_loop, 0, steps, init_val=0)
    def _(step, _):
        results = []
        for item in [4 * step + part for part in range(4)]:
            unit, slots, _ = entries(item)
            values_t = spans(slots, 1).T
            for lanes in sides:
                logits = scores[item, :, lanes].reshape(32, 8, 256)
                probs = jnp.exp2(logits - shift[unit, :, lanes][None])
                part = jnp.dot(
                    values_t, probs.reshape(256, 256).astype(BF16), preferred_element_type=F32
                )
                results.append((unit, lanes, jnp.sum(probs, axis=0), part))
        for unit, lanes, total, part in results:
            sums[unit, :, lanes] += total
            out_acc[unit, :, lanes] += part
        return 0

    for load in loads[5:]:
        load.wait()
    for unit in range(4):
        row_sum = jnp.sum(sums[unit], axis=0, keepdims=True)
        out = (out_acc[unit] * (1.0 / row_sum)).astype(BF16)
        attn[unit] = out
        row_dot = jnp.sum(
            out.astype(F32) * g_cols[unit].astype(F32), axis=0, keepdims=True
        )
        dots[unit] = jnp.broadcast_to(row_dot, (8, LANES))
        shift[unit] = shift[unit] + jnp.log(row_sum) * LOG2E
    attn_store = pltpu.make_async_copy(attn, attn_out, out_sem.at[2 * NZ])
    attn_store.start()

    @functools.partial(lax.fori_loop, 0, steps, init_val=0)
    def _(step, _):
        results = []
        for item in [4 * step + part for part in range(4)]:
            unit, slots, _ = entries(item)
            keys_t = spans(slots, 0).T
            values = spans(slots, 1)
            probs_b = []
            score_grads = []
            for lanes in sides:
                logits = scores[item, :, lanes].reshape(32, 8, 256)
                probs = jnp.exp2(logits - shift[unit, :, lanes][None])
                steep = jnp.dot(values, g_cols[unit, :, lanes], preferred_element_type=F32)
                steep = probs * (steep.reshape(32, 8, 256) - dots[unit, :, lanes][None])
                probs_b.append(probs.reshape(256, 256).astype(BF16))
                score_grads.append(steep.reshape(256, 256).astype(BF16))
            probs_b = jnp.concatenate(probs_b, axis=1)
            score_grads = jnp.concatenate(score_grads, axis=1)
            to_values = jnp.dot(probs_b, g_rows[unit], preferred_element_type=F32)
            to_keys = jnp.dot(score_grads, q_rows[unit], preferred_element_type=F32)
            to_query = jnp.dot(keys_t, score_grads, preferred_element_type=F32)
            results.append((slots, unit, to_values, to_keys, to_query))
        for slots, unit, to_values, to_keys, to_query in results:
            dq[unit] += to_query
            for acc, part in ((key_acc, to_keys), (value_acc, to_values)):
                sums_of = [
                    acc[slot] + part[index * SPAN : (index + 1) * SPAN]
                    for index, slot in enumerate(slots)
                ]
                for slot, total in zip(slots, sums_of):
                    acc[slot] = total
        return 0

    dq_b[...] = (dq[...] * SCALE).astype(BF16)
    dq_store = pltpu.make_async_copy(dq_b, dq_out, out_sem.at[2 * NZ + 1])
    dq_store.start()
    stores = [attn_store, dq_store]
    for index in range(2 * NZ):
        for part in range(4):
            kv[index, 0, part] = (key_acc[index * 4 + part] * SCALE).astype(BF16)
            kv[index, 1, part] = value_acc[index * 4 + part].astype(BF16)
        store = pltpu.make_async_copy(kv.at[index], dkv.at[index], out_sem.at[index])
        store.start()
        stores.append(store)
    for store in stores:
        store.wait()


def attend(order, docs, q_cols, g_cols, q_rows, g_rows, kv):
    return pl.pallas_call(
        attend_kernel,
        out_shape=(
            jax.ShapeDtypeStruct((4, HD, LANES), BF16),
            jax.ShapeDtypeStruct((4, HD, LANES), BF16),
            jax.ShapeDtypeStruct((2 * NZ, 2, 4, SPAN, HD), BF16),
        ),
        in_specs=[HBM] * 7,
        out_specs=(HBM,) * 3,
        scratch_shapes=[
            pltpu.SMEM((2 * SLOTS,), jnp.int32),
            pltpu.VMEM((SLOTS, ROWS), jnp.int32),
            pltpu.VMEM((4, HD, LANES), BF16),
            pltpu.VMEM((4, HD, LANES), BF16),
            pltpu.VMEM((4, LANES, HD), BF16),
            pltpu.VMEM((4, LANES, HD), BF16),
            pltpu.VMEM((4, HD, LANES), BF16),
            pltpu.VMEM((4, HD, LANES), F32),
            pltpu.VMEM((4, HD, LANES), BF16),
            pltpu.VMEM((2 * NZ + 1, 2, 4, SPAN, HD), BF16),
            pltpu.VMEM((4 * SLOTS // ITEM, ITEM * SPAN, LANES), F32),
            pltpu.VMEM((SLOTS + 1, SPAN, HD), F32),
            pltpu.VMEM((SLOTS + 1, SPAN, HD), F32),
            pltpu.VMEM((4, HD, LANES), F32),
            pltpu.VMEM((4, 8, LANES), F32),
            pltpu.VMEM((4, 8, LANES), F32),
            pltpu.VMEM((4, 8, LANES), F32),
            pltpu.VMEM((4, 8, LANES), F32),
            pltpu.VMEM((4, 8, ROWS), jnp.int32),
            pltpu.VMEM((4, 8, ROWS), jnp.int32),
            pltpu.SMEM((80,), jnp.int32),
            pltpu.SMEM((512,), jnp.int32),
            pltpu.SemaphoreType.DMA((8,)),
            pltpu.SemaphoreType.DMA((2 * NZ + 2,)),
        ],
        compiler_params=pltpu.CompilerParams(vmem_limit_bytes=60 << 20),
        cost_estimate=pl.CostEstimate(
            flops=6 * 2 * 2048 * 2048 * HD, bytes_accessed=12 << 20, transcendentals=2048 * 2048
        ),
        name="attend",
    )(order, docs, q_cols, g_cols, q_rows, g_rows, kv)


def return_kernel(
    attn_in, dq_in, dkv, attn_out, dq_out, dkv_out,
    attn, dq, terms, attn_rows, dq_rows, rows_tmp, landed, final, pair_send, pair_recv, own_sem, l_send, l_recv,
):
    x, y, z, core = place()
    sibling = where_is(x, y, z, 1 - core)
    up = where_is(x, y, lax.rem(z + 1, NZ), core)
    down = where_is(x, y, lax.rem(z + NZ - 1, NZ), core)
    later = where_is(x, lax.rem(y + 1, NY), z, core)
    earlier = where_is(x, lax.rem(y + NY - 1, NY), z, core)
    loads = [
        pltpu.make_async_copy(attn_in, attn, own_sem.at[5]),
        pltpu.make_async_copy(dq_in, dq, own_sem.at[6]),
        pltpu.make_async_copy(dkv, terms, own_sem.at[4]),
    ]
    for load in loads:
        load.start()
    greet([sibling, up, down, later, earlier])

    ways = (up, down)
    sent = []

    def at(group, distance, way):
        return group * NZ + lax.rem(z + NZ + distance * (-1 if way else 1), NZ)

    def ship(src, index, partner):
        copy = send(src, landed.at[index], l_send.at[index], l_recv.at[index], partner)
        sent.append(copy)
        return copy

    def add(block, kind, *indices):
        total = terms[block, kind].astype(F32)
        for index in indices:
            total = total + landed[index].astype(F32)
        terms[block, kind] = total.astype(BF16)

    flying = {}
    for step, distance in ((0, 3), (1, 1)):
        for kind in range(2):
            for way in range(2):
                if step == 1 and kind == way:
                    continue
                flying["z", step, way, kind] = ship(
                    dkv.at[at(1, distance, way), kind], step * 4 + way * 2 + kind, ways[way]
                )
        if step == 0:
            for kind in range(2):
                flying["y", 4, kind] = ship(dkv.at[at(1, 4, 0), kind], 8 + kind, earlier)
    swaps = []
    own = []

    def turn(block):
        for half in range(2):
            unit = 2 * block + half
            rows = pl.ds(half * LANES, LANES)
            for source, target in ((attn, attn_rows), (dq, dq_rows)):
                for pair in range(4):
                    tile = source[unit, :, pair * ROWS : (pair + 1) * ROWS].astype(F32).T
                    for part in range(2):
                        rows_tmp[pl.ds(2 * pair + part, SPAN, stride=GROUP), :] = tile[
                            part * SPAN : (part + 1) * SPAN
                        ]
                target[block, rows, :] = rows_tmp[...].astype(BF16)

    def swap():
        turn(1 - core)
        for kind, (src, dst) in enumerate(((attn_rows, attn_out), (dq_rows, dq_out))):
            swaps.append(
                send(src.at[1 - core], dst.at[core], pair_send.at[kind], pair_recv.at[kind], sibling)
            )

    def stay():
        turn(core)
        for kind, (src, dst) in enumerate(((attn_rows, attn_out), (dq_rows, dq_out))):
            copy = pltpu.make_async_copy(src.at[core], dst.at[core], own_sem.at[kind])
            copy.start()
            own.append(copy)

    loads[2].wait()
    for kind in range(2):
        for way in range(2):
            flying["z", 0, way, kind].wait_recv()
            block = at(1, 2, way)
            add(block, kind, way * 2 + kind)
            flying["y", 2, way, kind] = ship(
                terms.at[block, kind], 10 + way * 2 + kind, earlier
            )
    for way in range(2):
        flying["y", 1, way] = ship(dkv.at[at(1, 1, way), way], 30 + way, earlier)
    for way in range(2):
        flying["y", 4, way].wait_recv()
        block = at(0, 4, 0)
        add(block, way, 8 + way)
        flying["s", 1, way, way] = ship(terms.at[block, way], 16 + way, ways[way])
    for way in range(2):
        kind = 1 - way
        flying["s", 2, way, kind] = ship(
            terms.at[at(0, 3, way), kind], 18 + way * 2 + kind, ways[way]
        )
    loads[0].wait()
    loads[1].wait()
    swap()
    for way in range(2):
        flying["s", 1, way, way].wait_recv()
        add(at(0, 3, way), way, 16 + way)
        flying["s", 2, way, way] = ship(
            terms.at[at(0, 3, way), way], 18 + way * 2 + way, ways[way]
        )
    for kind in range(2):
        way = 1 - kind
        flying["z", 1, way, kind].wait_recv()
        add(NZ + z, kind, 4 + way * 2 + kind)
        flying["y", 0, kind] = ship(terms.at[NZ + z, kind], 14 + kind, earlier)
    for step in (3, 4):
        for turn_of in range(2):
            for way in range(2):
                kind = turn_of if way else 1 - turn_of
                flying["s", step - 1, way, kind].wait_recv()
                indices = [18 + (step - 3) * 4 + way * 2 + kind]
                if step == 3:
                    flying["y", 2, way, kind].wait_recv()
                    indices.append(10 + way * 2 + kind)
                elif kind == way:
                    flying["y", 1, way].wait_recv()
                    indices.append(30 + way)
                block = at(0, 5 - step, way)
                add(block, kind, *indices)
                flying["s", step, way, kind] = ship(
                    terms.at[block, kind], 18 + (step - 2) * 4 + way * 2 + kind, ways[way]
                )
        if step == 3:
            stay()
    for kind in range(2):
        flying["y", 0, kind].wait_recv()
        for way in range(2):
            flying["s", 4, way, kind].wait_recv()
        total = terms[z, kind].astype(F32)
        for index in (14 + kind, 26 + kind, 28 + kind):
            total = total + landed[index].astype(F32)
        final[kind] = total
    mine = pl.ds(pl.multiple_of(core * ROWS, ROWS), ROWS)
    other = pl.ds(pl.multiple_of((1 - core) * ROWS, ROWS), ROWS)
    for kind in range(2):
        swaps.append(
            send(
                final.at[kind, other], dkv_out.at[kind, core],
                pair_send.at[2 + kind], pair_recv.at[2 + kind], sibling,
            )
        )
        copy = pltpu.make_async_copy(
            final.at[kind, mine], dkv_out.at[kind, core], own_sem.at[2 + kind]
        )
        copy.start()
        own.append(copy)
    for copy in sent:
        copy.wait_send()
    for copy in swaps:
        copy.wait()
    for copy in own:
        copy.wait()


def give_back(attn, dq, dkv):
    return pl.pallas_call(
        return_kernel,
        out_shape=(
            jax.ShapeDtypeStruct((2, ROWS * GROUP, HD), BF16),
            jax.ShapeDtypeStruct((2, ROWS * GROUP, HD), BF16),
            jax.ShapeDtypeStruct((2, 2, ROWS, HD), F32),
        ),
        in_specs=[HBM] * 3,
        out_specs=(HBM,) * 3,
        scratch_shapes=[
            pltpu.VMEM((4, HD, LANES), BF16),
            pltpu.VMEM((4, HD, LANES), BF16),
            pltpu.VMEM((2 * NZ, 2, 2 * ROWS, HD), BF16),
            pltpu.VMEM((2, ROWS * GROUP, HD), BF16),
            pltpu.VMEM((2, ROWS * GROUP, HD), BF16),
            pltpu.VMEM((LANES, HD), F32),
            pltpu.VMEM((32, 2 * ROWS, HD), BF16),
            pltpu.VMEM((2, 2 * ROWS, HD), F32),
            pltpu.SemaphoreType.DMA((4,)),
            pltpu.SemaphoreType.DMA((4,)),
            pltpu.SemaphoreType.DMA((7,)),
            pltpu.SemaphoreType.DMA((32,)),
            pltpu.SemaphoreType.DMA((32,)),
        ],
        compiler_params=pltpu.CompilerParams(
            collective_id=1, has_side_effects=True, vmem_limit_bytes=60 << 20
        ),
        name="give_back",
    )(attn, dq, dkv)


def finish_kernel(
    attn, dq, dkv, attn_out, dq_out, dk_out, dv_out, halves, joined, wide, wide_joined, parts, dk, dv, sem
):
    loads = [
        pltpu.make_async_copy(dkv, parts, sem.at[0]),
        pltpu.make_async_copy(attn, halves, sem.at[1]),
        pltpu.make_async_copy(dq, wide, sem.at[2]),
    ]
    for load in loads:
        load.start()
    stores = []
    loads[0].wait()
    for kind, (rows, dst) in enumerate(((dk, dk_out), (dv, dv_out))):
        for half in range(2):
            rows[pl.ds(half, ROWS, stride=2), :] = parts[kind, half]
        store = pltpu.make_async_copy(rows, dst, sem.at[4 + kind])
        store.start()
        stores.append(store)
    loads[1].wait()
    both = [halves[half].astype(F32).reshape(ROWS, GROUP, HD) for half in range(2)]
    joined[...] = jnp.concatenate(both, axis=1).astype(BF16)
    store = pltpu.make_async_copy(joined, attn_out, sem.at[6])
    store.start()
    stores.append(store)
    loads[2].wait()
    wide_joined[...] = jnp.concatenate(
        [wide[half].astype(F32).reshape(ROWS, GROUP, HD) for half in range(2)], axis=1
    )
    store = pltpu.make_async_copy(wide_joined, dq_out, sem.at[3])
    store.start()
    stores.append(store)
    for store in stores:
        store.wait()


def finish(attn, dq, dkv):
    return pl.pallas_call(
        finish_kernel,
        out_shape=(
            jax.ShapeDtypeStruct((ROWS, 2 * GROUP, HD), BF16),
            jax.ShapeDtypeStruct((ROWS, 2 * GROUP, HD), F32),
            jax.ShapeDtypeStruct((2 * ROWS, HD), F32),
            jax.ShapeDtypeStruct((2 * ROWS, HD), F32),
        ),
        in_specs=[HBM] * 3,
        out_specs=(HBM,) * 4,
        scratch_shapes=[
            pltpu.VMEM((2, ROWS * GROUP, HD), BF16),
            pltpu.VMEM((ROWS, 2 * GROUP, HD), BF16),
            pltpu.VMEM((2, ROWS * GROUP, HD), BF16),
            pltpu.VMEM((ROWS, 2 * GROUP, HD), F32),
            pltpu.VMEM((2, 2, ROWS, HD), F32),
            pltpu.VMEM((2 * ROWS, HD), F32),
            pltpu.VMEM((2 * ROWS, HD), F32),
            pltpu.SemaphoreType.DMA((7,)),
        ],
        compiler_params=pltpu.CompilerParams(vmem_limit_bytes=60 << 20),
        cost_estimate=pl.CostEstimate(flops=0, bytes_accessed=4 << 20, transcendentals=0),
        name="finish",
    )(attn, dq, dkv)


def local(queries, keys, values, grad_out, span_order, doc_ids):
    turned = [jnp.transpose(a, (1, 2, 0)) for a in (queries, keys, values, grad_out)]
    q_cols, g_cols, q_rows, g_rows, kv = bring(*turned)
    kv = kv.reshape(2 * NZ, 2, 4, SPAN, HD)
    attn, dq, dkv = attend(
        span_order, doc_ids.reshape(SLOTS, ROWS), q_cols, g_cols, q_rows, g_rows, kv
    )
    attn, dq, dkv = give_back(attn, dq, dkv.reshape(2 * NZ, 2, 2 * ROWS, HD))
    attn, dq, dk, dv = finish(attn, dq, dkv)
    return (attn, dq, dk.reshape(ROWS, 2, HD), dv.reshape(ROWS, 2, HD))


def solution(mesh):
    entry = P(("outer", "inner"), None, "head")
    leave = P(("outer", "inner"), "head", None)
    return jax.shard_map(
        local,
        mesh=mesh,
        in_specs=(entry, entry, entry, entry, P(), P()),
        out_specs=(leave, leave, leave, leave),
        check_vma=False,
    )
```
